32 devices in a mesh: scene: 8 (over z, x), view: 4 (over y, core).
Axes of the slice: x: 2, y: 2, z: 4, core: 2. Of those that a mesh axis runs over, the one named last changes fastest.
Arguments:
- inputs: bfloat16 [8, 4, 328, 768], P('scene', 'view'), may hold values from -6 to 6
- cameras: int32 [8, 4, 328], P('scene', 'view'), may hold values from 0 to 15
- embedding: float32 [16, 768], replicated, may hold values from -2.5 to 2.5
- scaling: float32 [768], replicated, may hold values from 0.1 to 1.9
- shifting: float32 [768], replicated, may hold values from -2.5 to 2.5
- projector: bfloat16 [768, 2304], replicated, may hold values from -0.3125 to 0.3125
- combiner: bfloat16 [768, 768], replicated, may hold values from -0.625 to 0.625
- baseline: float32 [768], replicated, may hold values from -2.5 to 2.5
- rescaling: float32 [768], replicated, may hold values from 0.1 to 1.9
- reshifting: float32 [768], replicated, may hold values from -2.5 to 2.5
- expander: bfloat16 [768, 1536], replicated, may hold values from -0.21875 to 0.21875
- priming: float32 [1536], replicated, may hold values from -2.5 to 2.5
- squeezer: bfloat16 [1536, 768], replicated, may hold values from -0.15625 to 0.15625
- leveling: float32 [768], replicated, may hold values from -2.5 to 2.5
- cotangent: bfloat16 [8, 4, 328, 768], P('scene', 'view'), may hold values from -6 to 6
Outputs:
- outcome: bfloat16 [8, 4, 328, 768], P('scene', 'view')
- adjoint_inputs: bfloat16 [8, 4, 328, 768], P('scene', 'view')
- adjoint_embedding: float32 [16, 768], replicated
- adjoint_scaling: float32 [768], replicated
- adjoint_shifting: float32 [768], replicated
- adjoint_projector: float32 [768, 2304], replicated
- adjoint_combiner: float32 [768, 768], replicated
- adjoint_baseline: float32 [768], replicated
- adjoint_rescaling: float32 [768], replicated
- adjoint_reshifting: float32 [768], replicated
- adjoint_expander: float32 [768, 1536], replicated
- adjoint_priming: float32 [1536], replicated
- adjoint_squeezer: float32 [1536, 768], replicated
- adjoint_leveling: float32 [768], replicated
The draws below stay inside these ranges and needn't reach their ends.
All inputs are finite; a program needn't handle non-finite values.
Results may differ from the reference program's by a relative error of at most 0.015.
Values may be sent and summed in bfloat16 or wider, within the bound.
No kernel may reach another device: no remote copies, remote signals or barrier semaphores. Data moves between devices by JAX's collectives and lax.ppermute only.
A program may use at most 192 MiB of HBM per device.

```python
import jax
import jax.numpy as jnp
from jax import lax

D = 768
HEADS = 12
HEAD = 64
FF = 1536
GROUPS = 16
PATCH = 328
VIEWS = 4
SCENES = 8


def set_ends(values, key, low, high):
    index_at = [jax.random.randint(jax.random.fold_in(key, axis), (), 0, length) for axis, length in enumerate(values.shape)]
    widest = values.shape.index(max(values.shape))
    next_to = index_at[:widest] + [(index_at[widest] + 1) % values.shape[widest]] + index_at[widest + 1:]
    return values.at[tuple(index_at)].set(low).at[tuple(next_to)].set(high)


def block_scale(rng, shape, split, smallest, high):
    loudness = 1.0
    for dim, blocks in split:
        heights = jax.random.uniform(jax.random.fold_in(jax.random.fold_in(rng, 6), dim), (blocks,), jnp.float32, smallest / len(split), high / len(split))
        loudness = loudness * jnp.repeat(jnp.exp(heights), shape[dim] // blocks).reshape((-1,) + (1,) * (len(shape) - 1 - dim))
    return loudness


def scatter_about(stream_key, dims, width, reach, cuts=(), kind=jnp.bfloat16):
    values = width * jax.random.normal(stream_key, dims, jnp.float32)
    if cuts:
        values = values * block_scale(stream_key, dims, cuts, -0.22, 0.18)
    return jnp.clip(values, -reach, reach).astype(kind)


def setup_inputs(seed: int = 0) -> dict:
    streams_of = jax.random.split(jax.random.key(seed), 16)
    inputs = scatter_about(streams_of[0], (SCENES, VIEWS, PATCH, D), 1.0, 6.0, ((0, 8), (1, 4)))
    cameras = set_ends(jax.random.randint(streams_of[1], (SCENES, VIEWS, PATCH), 0, GROUPS), jax.random.fold_in(streams_of[1], 1), 0, GROUPS - 1).astype(jnp.int32)
    embedding = scatter_about(streams_of[2], (GROUPS, D), 0.5, 2.5, (), jnp.float32)
    scaling = jnp.clip(1.0 + 0.18 * jax.random.normal(streams_of[3], (D,), jnp.float32), 0.1, 1.9)
    shifting = scatter_about(streams_of[4], (D,), 0.3, 2.5, (), jnp.float32)
    projector = scatter_about(streams_of[5], (D, 3 * D), (D // 2) ** -0.5, 0.3125)
    combiner = scatter_about(streams_of[6], (D, D), (D // 8) ** -0.5, 0.625)
    baseline = scatter_about(streams_of[7], (D,), 0.3, 2.5, (), jnp.float32)
    rescaling = jnp.clip(1.0 + 0.18 * jax.random.normal(streams_of[8], (D,), jnp.float32), 0.1, 1.9)
    reshifting = scatter_about(streams_of[9], (D,), 0.3, 2.5, (), jnp.float32)
    expander = scatter_about(streams_of[10], (D, FF), D ** -0.5, 0.21875)
    priming = scatter_about(streams_of[11], (FF,), 0.5, 2.5, (), jnp.float32)
    squeezer = scatter_about(streams_of[12], (FF, D), FF ** -0.5, 0.15625)
    leveling = scatter_about(streams_of[13], (D,), 0.3, 2.5, (), jnp.float32)
    cotangent = scatter_about(streams_of[14], (SCENES, VIEWS, PATCH, D), 1.0, 6.0, ((0, 8), (1, 4)))
    return dict(inputs=inputs, cameras=cameras, embedding=embedding, scaling=scaling, shifting=shifting, projector=projector, combiner=combiner, baseline=baseline, rescaling=rescaling, reshifting=reshifting, expander=expander, priming=priming, squeezer=squeezer, leveling=leveling, cotangent=cotangent)


@jax.custom_vjp
def low(v):
    return lax.optimization_barrier(v.astype(jnp.bfloat16)).astype(jnp.float32)

@jax.custom_vjp
def low_back(v):
    return v

def low_keep(v):
    return (low(v), None)

def low_pass(kept, grad):
    return (grad,)

def back_keep(v):
    return (v, None)

def back_low(kept, grad):
    return (low(grad),)
low.defvjp(low_keep, low_pass)
low_back.defvjp(back_keep, back_low)
highest = lax.Precision.HIGHEST

def layer_norm(values, gain, shift):
    centre = values - lax.optimization_barrier(jnp.mean(values, axis=-1, keepdims=True))
    spread = lax.optimization_barrier(jnp.mean(centre * centre, axis=-1, keepdims=True))
    return centre * lax.rsqrt(spread + 1e-05) * gain + shift

def scene_forward(weights, tokens, onehot):
    embedding, scaling, shifting, projector, combiner, baseline, rescaling, reshifting, expander, priming, squeezer, leveling = weights
    model_width = tokens.shape[1]
    summed = tokens + jnp.dot(onehot, embedding, precision=highest)
    normed = low(layer_norm(summed, scaling, shifting))
    triple = jnp.dot(normed, projector, precision=highest)
    queries = low(low_back(triple[:, :model_width])).reshape(-1, HEADS, HEAD)
    keyset = low(low_back(triple[:, model_width:2 * model_width])).reshape(-1, HEADS, HEAD)
    valueset = low(low_back(triple[:, 2 * model_width:])).reshape(-1, HEADS, HEAD)
    scores = low_back(jnp.einsum('qhd,khd->hqk', queries, keyset, precision=highest) * HEAD ** (-0.5))
    probs = low(jax.nn.softmax(scores, axis=-1))
    mixture = jnp.einsum('hqk,khd->qhd', probs, valueset, precision=highest).reshape(-1, model_width)
    mixed_low = low(low_back(mixture))
    attended = low_back(jnp.dot(mixed_low, combiner, precision=highest) + baseline)
    residual = summed + attended
    second_low = low(layer_norm(residual, rescaling, reshifting))
    hidden = low_back(jnp.dot(second_low, expander, precision=highest) + priming)
    activated = low(jax.nn.gelu(hidden, approximate=False))
    return residual + jnp.dot(activated, squeezer, precision=highest) + leveling

def reference(inputs, cameras, embedding, scaling, shifting, projector, combiner, baseline, rescaling, reshifting, expander, priming, squeezer, leveling, cotangent):
    weights = tuple((array.astype(jnp.float32) for array in (embedding, scaling, shifting, projector, combiner, baseline, rescaling, reshifting, expander, priming, squeezer, leveling)))
    scene_count = inputs.shape[0]
    model_width = inputs.shape[3]
    flat_inputs = inputs.reshape(scene_count, -1, model_width).astype(jnp.float32)
    flat_tangent = cotangent.reshape(scene_count, -1, model_width).astype(jnp.float32)
    flat_cameras = cameras.reshape(scene_count, -1).astype(jnp.int32)
    table_ids = jnp.arange(embedding.shape[0], dtype=jnp.int32)

    def one_scene(totals, scan_item):
        tokens, camera_row, tangent = scan_item
        onehot = (camera_row[:, None] == table_ids[None, :]).astype(jnp.float32)
        outputs_here, pullback = jax.vjp(lambda params, activations: scene_forward(params, activations, onehot), weights, tokens)
        weight_grads, token_grads = pullback(tangent)
        totals = jax.tree.map(lambda a, b: a + b, totals, weight_grads)
        return (totals, (outputs_here.astype(jnp.bfloat16), token_grads.astype(jnp.bfloat16)))
    zero_grads = jax.tree.map(jnp.zeros_like, weights)
    totals, (outcomes, token_adjoints) = lax.scan(one_scene, zero_grads, (flat_inputs, flat_cameras, flat_tangent))
    return (outcomes.reshape(inputs.shape), token_adjoints.reshape(inputs.shape), totals[0], totals[1], totals[2], totals[3], totals[4], totals[5], totals[6], totals[7], totals[8], totals[9], totals[10], totals[11])
```

```python
import jax
import jax.numpy as jnp
from jax import lax
from jax.sharding import PartitionSpec as P

HEADS = 12
HEAD = 64
BF = jnp.bfloat16
F32 = jnp.float32
BOTH = ("scene", "view")


def swap(value, axis, mask):
    count = lax.axis_size(axis)
    return lax.ppermute(value, axis, [(i, i ^ mask) for i in range(count)])


def swap_by_core(value, masks):
    scenes, views = lax.axis_size("scene"), lax.axis_size("view")
    pairs = []
    for s in range(scenes):
        for v in range(views):
            ds, dv = masks[v % 2]
            pairs.append((s * views + v, (s ^ ds) * views + (v ^ dv)))
    return lax.ppermute(value, BOTH, pairs)


def side_of(masks):
    scene, view = lax.axis_index("scene"), lax.axis_index("view")
    bits = []
    for ds, dv in masks:
        bits.append(((scene & ds) + (view & dv) > 0).astype(jnp.int32))
    return jnp.where(view % 2 == 0, bits[0], bits[1])


CORE = ((0, 1), (0, 1))
X, Y, Z1, Z2 = (1, 0), (0, 2), (2, 0), (4, 0)
FULL = (CORE, (X, Z1), (Y, X), (Z1, Y), (Z2, Z2))
SCENE = ((X, Z1), (Z1, X), (Z2, Z2))
VIEW = ((Y, Y), CORE)


def reduce_scatter(value, stages):
    for masks in stages:
        half = value.shape[0] // 2
        side = side_of(masks)
        send = lax.dynamic_slice_in_dim(value, (1 - side) * half, half, 0)
        keep = lax.dynamic_slice_in_dim(value, side * half, half, 0)
        got = swap_by_core(send, masks)
        value = (keep.astype(F32) + got.astype(F32)).astype(BF)
    bit = 8
    while bit < lax.axis_size("scene"):
        value = (value.astype(F32) + swap(value, "scene", bit).astype(F32)).astype(BF)
        bit *= 2
    return value


def all_gather(value, stages):
    for masks in reversed(stages):
        side = side_of(masks)
        got = swap_by_core(value, masks)
        value = jnp.concatenate(
            [jnp.where(side == 0, value, got), jnp.where(side == 0, got, value)], 0
        )
    return value


def by_view(blocks, me):
    a, b, c, d = blocks
    one = (me & 1) == 1
    a, b = jnp.where(one, b, a), jnp.where(one, a, b)
    c, d = jnp.where(one, d, c), jnp.where(one, c, d)
    two = (me & 2) == 2
    a, c = jnp.where(two, c, a), jnp.where(two, a, c)
    b, d = jnp.where(two, d, b), jnp.where(two, b, d)
    return a, b, c, d


def normalise(values):
    centre = values - jnp.mean(values, axis=-1, keepdims=True)
    rstd = lax.rsqrt(jnp.mean(centre * centre, axis=-1, keepdims=True) + 1e-05)
    return centre * rstd, rstd


def norm_back(grad, unit, rstd):
    return (
        grad
        - jnp.mean(grad, axis=-1, keepdims=True)
        - unit * jnp.mean(grad * unit, axis=-1, keepdims=True)
    ) * rstd


def dot(a, b):
    return jnp.dot(a, b, preferred_element_type=F32)


def tdot(a, b):
    return lax.dot_general(a, b, (((0,), (0,)), ((), ())), preferred_element_type=F32)


def dott(a, b):
    return lax.dot_general(a, b, (((1,), (1,)), ((), ())), preferred_element_type=F32)


def on_device(
    inputs,
    cameras,
    embedding,
    scaling,
    shifting,
    projector,
    combiner,
    baseline,
    rescaling,
    reshifting,
    expander,
    priming,
    squeezer,
    leveling,
    cotangent,
):
    me = lax.axis_index("view")
    patches, width = inputs.shape[2], inputs.shape[3]
    mine = HEADS // 4 * HEAD
    tangent = cotangent.reshape(patches, width)
    x0 = inputs.reshape(patches, width)
    c0 = cameras.reshape(patches)
    x2, c2 = swap(x0, "view", 2), swap(c0, "view", 2)
    x1, c1 = swap(x0, "view", 1), swap(c0, "view", 1)
    x3, c3 = swap(x2, "view", 1), swap(c2, "view", 1)
    tokens = jnp.concatenate([x0, x1, x2, x3], 0)
    groups = jnp.concatenate([c0, c1, c2, c3], 0)
    onehot = (groups[:, None] == jnp.arange(embedding.shape[0])[None, :]).astype(F32)
    summed = tokens.astype(F32) + jnp.dot(onehot, embedding, precision=lax.Precision.HIGHEST)
    unit1, rstd1 = normalise(summed)
    normed = (unit1 * scaling + shifting).astype(BF)
    weight = jnp.concatenate(
        [
            lax.dynamic_slice_in_dim(projector, part * width + me * mine, mine, 1)
            for part in range(3)
        ],
        1,
    )
    triple = dot(normed, weight).astype(BF)
    total = 4 * patches
    q = triple[:, :mine].reshape(total, 3, HEAD) * BF(HEAD**-0.5)
    k = triple[:, mine : 2 * mine].reshape(total, 3, HEAD)
    v = triple[:, 2 * mine :].reshape(total, 3, HEAD)
    scores = jnp.einsum("qhd,khd->hqk", q, k, preferred_element_type=F32)
    top = jnp.max(scores, -1, keepdims=True)
    expo = jnp.exp(scores - top)
    denom = jnp.sum(expo, -1)
    expo = expo.astype(BF)
    inverse = (1.0 / denom).T[:, :, None]
    mixture = jnp.einsum("hqk,khd->qhd", expo, v, preferred_element_type=F32) * inverse
    mixed_mine = mixture.reshape(total, mine).astype(BF)
    mixed_rel = [mixed_mine[r * patches : (r + 1) * patches] for r in range(4)]
    mixed_rel = [mixed_rel[0]] + [swap(mixed_rel[r], "view", r) for r in (1, 2, 3)]
    mixed = jnp.concatenate(by_view(mixed_rel, me), 1)
    residual = summed[:patches] + dot(mixed, combiner) + baseline
    unit2, rstd2 = normalise(residual)
    second = (unit2 * rescaling + reshifting).astype(BF)
    hidden = dot(second, expander) + priming
    phi = 0.5 * (1.0 + lax.erf(hidden * (2.0**-0.5)))
    density = jnp.exp(-0.5 * hidden * hidden) * ((2.0 * jnp.pi) ** -0.5)
    active = (hidden * phi).astype(BF)
    outcome = residual + dot(active, squeezer) + leveling
    hidden_grad = (dott(tangent, squeezer) * (phi + hidden * density)).astype(BF)
    second_grad = dott(hidden_grad, expander)
    tangent_f = tangent.astype(F32)
    residual_grad = tangent_f + norm_back(second_grad * rescaling, unit2, rstd2)
    resid_low = residual_grad.astype(BF)
    mix_grad = dott(resid_low, combiner).astype(BF)
    mix_rel = by_view([mix_grad[:, r * mine : (r + 1) * mine] for r in range(4)], me)
    mix_rel = [mix_rel[0]] + [swap(mix_rel[r], "view", r) for r in (1, 2, 3)]

    grad_squeezer = tdot(active, tangent).astype(BF)
    grad_expander = tdot(second, hidden_grad).astype(BF)
    grad_combiner = tdot(mixed, resid_low).astype(BF)
    rows = [
        jnp.sum(tangent_f, 0),
        jnp.sum(resid_low.astype(F32), 0),
        jnp.sum(second_grad * unit2, 0),
        jnp.sum(second_grad, 0),
        jnp.sum(hidden_grad.astype(F32), 0).reshape(2, width),
    ]
    rows = jnp.concatenate([r.reshape(-1, width) for r in rows], 0)
    rows = jnp.concatenate([rows, jnp.zeros((32 - rows.shape[0], width), F32)], 0).astype(BF)
    big = jnp.concatenate([grad_squeezer, grad_expander.reshape(-1, width), grad_combiner, rows], 0)
    big = reduce_scatter(big, FULL)
    big = all_gather(big, FULL)

    grad_out = jnp.concatenate(mix_rel, 0).reshape(total, 3, HEAD)
    delta = jnp.sum(grad_out.astype(F32) * mixture, -1).T[:, :, None]
    probs = expo.astype(F32) * (1.0 / denom)[:, :, None]
    prob_grad = jnp.einsum("qhd,khd->hqk", grad_out, v, preferred_element_type=F32)
    score_grad = (probs * (prob_grad - delta)).astype(BF)
    v_grad = jnp.einsum("hqk,qhd->khd", probs.astype(BF), grad_out, preferred_element_type=F32)
    q_grad = jnp.einsum("hqk,khd->qhd", score_grad, k, preferred_element_type=F32) * HEAD**-0.5
    k_grad = jnp.einsum("hqk,qhd->khd", score_grad, q, preferred_element_type=F32)
    triple_grad = jnp.concatenate(
        [g.reshape(total, mine) for g in (q_grad, k_grad, v_grad)], 1
    ).astype(BF)
    grad_weight = tdot(normed, triple_grad).astype(BF)
    normed_grad = dott(triple_grad, weight)
    summed_part = norm_back(normed_grad * scaling, unit1, rstd1)
    onehot_sum = lax.dot_general(
        onehot, summed_part, (((0,), (0,)), ((), ())), precision=lax.Precision.HIGHEST
    ) + lax.dot_general(
        onehot[:patches], residual_grad, (((0,), (0,)), ((), ())), precision=lax.Precision.HIGHEST
    )
    tail = jnp.concatenate(
        [onehot_sum, jnp.sum(normed_grad * unit1, 0)[None], jnp.sum(normed_grad, 0)[None]], 0
    )
    tail = tail.astype(BF).reshape(24, 3 * mine)
    late = jnp.concatenate([grad_weight, tail], 0)
    late = reduce_scatter(late, SCENE)
    late = all_gather(late, VIEW + SCENE)

    part = [summed_part[r * patches : (r + 1) * patches] for r in range(4)]
    keep = part[0] + swap(part[1].astype(BF), "view", 1).astype(F32)
    send = part[2] + swap(part[3].astype(BF), "view", 1).astype(F32)
    inputs_grad = residual_grad + keep + swap(send.astype(BF), "view", 2).astype(F32)

    late = late.reshape(2, 2, width + 24, 3 * mine).astype(F32)
    late = late.transpose(1, 0, 2, 3).reshape(4, width + 24, 3 * mine) if False else late.reshape(4, width + 24, 3 * mine)
    small = jnp.sum(late[:, width:], 0).reshape(18, width)
    grad_projector = (
        late[:, :width].reshape(4, width, 3, mine).transpose(1, 2, 0, 3).reshape(width, 3 * width)
    )
    big = big.astype(F32)
    hid = grad_squeezer.shape[0]
    at = 2 * hid + width
    return (
        outcome.astype(BF).reshape(inputs.shape),
        inputs_grad.astype(BF).reshape(inputs.shape),
        small[:16],
        small[16],
        small[17],
        grad_projector,
        big[2 * hid : at],
        big[at + 1],
        big[at + 2],
        big[at + 3],
        big[hid : 2 * hid].reshape(width, hid),
        big[at + 4 : at + 6].reshape(hid),
        big[:hid],
        big[at],
    )


def solution(mesh):
    tokens = P("scene", "view", None, None)
    placed = (tokens, P("scene", "view", None)) + (P(),) * 12 + (tokens,)
    return jax.shard_map(
        on_device,
        mesh=mesh,
        in_specs=placed,
        out_specs=(tokens, tokens) + (P(),) * 12,
        check_vma=False,
    )
```

```python
import functools

import jax
import jax.numpy as jnp
from jax import lax
from jax.experimental import pallas as pl
from jax.experimental.pallas import tpu as pltpu
from jax.sharding import PartitionSpec as P

HEADS = 12
HEAD = 64
BF = jnp.bfloat16
F32 = jnp.float32
BOTH = ("scene", "view")
MINE = HEADS // 4 * HEAD
PAD = 256
MIB = 1 << 20


def swap(value, axis, mask):
    count = lax.axis_size(axis)
    return lax.ppermute(value, axis, [(i, i ^ mask) for i in range(count)])


def swap_by_core(value, masks):
    scenes, views = lax.axis_size("scene"), lax.axis_size("view")
    pairs = []
    for s in range(scenes):
        for v in range(views):
            ds, dv = masks[v % 2]
            pairs.append((s * views + v, (s ^ ds) * views + (v ^ dv)))
    return lax.ppermute(value, BOTH, pairs)


def side_of(masks, core):
    scene, view = lax.axis_index("scene"), lax.axis_index("view")
    bits = [((scene & ds) + (view & dv) > 0).astype(jnp.int32) for ds, dv in masks]
    return jnp.where(core == 0, bits[0], bits[1])


def code_of(stages, core):
    total = 0
    for masks in stages:
        total = 2 * total + side_of(masks, core)
    return total


X, Y, Z1, Z2 = (1, 0), (0, 2), (2, 0), (4, 0)
WIDE = ((X, Z1), (Y, X), (Z1, Y), (Z2, Z2))
THIN = ((Y, Y), (Z1, Z1), (X, X), (Z2, Z2))
SCENE = ((X, Z1), (Z1, X), (Z2, Z2))


def rounded(value):
    return lax.optimization_barrier(lax.reduce_precision(value, 8, 7).astype(BF))


def whole_slice(value):
    bit = 8
    while bit < lax.axis_size("scene"):
        value = rounded(value.astype(F32) + swap(value, "scene", bit).astype(F32))
        bit *= 2
    return value


def by_view(blocks, me):
    a, b, c, d = blocks
    one = (me & 1) == 1
    a, b = jnp.where(one, b, a), jnp.where(one, a, b)
    c, d = jnp.where(one, d, c), jnp.where(one, c, d)
    two = (me & 2) == 2
    a, c = jnp.where(two, c, a), jnp.where(two, a, c)
    b, d = jnp.where(two, d, b), jnp.where(two, b, d)
    return a, b, c, d


def normalise(values):
    centre = values - jnp.mean(values, axis=-1, keepdims=True)
    rstd = lax.rsqrt(jnp.mean(centre * centre, axis=-1, keepdims=True) + 1e-05)
    return centre * rstd, rstd


def norm_back(grad, unit, rstd):
    return (
        grad
        - jnp.mean(grad, axis=-1, keepdims=True)
        - unit * jnp.mean(grad * unit, axis=-1, keepdims=True)
    ) * rstd


def dot(a, b):
    return jnp.dot(a, b, preferred_element_type=F32)


def tdot(a, b):
    return lax.dot_general(a, b, (((0,), (0,)), ((), ())), preferred_element_type=F32)


def dott(a, b):
    return lax.dot_general(a, b, (((1,), (1,)), ((), ())), preferred_element_type=F32)


def split3(values):
    high = values.astype(BF)
    rest = values - high.astype(F32)
    middle = rest.astype(BF)
    return high, middle, (rest - middle.astype(F32)).astype(BF)


def onehot_t(cameras, groups):
    rows = lax.broadcasted_iota(jnp.int32, (groups, cameras.shape[1]), 0)
    return (rows == cameras).astype(F32).astype(BF)


class Incoming:
    def __init__(self, source, buffer, sem):
        self.copy, self.buffer, self.there = pltpu.make_async_copy(source, buffer, sem), buffer, False
        self.copy.start()

    def __call__(self):
        if not self.there:
            self.copy.wait()
            self.there = True
        return self.buffer


class Present:
    def __init__(self, ref):
        self.buffer = ref

    def __call__(self):
        return self.buffer


class Outgoing:
    def __init__(self, target, buffer, sems, moves):
        self.target, self.ref, self.sems, self.moves = target, buffer, sems, moves

    def send(self, here=None, there=None):
        source = self.ref if here is None else self.ref.at[here]
        target = self.target if there is None else self.target.at[there]
        move = pltpu.make_async_copy(source, target, self.sems.at[len(self.moves)])
        move.start()
        self.moves.append(move)


class Operand:
    def __init__(self, array, *, home=False, ready=False, cut=None, shape=None, room=None):
        self.array, self.ready, self.cut, self.room, self.apart = array, ready, cut, room, False
        if home:
            self.array = pltpu.with_memory_space_constraint(array, pltpu.HBM)
        self.shape = array.shape if shape is None else shape


def apart(array):
    operand = Operand(array, home=True)
    operand.apart = True
    return operand


def home(array, **more):
    return Operand(array, home=True, **more)


def ready(array):
    return Operand(array, ready=True)


def staged(body, args, outs, *, name, mib, scratch=(), code=None, held=(), buffers=None):
    buffers = buffers or {}
    args = [a if isinstance(a, Operand) else Operand(a) for a in args]
    n_code, n_in, n_held, n_out = int(code is not None), len(args), len(held), len(outs)
    loads = [i for i, a in enumerate(args) if not (a.ready or a.apart)]

    def kernel(*refs):
        code_ref = refs[0] if n_code else None
        refs = refs[n_code:]
        ins, refs = refs[:n_in], refs[n_in + n_held :]
        targets, refs = refs[:n_out], refs[n_out:]
        in_bufs, refs = refs[: len(loads)], refs[len(loads) :]
        out_bufs, refs = refs[:n_out], refs[n_out:]
        in_sems, out_sems, rest = refs[0], refs[1], refs[2:]
        arrivals = [Present(ref) for ref in ins]
        for n, i in enumerate(loads):
            source = ins[i] if args[i].cut is None else ins[i].at[args[i].cut]
            buffer = in_bufs[n] if args[i].room is None else in_bufs[n].at[: args[i].shape[0]]
            arrivals[i] = Incoming(source, buffer, in_sems.at[n])
            if args[i].room is not None:
                arrivals[i].buffer = in_bufs[n]
        moves = []
        leaving = [Outgoing(t, b, out_sems, moves) for t, b in zip(targets, out_bufs, strict=True)]
        body(code_ref, arrivals, leaving, *rest)
        for arrival in arrivals:
            arrival()
        for move in moves:
            move.wait()

    anywhere, vmem = pl.BlockSpec(memory_space=pl.ANY), pl.BlockSpec(memory_space=pltpu.VMEM)
    specs = [pl.BlockSpec(memory_space=pltpu.SMEM)] * n_code
    specs += [vmem if a.ready else anywhere for a in args] + [anywhere] * n_held
    operands = ([code] if n_code else []) + [a.array for a in args]
    operands += [pltpu.with_memory_space_constraint(a, pltpu.HBM) for a in held]
    bufs = []
    for i in loads:
        shape = args[i].shape
        if args[i].room is not None:
            shape = (args[i].room, *shape[1:])
        bufs.append(pltpu.VMEM(shape, args[i].array.dtype))
    return pl.pallas_call(
        kernel,
        in_specs=specs,
        out_specs=[anywhere] * n_out,
        out_shape=[pltpu.HBM(shape, dtype) for shape, dtype in outs],
        scratch_shapes=bufs
        + [pltpu.VMEM(buffers.get(i, o[0]), o[1]) for i, o in enumerate(outs)]
        + [pltpu.SemaphoreType.DMA((max(len(loads), 1),)), pltpu.SemaphoreType.DMA((48,))]
        + list(scratch),
        input_output_aliases={n_code + n_in + i: i for i in range(n_held)},
        compiler_params=pltpu.CompilerParams(vmem_limit_bytes=mib * MIB),
        cost_estimate=pl.CostEstimate(flops=0, bytes_accessed=0, transcendentals=0),
        name=name,
    )(*operands)


def project_rows(tokens, cams, embedding, gain, shift, weight, outs, there, hold_ref, summed=None):
    normed, unit, rstd, *triple = outs
    rows = tokens[0].buffer.shape[0]
    pair = 2 * rows
    table = jnp.concatenate(split3(embedding()[...]), 0)
    for at, (x, c) in enumerate(zip(tokens, cams, strict=True)):
        hot = onehot_t(c()[...], embedding().shape[0])
        values = x()[...].astype(F32) + tdot(jnp.concatenate([hot] * 3, 0), table)
        if at == 0 and summed is not None:
            summed.ref[...] = values
            summed.send()
        values, scale = normalise(values)
        hold_ref[pl.ds(at * rows, rows), :] = values
        rstd.ref[pl.ds(at * rows, rows), :] = scale
    values = hold_ref[...]
    low = (values * gain()[...] + shift()[...]).astype(BF)
    normed.ref[...] = low
    lane = lax.broadcasted_iota(jnp.int32, (pair, PAD), 1)
    for i, (ref, first, out) in enumerate(triple):
        block = dot(low, weight()[:, i * PAD : (i + 1) * PAD])
        if i == 0:
            block = block * HEAD**-0.5
        if i == 2:
            block = jnp.where(lane < MINE, block, 1.0)
        ref[first : first + pair, :] = block.astype(BF)
        out.send((pl.ds(first, pair),), there)
    normed.send(None, there)
    unit.ref[...] = values.astype(BF)
    unit.send(None, there)
    rstd.send(None, there)


def project_outs(total, width):
    outs = [((total, width), BF), ((total, width), BF), ((total, 1), F32)]
    return outs + [((total, PAD), BF)] * 3


def project_body(_, ins, outs, hold_ref):
    xa, xb, ca, cb, embedding, gain, shift, weight = ins
    there = (pl.ds(0, hold_ref.shape[0]),)
    triple = [(out.ref, 0, out) for out in outs[3:6]]
    project_rows((xa, xb), (ca, cb), embedding, gain, shift, weight, [*outs[:3], *triple], there, hold_ref, outs[6])


def project(xa, xb, ca, cb, embedding, gain, shift, weight):
    rows, width = xa.shape[-2:]
    pair, total = 2 * rows, 4 * rows
    outs = project_outs(total, width)
    return staged(
        project_body,
        [xa, xb, ca, cb, embedding, gain, shift, weight],
        [*outs, ((rows, width), F32)],
        name="project",
        mib=32,
        scratch=[pltpu.VMEM((pair, width), F32)],
        buffers={i: (pair, o[0][1]) for i, o in enumerate(outs)},
    )


def blocks_of(total):
    return [(at, min(256, total - at)) for at in range(0, total, 256)]


def one_head(block, head):
    lane = lax.broadcasted_iota(jnp.int32, block.shape, 1) // HEAD
    return jnp.where(lane == head, block, jnp.zeros_like(block))


def attend_rows(q_ref, keys, values_of, outs, vt_ref, mt_ref, it_ref):
    e, first, second, mix, inv = outs
    pair, heads = q_ref.shape[0], e.ref.shape[0]
    work = [(h, at, size) for h in range(heads) for at, size in blocks_of(pair)]

    def scores(h, at, size):
        return dott(keys()[...], one_head(q_ref[at : at + size, :], h))

    ahead = scores(*work[0])
    vt_ref[...] = values_of()[...].astype(F32).T.astype(BF)
    mt_ref[...] = jnp.zeros_like(mt_ref)
    it_ref[...] = jnp.zeros_like(it_ref)
    for i, (h, at, size) in enumerate(work):
        here = ahead
        if i + 1 < len(work):
            ahead = scores(*work[i + 1])
        mine = slice(h * HEAD, (h + 1) * HEAD)
        expo = jnp.exp(here - jnp.max(here, 0, keepdims=True)).astype(BF)
        cut = (h, slice(None), slice(at, at + size))
        e.ref[cut] = expo
        e.send((h, slice(None), pl.ds(at, size)), (h, slice(None), pl.ds(at, size)))
        values = jnp.concatenate([vt_ref[mine, :], vt_ref[MINE : MINE + 16, :]], 0)
        out = dot(values, expo)
        inverse = 1.0 / out[HEAD : HEAD + 1, :]
        mt_ref[mine, at : at + size] = out[:HEAD, :] * inverse
        it_ref[mine, at : at + size] = jnp.broadcast_to(inverse, (HEAD, size))
    mixed = mt_ref[...].T[:pair]
    first.ref[...] = mixed[: pair // 2, :MINE].astype(BF)
    first.send()
    second.ref[...] = mixed[pair // 2 :, :MINE].astype(BF)
    second.send()
    mix.ref[...] = mixed[:, :MINE]
    mix.send()
    inv.ref[...] = it_ref[...].T[:pair, :MINE]
    inv.send()


def attend_outs(total):
    pair, heads = total // 2, MINE // HEAD
    part, soft = ((pair // 2, MINE), BF), ((pair, MINE), F32)
    return [((heads, total, pair), BF), part, part, soft, soft]


def attend_scratch(total):
    wide = -(-(total // 2) // 128) * 128
    return [pltpu.VMEM((PAD, total), BF), pltpu.VMEM((PAD, wide), F32), pltpu.VMEM((PAD, wide), F32)]


def attend_body(_, ins, outs, *scratch):
    q, k, v = ins
    attend_rows(q(), k, v, outs, *scratch)


def attend(q, k, v):
    total = k.shape[0]
    pair = total // 2
    return staged(
        attend_body,
        [home(q, cut=(pl.ds(0, pair),), shape=(pair, PAD)), home(k), home(v)],
        attend_outs(total),
        name="attend",
        mib=32,
        scratch=attend_scratch(total),
    )


def second_body(_, ins, outs, hold_ref, *scratch):
    xa, xb, ca, cb, embedding, gain, shift, weight, k, v = ins
    pair = hold_ref.shape[0]
    there = (pl.ds(pair, pair),)
    triple = [(outs[3].ref, 0, outs[3]), (k.buffer, pair, outs[4]), (v.buffer, pair, outs[5])]
    outs[4].ref, outs[5].ref = k.buffer, v.buffer
    project_rows((xa, xb), (ca, cb), embedding, gain, shift, weight, [*outs[:3], *triple], there, hold_ref)
    attend_rows(outs[3].ref, k, v, outs[6:], *scratch)


def second_half(xa, xb, ca, cb, embedding, gain, shift, weight, held):
    rows, width = xa.shape[-2:]
    pair, total = 2 * rows, 4 * rows
    outs = project_outs(total, width)
    buffers = {i: (pair, o[0][1]) for i, o in enumerate(outs)}
    buffers[4] = buffers[5] = (16, PAD)
    first = dict(cut=(pl.ds(0, pair),), shape=(pair, PAD), room=total)
    return staged(
        second_body,
        [xa, xb, ca, cb, embedding, gain, shift, weight, home(held[4], **first), home(held[5], **first)],
        [*outs, *attend_outs(total)],
        name="second_half",
        mib=44,
        scratch=[pltpu.VMEM((pair, width), F32), *attend_scratch(total)],
        held=held,
        buffers=buffers,
    )


def back_body(code, ins, outs, g_ref, kt_ref, delta_ref, dq_ref, dka_ref, dva_ref, hold_ref, piece_ref):
    q, k, v, *ins = ins
    grads, mixes, invs, expos, normed = ins[:4], ins[4:6], ins[6:8], ins[8:-1], ins[-1]
    dqk, dv = outs[:2]
    total = q.buffer.shape[0]
    pair, rows = total // 2, grads[0].buffer.shape[0]
    heads = len(expos) // 2
    hold_ref[...] = jnp.zeros_like(hold_ref)
    for i, grad in enumerate(grads):
        hold_ref[i * rows : (i + 1) * rows, :MINE] = grad()[...].astype(F32)
    lane = lax.broadcasted_iota(jnp.int32, (8, PAD), 1) // HEAD
    pick = (lane == lax.broadcasted_iota(jnp.int32, (8, PAD), 0)).astype(F32).astype(BF)
    for i in range(2):
        here = slice(i * pair, (i + 1) * pair)
        hold_ref[here, :MINE] = hold_ref[here, :MINE] * invs[i]()[...]
        scaled = hold_ref[here, :].astype(BF)
        g_ref[here, :] = scaled
        hold_ref[here, :MINE] = scaled[:, :MINE].astype(F32) * mixes[i]()[...]
        prod = hold_ref[here, :]
        high = prod.astype(BF)
        low = (prod - high.astype(F32)).astype(BF)
        delta_ref[i, :, :pair] = dott(pick, high) + dott(pick, low)
    kt_ref[...] = k()[...].astype(F32).T.astype(BF)
    dq_ref[...] = jnp.zeros_like(dq_ref)
    work = [(h, i, at, size) for h in range(heads) for i in range(2) for at, size in blocks_of(pair)]

    def cut(ref, h, i, at, size):
        return one_head(ref[i * pair + at : i * pair + at + size, :], h)

    ahead_grad = cut(g_ref, *work[0])
    ahead = dott(v()[...], ahead_grad)
    for n, (h, i, at, size) in enumerate(work):
        grad, prob_grad = ahead_grad, ahead
        if n + 1 < len(work):
            ahead_grad = cut(g_ref, *work[n + 1])
            ahead = dott(v()[...], ahead_grad)
        expo = expos[2 * h + i]()[:, at : at + size]
        delta = delta_ref[i, h : h + 1, at : at + size]
        score_grad = (expo.astype(F32) * (prob_grad - delta)).astype(BF)
        value_part = dot(expo, grad)
        key_part = dot(score_grad, cut(q(), h, i, at, size))
        if n:
            value_part += dva_ref[...]
            key_part += dka_ref[...]
        dva_ref[...] = value_part
        dka_ref[...] = key_part
        mine = slice(h * HEAD, (h + 1) * HEAD)
        dq_ref[i, mine, at : at + size] = dot(kt_ref[mine, :], score_grad)
    for i in range(2):
        dq = dq_ref[i].T[:pair] * HEAD**-0.5
        dqk.ref[i * pair : (i + 1) * pair, :MINE] = dq[:, :MINE].astype(BF)
    dqk.ref[:, MINE:] = dka_ref[:, :MINE].astype(BF)
    dqk.send()
    dv.ref[...] = dva_ref[:, :MINE].astype(BF)
    dv.send()
    weight_grad(code, normed, dqk.ref, dv.ref, outs[2], outs[3], piece_ref)


PIECES = 8


def weight_grad(code, normed, dqk_ref, dv_ref, keep, send, hold_ref):
    width = normed().shape[1]
    rows = width // PIECES
    piece = rows + rows // 2
    mine = code[0]
    qk = tdot(normed()[...], dqk_ref[...]).astype(BF)
    v = tdot(normed()[...], dv_ref[...]).astype(BF)
    for p in range(PIECES):
        at = pl.multiple_of((p ^ mine) * piece, 16)
        hold_ref[pl.ds(at, rows), :] = qk[p * rows : (p + 1) * rows]
        at = pl.multiple_of((p ^ mine) * piece + rows, 16)
        top = v[p * rows : p * rows + rows // 2]
        low = v[p * rows + rows // 2 : (p + 1) * rows]
        hold_ref[pl.ds(at, rows // 2), :] = jnp.concatenate([top, low], 1)
    half = PIECES * piece // 2
    send.ref[...] = hold_ref[half:, :]
    send.send()
    keep.ref[...] = hold_ref[:half, :]
    keep.send()


def attend_back(codes, q, k, v, e0, e1, grads, mix0, mix1, inv0, inv1, normed):
    total, heads = k.shape[0], MINE // HEAD
    pair = total // 2
    wide = -(-pair // 128) * 128
    width = normed.shape[1]
    piece = width // PIECES * 3 // 2
    args = [home(q), home(k), home(v), *grads, home(mix0), home(mix1), home(inv0), home(inv1)]
    for h in range(heads):
        args += [home(e, cut=(h,), shape=(total, pair)) for e in (e0, e1)]
    args.append(home(normed))
    half = ((PIECES * piece // 2, 2 * MINE), BF)
    return staged(
        back_body,
        args,
        [((total, 2 * MINE), BF), ((total, MINE), BF), half, half],
        name="attend_back",
        mib=52,
        scratch=[
            pltpu.VMEM((total, PAD), BF),
            pltpu.VMEM((PAD, total), BF),
            pltpu.VMEM((2, 8, wide), F32),
            pltpu.VMEM((2, PAD, wide), F32),
            pltpu.VMEM((total, PAD), F32),
            pltpu.VMEM((total, PAD), F32),
            pltpu.VMEM((total, PAD), F32),
            pltpu.VMEM((PIECES * piece, 2 * MINE), BF),
        ],
        code=codes,
    )


STEP = 512


def feed_forward_body(code, ins, outs):
    summed, own, near, far, rest, combiner, baseline, gain, shift, expander, priming, squeezer, tangent = ins
    residual, own_wide, wide, own_slim, slim = outs
    me = code[2]
    first = code[3] == 0
    total = summed()[...] + baseline()[...]
    for r, block in ((2, far), (3, rest), (0, own), (1, near)):
        at = pl.multiple_of((me ^ r) * MINE, 16)
        total += dot(block()[...], combiner()[pl.ds(at, MINE), :])
    residual.ref[...] = total
    residual.send()
    unit, _ = normalise(total)
    low = (unit * gain()[...] + shift()[...]).astype(BF)
    own_slim.ref[...] = jnp.where(first, tangent()[...], low)
    own_slim.send()
    slim.ref[...] = jnp.where(first, low, tangent()[...])
    slim.send()
    for at in range(0, expander().shape[1], STEP):
        cut = slice(at, at + STEP)
        hidden = dot(low, expander()[:, cut]) + priming()[cut]
        back = dott(tangent()[...], squeezer()[cut, :])
        phi = 0.5 * (1.0 + lax.erf(hidden * (2.0**-0.5)))
        density = jnp.exp(-0.5 * hidden * hidden) * 0.3989422804014327
        active = (hidden * phi).astype(BF)
        grad = (back * (phi + hidden * density)).astype(BF)
        own_wide.ref[:, cut] = jnp.where(first, active, grad)
        wide.ref[:, cut] = jnp.where(first, grad, active)
        part = (slice(None), pl.ds(at, STEP))
        own_wide.send(part, part)
        wide.send(part, part)


def feed_forward(codes, summed, own, near, far, rest, combiner, baseline, gain, shift, expander, priming, squeezer, tangent):
    rows, width = summed.shape
    hid = expander.shape[1]
    weights = [ready(combiner), baseline, gain, shift, ready(expander), priming, ready(squeezer), ready(tangent)]
    return staged(
        feed_forward_body,
        [home(summed), own, near, far, rest, *weights],
        [((rows, width), F32), ((rows, hid), BF), ((rows, hid), BF), ((rows, width), BF), ((rows, width), BF)],
        name="feed_forward",
        mib=24,
        code=codes,
    )


def feed_back_body(code, ins, outs, grad_ref, sem):
    residual, tangent, expander, gain, combiner, own_wide, wide = ins
    residual_grad, low, *grads, rows = outs
    me = code[2]

    for core, source in enumerate((wide, own_wide)):

        @pl.when(code[3] == core)
        def _():
            pltpu.make_async_copy(source(), grad_ref, sem.at[0]).start()

    pltpu.make_async_copy(wide(), grad_ref, sem.at[0]).wait()
    second_grad = dott(grad_ref[...], expander()[...])
    unit, rstd = normalise(residual()[...])
    slope = tangent()[...].astype(F32)
    total = slope + norm_back(second_grad * gain()[...], unit, rstd)
    low.ref[...] = total.astype(BF)
    low.send()
    for r in (2, 3, 1, 0):
        at = pl.multiple_of((me ^ r) * MINE, 16)
        grads[r].ref[...] = dott(low.ref[...], combiner()[pl.ds(at, MINE), :]).astype(BF)
        grads[r].send()
    residual_grad.ref[...] = total
    residual_grad.send()
    width = total.shape[1]
    rows.ref[0:1, :] = jnp.sum(slope, 0, keepdims=True)
    rows.ref[1:2, :] = jnp.sum(low.ref[...].astype(F32), 0, keepdims=True)
    rows.ref[2:3, :] = jnp.sum(second_grad * unit, 0, keepdims=True)
    rows.ref[3:4, :] = jnp.sum(second_grad, 0, keepdims=True)
    for j in range(grad_ref.shape[1] // width):
        block = grad_ref[:, j * width : (j + 1) * width].astype(F32)
        rows.ref[4 + j : 5 + j, :] = jnp.sum(block, 0, keepdims=True)
    rows.ref[6:8, :] = jnp.zeros((2, width), F32)
    rows.send()


def feed_back(codes, residual, own_wide, wide, tangent, expander, gain, combiner):
    rows, width = residual.shape
    return staged(
        feed_back_body,
        [home(residual), ready(tangent), ready(expander), gain, ready(combiner), apart(own_wide), apart(wide)],
        [((rows, width), F32), ((rows, width), BF)] + [((rows, MINE), BF)] * 4 + [((8, width), F32)],
        name="feed_back",
        mib=24,
        scratch=[pltpu.VMEM(wide.shape, BF), pltpu.SemaphoreType.DMA((1,))],
        code=codes,
    )


def outcome_body(code, ins, outs, active_ref, sem):
    residual, squeezer, leveling, own_wide, wide = ins

    for core, source in enumerate((own_wide, wide)):

        @pl.when(code[3] == core)
        def _():
            pltpu.make_async_copy(source(), active_ref, sem.at[0]).start()

    pltpu.make_async_copy(wide(), active_ref, sem.at[0]).wait()
    outs[0].ref[...] = (residual()[...] + dot(active_ref[...], squeezer()[...]) + leveling()[...]).astype(BF)
    outs[0].send()


def outcome_of(codes, residual, own_wide, wide, squeezer, leveling):
    rows, width = residual.shape
    return staged(
        outcome_body,
        [home(residual), ready(squeezer), leveling, apart(own_wide), apart(wide)],
        [((rows, width), BF)],
        name="outcome",
        mib=16,
        scratch=[pltpu.VMEM(wide.shape, BF), pltpu.SemaphoreType.DMA((1,))],
        code=codes,
    )[0]


PARTS = 16


def place(code, piece, size):
    return pl.multiple_of((piece ^ code) * size, 8)


def segments(first, rows, low, size):
    out, at = [], first
    while at < first + rows:
        piece, offset = divmod(at - low, size)
        count = min(size - offset, first + rows - at)
        out.append((piece, offset, at - first, count))
        at += count
    return out


def spread(hold_ref, block, first, low, size, code):
    for piece, offset, start, count in segments(first, block.shape[0], low, size):
        at = pl.multiple_of(place(code, piece, size) + offset, 8)
        hold_ref[pl.ds(at, count), :] = block[start : start + count]


def feed_grad_body(sizes, code, ins, outs, *holds):
    own_wide, own_slim, wide, slim, own, far, near, rest, resid, other = ins
    hid, width = own_wide().shape[1], own_slim().shape[1]
    bulk = PARTS * sizes[0]
    refs = [arrival() for arrival in (own_wide, own_slim, wide, slim)]

    def put(block, row):
        for part, low, high in ((0, 0, bulk), (1, bulk, bulk + PARTS * sizes[1])):
            first, last = max(row, low), min(row + block.shape[0], high)
            if first < last:
                spread(holds[part], block[first - row : last - row], first, low, sizes[part], code[4 + 2 * part])

    for j in range(hid // width):
        cut = slice(j * width, (j + 1) * width)
        for one in range(2):

            @pl.when(code[3] == one)
            def _():
                if one:
                    block = tdot(refs[1][...], refs[0][:, cut]) + tdot(refs[3][...], refs[2][:, cut])
                else:
                    block = tdot(refs[0][:, cut], refs[1][...]) + tdot(refs[2][:, cut], refs[3][...])
                put(block, j * width)

    upper = code[2] < 2
    for i in range(2):
        here = jnp.where(upper, (own, far)[i]()[...], (far, own)[i]()[...])
        peer = jnp.where(upper, (near, rest)[i]()[...], (rest, near)[i]()[...])
        put(tdot(here, resid()[...]) + tdot(peer, other()[...]), hid + i * MINE)
    for part, hold_ref in enumerate(holds):
        keep, send = outs[2 * part : 2 * part + 2]
        half = hold_ref.shape[0] // 2
        send.ref[...] = hold_ref[half:, :].astype(BF)
        send.send()
        keep.ref[...] = hold_ref[:half, :].astype(BF)
        keep.send()


def feed_grad(codes, sizes, feed, mixed):
    width = feed[1].shape[1]
    halves = [((PARTS * size // 2, width), BF) for size in sizes]
    return staged(
        functools.partial(feed_grad_body, sizes),
        [home(feed[0]), home(feed[1]), *feed[2:], *mixed],
        [halves[0], halves[0], halves[1], halves[1]],
        name="feed_grad",
        mib=40,
        scratch=[pltpu.VMEM((PARTS * size, width), F32) for size in sizes],
        code=codes,
    )


def feed_assemble_body(sizes, code, ins, outs, *holds):
    squeezer, expander, combiner = outs
    hid, width = squeezer.target.shape
    sems, moves = squeezer.sems, squeezer.moves

    def targets(core, row, count):
        out = []
        while count:
            if row < hid and core == 0:
                take = min(count, hid - row)
                out.append((squeezer.target.at[pl.ds(row, take), :], take))
            elif row < hid:
                j = row // width
                take = min(count, (j + 1) * width - row)
                cut = pl.ds(row - j * width, take), pl.ds(j * width, width)
                out.append((expander.target.at[cut], take))
            else:
                view, at = divmod(row - hid, MINE)
                take = min(count, MINE - at)
                out.append((combiner.target.at[pl.ds((core + 2 * view) * MINE + at, take), :], take))
            row, count = row + take, count - take
        return out

    def copies(me):
        out = []
        for side in range(2):
            core = me if side == 0 else 1 - me
            low = 0
            for part, size in enumerate(sizes):
                code_here = code[4 + 2 * part + side]
                for piece in range(PARTS):
                    at = 0
                    for target, count in targets(core, low + piece * size, size):
                        start = pl.multiple_of(place(code_here, piece, size) + at, 8)
                        source = holds[2 * side + part].at[pl.ds(start, count), :]
                        out.append(pltpu.make_async_copy(source, target, sems.at[len(out)]))
                        at += count
                low += PARTS * size
        return out

    for i, hold_ref in enumerate(holds):
        half = hold_ref.shape[0] // 2
        hold_ref[:half, :] = ins[2 * i]()[...].astype(F32)
        hold_ref[half:, :] = ins[2 * i + 1]()[...].astype(F32)
    for me in range(2):

        @pl.when(code[3] == me)
        def _():
            here = copies(me)
            for move in here:
                move.start()
            for move in here:
                move.wait()


def feed_assemble(codes, blocks, hid, width):
    sizes = [blocks[0].shape[0] // 8, blocks[2].shape[0] // 8]

    def kernel(code_ref, *refs):
        ins, targets, bufs, rest = refs[:8], refs[8:11], refs[11:19], refs[19:]
        in_sems, out_sems, holds = rest[0], rest[1], rest[2:]
        arrivals = [Incoming(s, b, in_sems.at[i]) for i, (s, b) in enumerate(zip(ins, bufs, strict=True))]
        outs = [Outgoing(t, None, out_sems, []) for t in targets]
        feed_assemble_body(sizes, code_ref, arrivals, outs, *holds)

    anywhere = pl.BlockSpec(memory_space=pl.ANY)
    return pl.pallas_call(
        kernel,
        in_specs=[pl.BlockSpec(memory_space=pltpu.SMEM)] + [anywhere] * 8,
        out_specs=[anywhere] * 3,
        out_shape=[pltpu.HBM(s, F32) for s in ((hid, width), (width, hid), (width, width))],
        scratch_shapes=[pltpu.VMEM(b.shape, BF) for b in blocks]
        + [pltpu.SemaphoreType.DMA((8,)), pltpu.SemaphoreType.DMA((96,))]
        + [pltpu.VMEM((PARTS * size, width), F32) for size in sizes + sizes],
        compiler_params=pltpu.CompilerParams(vmem_limit_bytes=40 * MIB),
        cost_estimate=pl.CostEstimate(flops=0, bytes_accessed=0, transcendentals=0),
        name="feed_assemble",
    )(codes, *[pltpu.with_memory_space_constraint(b, pltpu.HBM) for b in blocks])


def input_grad_body(_, ins, outs, hold_ref):
    dqk, dv, weight, unit, rstd, gain, *rest = ins
    cams, resid = rest[:4], rest[4]
    small = outs[4]
    patches = resid.buffer.shape[0]
    groups = small.ref.shape[0] - 2
    slope = dott(dqk()[:, :MINE], weight()[:, :MINE]) + dott(dqk()[:, MINE:], weight()[:, PAD : PAD + MINE])
    slope += dott(dv()[...], weight()[:, 2 * PAD : 2 * PAD + MINE])
    values = unit()[...].astype(F32)
    small.ref[groups : groups + 1, :] = jnp.sum(slope * values, 0, keepdims=True)
    small.ref[groups + 1 : groups + 2, :] = jnp.sum(slope, 0, keepdims=True)
    hold_ref[...] = norm_back(slope * gain()[...], values, rstd()[...])
    table = jnp.zeros((groups, slope.shape[1]), F32)
    for r in (1, 3, 0, 2):
        part = hold_ref[r * patches : (r + 1) * patches, :]
        outs[r].ref[...] = part.astype(outs[r].ref.dtype)
        outs[r].send()
        if r == 0:
            part = part + resid()[...]
        hot = onehot_t(cams[r]()[...], groups)
        for piece in split3(part):
            table += dot(hot, piece)
    small.ref[:groups, :] = table
    small.send()


def input_grad(dqk, dv, weight, unit, rstd, gain, cams, resid, groups):
    total, width = unit.shape
    patches = resid.shape[0]
    low, full = ((patches, width), BF), ((patches, width), F32)
    return staged(
        input_grad_body,
        [home(dqk), home(dv), home(weight), home(unit), home(rstd), gain, *cams, home(resid)],
        [full, low, full, low, ((groups + 2, width), F32)],
        name="input_grad",
        mib=48,
        scratch=[pltpu.VMEM((total, width), F32)],
    )


def assemble_kernel(code_ref, a_ref, b_ref, c_ref, d_ref, out_ref):
    me = code_ref[2]
    rows = out_ref.shape[0]
    width = out_ref.shape[1] // 3
    blocks = [r[...].astype(F32) for r in (a_ref, b_ref, c_ref, d_ref)]
    for v, block in enumerate(by_view(blocks, me)):
        at = v * MINE
        out_ref[:, at : at + MINE] = block[:rows, :MINE]
        out_ref[:, width + at : width + at + MINE] = block[:rows, MINE:]
        out_ref[: rows // 2, 2 * width + at : 2 * width + at + MINE] = block[rows:, :MINE]
        out_ref[rows // 2 :, 2 * width + at : 2 * width + at + MINE] = block[rows:, MINE:]


def assemble(codes, blocks, width):
    rows = width // PIECES
    piece = rows * 3 // 2

    def part(which, far):
        def place(p, code):
            r = p ^ code[which]
            return ((r // 2 * 2 + far) * 2 + r % 2, 0)

        return pl.BlockSpec((piece, 2 * MINE), place)

    own, near = blocks
    return pl.pallas_call(
        assemble_kernel,
        grid_spec=pltpu.PrefetchScalarGridSpec(
            num_scalar_prefetch=1,
            grid=(PIECES,),
            in_specs=[part(0, 0), part(1, 0), part(0, 1), part(1, 1)],
            out_specs=pl.BlockSpec((rows, 3 * width), lambda p, code: (p, 0)),
        ),
        out_shape=jax.ShapeDtypeStruct((width, 3 * width), F32),
        compiler_params=pltpu.CompilerParams(vmem_limit_bytes=24 * MIB),
        cost_estimate=pl.CostEstimate(flops=0, bytes_accessed=0, transcendentals=0),
        name="assemble",
    )(codes, own, near, own, near)


def small_kernel(here_ref, there_ref, table_ref, *refs):
    groups, width = table_ref.shape
    total = here_ref[...].astype(F32) + there_ref[...].astype(F32)
    table_ref[...] = total[:groups, :]
    row = groups
    for ref in refs:
        for at in range(0, ref.shape[0], width):
            ref[at : at + width] = total[row, :]
            row += 1


def small_outputs(here, there, groups, sizes):
    shapes = [(groups, here.shape[1])] + [(n,) for n in sizes]
    return pl.pallas_call(
        small_kernel,
        out_shape=[jax.ShapeDtypeStruct(s, F32) for s in shapes],
        cost_estimate=pl.CostEstimate(flops=0, bytes_accessed=0, transcendentals=0),
        name="small_outputs",
    )(here, there)


def after(values, *others):
    out = lax.optimization_barrier((*values, *others))
    return out[: len(values)]


def on_device(
    inputs,
    cameras,
    embedding,
    scaling,
    shifting,
    projector,
    combiner,
    baseline,
    rescaling,
    reshifting,
    expander,
    priming,
    squeezer,
    leveling,
    cotangent,
):
    me = lax.axis_index("view")
    core = me % 2
    patches, width = inputs.shape[2], inputs.shape[3]
    groups, hid = embedding.shape[0], expander.shape[1]
    codes = [code_of(SCENE, core), code_of(SCENE, 1 - core), me, core]
    codes += [code_of(WIDE, core), code_of(WIDE, 1 - core), code_of(THIN, core), code_of(THIN, core)]
    codes = jnp.stack(codes).astype(jnp.int32)
    tangent = cotangent.reshape(patches, width)
    x0 = inputs.reshape(patches, width)
    c0 = cameras.reshape(1, patches)
    x2, c2 = swap(x0, "view", 2), swap(c0, "view", 2)
    x1, c1 = swap(x0, "view", 1), swap(c0, "view", 1)
    hole = jnp.zeros((width, PAD - MINE), BF)
    padded = []
    for part in range(3):
        padded += [lax.dynamic_slice_in_dim(projector, part * width + me * MINE, MINE, 1), hole]
    padded = jnp.concatenate(padded, 1)
    *held, summed = project(x0, x1, c0, c1, embedding, scaling, shifting, padded)
    x2, c2 = after((x2, c2), *held)
    x3, c3 = swap(x2, "view", 1), swap(c2, "view", 1)
    normed, unit1, rstd1, q, k, v, e1, far, rest, mix1, inv1 = second_half(
        x2, x3, c2, c3, embedding, scaling, shifting, padded, held
    )
    far, rest = swap(far, "view", 2), swap(rest, "view", 3)
    e0, own, near, mix0, inv0 = attend(q, k, v)
    near, own, far, rest = after((near, own, far, rest))
    near, peer_rest = swap(near, "view", 1), swap(rest, "view", 1)

    residual, own_wide, wide, own_slim, slim = feed_forward(
        codes, summed, own, near, far, rest, combiner, baseline, rescaling, reshifting, expander, priming,
        squeezer, tangent,
    )
    peer_near = swap(near, "view", 1)
    peer_wide, peer_slim = swap(wide, "view", 1), swap(slim, "view", 1)
    residual_grad, resid_low, *grads, rows = feed_back(
        codes, residual, own_wide, wide, tangent, expander, rescaling, combiner
    )
    grads = [grads[0]] + [swap(grads[r], "view", r) for r in (1, 2, 3)]
    other = swap(resid_low, "view", 1)
    outcome = outcome_of(codes, residual, own_wide, wide, squeezer, leveling)
    other, peer_wide, peer_slim, peer_near, peer_rest, outcome = after(
        (other, peer_wide, peer_slim, peer_near, peer_rest, outcome)
    )
    sizes = [(hid + width // 2) // 24, (hid + width // 2) // 48]
    keep0, send0, keep1, send1 = feed_grad(
        codes, sizes, [own_wide, own_slim, peer_wide, peer_slim],
        [own, far, peer_near, peer_rest, resid_low, other],
    )
    *grads, keep0, send0, keep1, send1 = after((*grads, keep0, send0, keep1, send1))
    got0, got1 = swap_by_core(send0, WIDE[0]), swap_by_core(send1, THIN[0])
    dqk, dv, keep, send = attend_back(codes, q, k, v, e0, e1, grads, mix0, mix1, inv0, inv1, normed)
    got0, got1, dqk, dv, keep, send = after((got0, got1, dqk, dv, keep, send))

    def split(keep, got):
        cut = keep.shape[0] // 2
        return keep[:cut] + got[:cut], keep[cut:] + got[cut:]

    got = swap_by_core(send, SCENE[0])
    keep0, send0 = split(keep0, got0)
    keep1, send1 = split(keep1, got1)
    got0, got1 = swap_by_core(send0, WIDE[1]), swap_by_core(send1, THIN[1])
    own, near, far, rest, small = input_grad(
        dqk, dv, padded, unit1, rstd1, scaling, (c0, c1, c2, c3), residual_grad, groups
    )
    got, got0, got1, own, near, far, rest, small = after((got, got0, got1, own, near, far, rest, small))
    near, rest = swap(near, "view", 1), swap(rest, "view", 1)
    keep0, send0 = split(keep0, got0)
    keep1, send1 = split(keep1, got1)
    got0, got1 = swap_by_core(send0, WIDE[2]), swap_by_core(send1, THIN[2])
    keep, send = split(keep, got)
    got = swap_by_core(send, SCENE[1])
    small = rounded(jnp.concatenate([small, rows[:6]], 0)).reshape(-1, 2 * MINE)
    small = whole_slice(small)
    got0, got1, near, rest, small = after((got0, got1, near, rest, small))
    keep0, send0 = split(keep0, got0)
    keep1, send1 = split(keep1, got1)
    joint = jnp.concatenate([keep0, keep1], 0)
    got0 = swap_by_core(jnp.concatenate([send0, send1], 0), WIDE[3])
    far = swap((far + rest.astype(F32)).astype(BF), "view", 2)
    got, got0 = after((got, got0))
    keep, send = split(keep, got)
    got = swap_by_core(send, SCENE[2])
    joint = lax.optimization_barrier(whole_slice(joint + got0))
    got0 = swap_by_core(joint, WIDE[3])
    got, got0 = after((got, got0))
    keep = lax.optimization_barrier(whole_slice(keep + got))
    extra = small.shape[0]

    def grow(keep, small, got):
        small = rounded(small.astype(F32) + got[-extra:].astype(F32))
        return jnp.concatenate([keep, got[:-extra]], 0), small

    got = swap_by_core(jnp.concatenate([keep, small], 0), SCENE[2])
    all0 = jnp.concatenate([joint[: sizes[0]], got0[: sizes[0]]], 0)
    all1 = jnp.concatenate([joint[sizes[0] :], got0[sizes[0] :]], 0)
    got0, got1 = swap_by_core(all0, WIDE[2]), swap_by_core(all1, THIN[2])
    got, got0, got1 = after((got, got0, got1))
    all0, all1 = jnp.concatenate([all0, got0], 0), jnp.concatenate([all1, got1], 0)
    got0, got1 = swap_by_core(all0, WIDE[1]), swap_by_core(all1, THIN[1])
    keep, small = grow(keep, small, got)
    got = swap_by_core(jnp.concatenate([keep, small], 0), (Y, Y))
    inputs_grad = residual_grad + own + near.astype(F32) + far.astype(F32)
    got, got0, got1, inputs_grad = after((got, got0, got1, inputs_grad.astype(BF)))
    all0, all1 = jnp.concatenate([all0, got0], 0), jnp.concatenate([all1, got1], 0)
    got0, got1 = swap_by_core(all0, WIDE[0]), swap_by_core(all1, THIN[0])
    peer0, peer1 = swap(all0, "view", 1), swap(all1, "view", 1)
    keep, small = grow(keep, small, got)
    got = swap_by_core(jnp.concatenate([keep, small], 0), SCENE[1])
    got, peer0, peer1 = after((got, peer0, peer1))
    keep, small = grow(keep, small, got)
    got = swap_by_core(jnp.concatenate([keep, small], 0), SCENE[0])
    got0, got1, got = after((got0, got1, got))
    blocks = [all0, got0, all1, got1, peer0, swap(got0, "view", 1), peer1, swap(got1, "view", 1)]
    keep, small = grow(keep, small, got)
    near, other = swap(keep, "view", 1), swap(small, "view", 1)
    grad_squeezer, grad_expander, grad_combiner = feed_assemble(codes, blocks, hid, width)
    grad_projector = assemble(codes, [keep, near], width)
    vectors = [width] * 6 + [hid]
    table, *vectors = small_outputs(
        small.reshape(-1, width), other.reshape(-1, width), groups, vectors
    )
    grad_scaling, grad_shifting, grad_leveling, grad_baseline, grad_rescaling, grad_reshifting, grad_priming = vectors

    return (
        outcome.reshape(inputs.shape),
        inputs_grad.reshape(inputs.shape),
        table,
        grad_scaling,
        grad_shifting,
        grad_projector,
        grad_combiner,
        grad_baseline,
        grad_rescaling,
        grad_reshifting,
        grad_expander,
        grad_priming,
        grad_squeezer,
        grad_leveling,
    )


def solution(mesh):
    tokens = P("scene", "view", None, None)
    placed = (tokens, P("scene", "view", None)) + (P(),) * 12 + (tokens,)
    return jax.shard_map(
        on_device,
        mesh=mesh,
        in_specs=placed,
        out_specs=(tokens, tokens) + (P(),) * 12,
        check_vma=False,
    )
```

```python
import functools

import jax
import jax.numpy as jnp
from jax import lax
from jax.experimental import pallas as pl
from jax.experimental.pallas import tpu as pltpu
from jax.sharding import PartitionSpec as P

HEADS = 12
HEAD = 64
BF = jnp.bfloat16
F32 = jnp.float32
BOTH = ("scene", "view")
MINE = HEADS // 4 * HEAD
PAD = 256
MIB = 1 << 20


def swap(value, axis, mask):
    count = lax.axis_size(axis)
    return lax.ppermute(value, axis, [(i, i ^ mask) for i in range(count)])


def swap_by_core(value, masks):
    scenes, views = lax.axis_size("scene"), lax.axis_size("view")
    pairs = []
    for s in range(scenes):
        for v in range(views):
            ds, dv = masks[v % 2]
            pairs.append((s * views + v, (s ^ ds) * views + (v ^ dv)))
    return lax.ppermute(value, BOTH, pairs)


def side_of(masks, core):
    scene, view = lax.axis_index("scene"), lax.axis_index("view")
    bits = [((scene & ds) + (view & dv) > 0).astype(jnp.int32) for ds, dv in masks]
    return jnp.where(core == 0, bits[0], bits[1])


def code_of(stages, core):
    total = 0
    for masks in stages:
        total = 2 * total + side_of(masks, core)
    return total


X, Y, Z1, Z2 = (1, 0), (0, 2), (2, 0), (4, 0)
WIDE = ((X, Z1), (Y, X), (Z1, Y), (Z2, Z2))
THIN = ((Y, Y), (Z1, Z1), (X, X), (Z2, Z2))
SCENE = ((X, Z1), (Z1, X), (Z2, Z2))
LATE = ((Y, X), (Z1, Y), (X, Z1))


def rounded(value):
    return lax.optimization_barrier(lax.reduce_precision(value, 8, 7).astype(BF))


def whole_slice(value):
    bit = 8
    while bit < lax.axis_size("scene"):
        value = rounded(value.astype(F32) + swap(value, "scene", bit).astype(F32))
        bit *= 2
    return value


def by_view(blocks, me):
    a, b, c, d = blocks
    one = (me & 1) == 1
    a, b = jnp.where(one, b, a), jnp.where(one, a, b)
    c, d = jnp.where(one, d, c), jnp.where(one, c, d)
    two = (me & 2) == 2
    a, c = jnp.where(two, c, a), jnp.where(two, a, c)
    b, d = jnp.where(two, d, b), jnp.where(two, b, d)
    return a, b, c, d


def normalise(values):
    centre = values - jnp.mean(values, axis=-1, keepdims=True)
    rstd = lax.rsqrt(jnp.mean(centre * centre, axis=-1, keepdims=True) + 1e-05)
    return centre * rstd, rstd


def norm_back(grad, unit, rstd):
    return (
        grad
        - jnp.mean(grad, axis=-1, keepdims=True)
        - unit * jnp.mean(grad * unit, axis=-1, keepdims=True)
    ) * rstd


def dot(a, b):
    return jnp.dot(a, b, preferred_element_type=F32)


def tdot(a, b):
    return lax.dot_general(a, b, (((0,), (0,)), ((), ())), preferred_element_type=F32)


def dott(a, b):
    return lax.dot_general(a, b, (((1,), (1,)), ((), ())), preferred_element_type=F32)


def split3(values):
    high = values.astype(BF)
    rest = values - high.astype(F32)
    middle = rest.astype(BF)
    return high, middle, (rest - middle.astype(F32)).astype(BF)


def onehot_t(cameras, groups):
    rows = lax.broadcasted_iota(jnp.int32, (groups, cameras.shape[1]), 0)
    return (rows == cameras).astype(F32).astype(BF)


class Incoming:
    def __init__(self, source, buffer, sem, whole=None):
        self.copy, self.there = pltpu.make_async_copy(source, buffer, sem), False
        self.buffer = buffer if whole is None else whole
        self.copy.start()

    def __call__(self):
        if not self.there:
            self.copy.wait()
            self.there = True
        return self.buffer


class Present:
    def __init__(self, ref):
        self.buffer = ref

    def __call__(self):
        return self.buffer


class Outgoing:
    def __init__(self, target, buffer, sems, moves):
        self.target, self.ref, self.sems, self.moves = target, buffer, sems, moves

    def send(self, here=None, there=None):
        source = self.ref if here is None else self.ref.at[here]
        target = self.target if there is None else self.target.at[there]
        move = pltpu.make_async_copy(source, target, self.sems.at[len(self.moves)])
        move.start()
        self.moves.append(move)


class Operand:
    def __init__(self, array, *, home=False, ready=False, cut=None, shape=None):
        self.array, self.ready, self.cut, self.apart = array, ready, cut, False
        if home:
            self.array = pltpu.with_memory_space_constraint(array, pltpu.HBM)
        self.shape = array.shape if shape is None else shape


def apart(array):
    operand = Operand(array, home=True)
    operand.apart = True
    return operand


def home(array, **more):
    return Operand(array, home=True, **more)


def ready(array):
    return Operand(array, ready=True)


def staged(body, args, outs, *, name, mib, us, scratch=(), code=None, held=(), buffers=None):
    buffers = buffers or {}
    args = [a if isinstance(a, Operand) else home(a) for a in args]
    n_code, n_in, n_held, n_out = int(code is not None), len(args), len(held), len(outs)
    loads = [i for i, a in enumerate(args) if not (a.ready or a.apart)]

    def kernel(*refs):
        code_ref = refs[0] if n_code else None
        refs = refs[n_code:]
        ins, refs = refs[:n_in], refs[n_in + n_held :]
        targets, refs = refs[:n_out], refs[n_out:]
        in_bufs, refs = refs[: len(loads)], refs[len(loads) :]
        out_bufs, refs = refs[:n_out], refs[n_out:]
        in_sems, out_sems, rest = refs[0], refs[1], refs[2:]
        arrivals = [Present(ref) for ref in ins]
        for n, i in enumerate(loads):
            source = ins[i] if args[i].cut is None else ins[i].at[args[i].cut]
            arrivals[i] = Incoming(source, in_bufs[n], in_sems.at[n])
        moves = []
        leaving = [Outgoing(t, b, out_sems, moves) for t, b in zip(targets, out_bufs, strict=True)]
        body(code_ref, arrivals, leaving, *rest)
        for arrival in arrivals:
            arrival()
        for move in moves:
            move.wait()

    anywhere, vmem = pl.BlockSpec(memory_space=pl.ANY), pl.BlockSpec(memory_space=pltpu.VMEM)
    specs = [pl.BlockSpec(memory_space=pltpu.SMEM)] * n_code
    specs += [vmem if a.ready else anywhere for a in args] + [anywhere] * n_held
    operands = ([code] if n_code else []) + [a.array for a in args]
    operands += [pltpu.with_memory_space_constraint(a, pltpu.HBM) for a in held]
    bufs = [pltpu.VMEM(args[i].shape, args[i].array.dtype) for i in loads]
    return pl.pallas_call(
        kernel,
        in_specs=specs,
        out_specs=[anywhere] * n_out,
        out_shape=[pltpu.HBM(shape, dtype) for shape, dtype in outs],
        scratch_shapes=bufs
        + [pltpu.VMEM(buffers.get(i, o[0]), o[1]) for i, o in enumerate(outs)]
        + [pltpu.SemaphoreType.DMA((max(len(loads), 1),)), pltpu.SemaphoreType.DMA((48,))]
        + list(scratch),
        input_output_aliases={n_code + n_in + i: i for i in range(n_held)},
        compiler_params=pltpu.CompilerParams(vmem_limit_bytes=mib * MIB),
        cost_estimate=pl.CostEstimate(flops=0, bytes_accessed=0, transcendentals=0),
        name=name,
    )(*operands)


def project_rows(tokens, cams, embedding, gain, shift, weight, outs, there, hold_ref, summed=None):
    normed, unit, rstd, *triple = outs
    rows = tokens[0].buffer.shape[0]
    pair = 2 * rows
    table = jnp.concatenate(split3(embedding()[...]), 0)
    for at, x in enumerate(tokens):
        hot = onehot_t(cams()[at : at + 1, :], embedding().shape[0])
        values = x()[...].astype(F32) + tdot(jnp.concatenate([hot] * 3, 0), table)
        if at == 0 and summed is not None:
            summed.ref[...] = values
            summed.send()
        values, scale = normalise(values)
        hold_ref[pl.ds(at * rows, rows), :] = values
        rstd.ref[pl.ds(at * rows, rows), :] = scale
    values = hold_ref[...]
    low = (values * gain()[...] + shift()[...]).astype(BF)
    normed.ref[...] = low
    lane = lax.broadcasted_iota(jnp.int32, (pair, PAD), 1)
    for i, (ref, first, out) in enumerate(triple):
        block = dot(low, weight()[:, i * PAD : (i + 1) * PAD])
        if i == 0:
            block = block * HEAD**-0.5
        if i == 2:
            block = jnp.where(lane < MINE, block, 1.0)
        ref[first : first + pair, :] = block.astype(BF)
        out.send((pl.ds(first, pair),), there)
    normed.send(None, there)
    unit.ref[...] = values.astype(BF)
    unit.send(None, there)
    rstd.send(None, there)


def project_outs(total, width):
    outs = [((total, width), BF), ((total, width), BF), ((total, 1), F32)]
    return outs + [((total, PAD), BF)] * 3


def project_body(_, ins, outs, hold_ref):
    xa, xb, cams, embedding, gain, shift, weight = ins
    there = (pl.ds(0, hold_ref.shape[0]),)
    triple = [(out.ref, 0, out) for out in outs[3:6]]
    project_rows((xa, xb), cams, embedding, gain, shift, weight, [*outs[:3], *triple], there, hold_ref, outs[6])


def project(xa, xb, cams, embedding, gain, shift, weight):
    rows, width = xa.shape[-2:]
    pair, total = 2 * rows, 4 * rows
    outs = project_outs(total, width)
    return staged(
        project_body,
        [xa, ready(xb), cams, embedding, gain, shift, weight],
        [*outs, ((rows, width), F32)],
        name="project",
        mib=32,
        us=5,
        scratch=[pltpu.VMEM((pair, width), F32)],
        buffers={i: (pair, o[0][1]) for i, o in enumerate(outs)},
    )


def blocks_of(total):
    return [(at, min(256, total - at)) for at in range(0, total, 256)]


TILE = 128


def tile_of(head):
    at = head * HEAD // TILE * TILE
    return slice(at, at + TILE)


def one_head(block, head):
    lane = lax.broadcasted_iota(jnp.int32, block.shape, 1) // HEAD
    return jnp.where(lane == head % (TILE // HEAD), block, jnp.zeros_like(block))


def attend_rows(q_ref, keys, values_of, outs, vt_ref, mt_ref):
    e, first, second, inv = outs
    pair, heads = q_ref.shape[0], e.ref.shape[0]
    work = [(h, at, size) for h in range(heads) for at, size in blocks_of(pair)]

    def scores(h, at, size):
        return dott(keys()[:, tile_of(h)], one_head(q_ref[at : at + size, tile_of(h)], h))

    keys(), values_of()
    ahead = scores(*work[0])
    vt_ref[...] = values_of()[...].astype(F32).T.astype(BF)
    mt_ref[...] = jnp.zeros_like(mt_ref)
    inv.ref[...] = jnp.zeros_like(inv.ref)
    for i, (h, at, size) in enumerate(work):
        here = ahead
        if i + 1 < len(work):
            ahead = scores(*work[i + 1])
        mine = slice(h * HEAD, (h + 1) * HEAD)
        expo = jnp.exp(here - jnp.max(here, 0, keepdims=True)).astype(BF)
        cut = (h, slice(None), slice(at, at + size))
        e.ref[cut] = expo
        if at + size == pair:
            e.send((h,), (h,))
        values = jnp.concatenate([vt_ref[mine, :], vt_ref[MINE : MINE + 16, :]], 0)
        out = dot(values, expo)
        inverse = 1.0 / out[HEAD : HEAD + 1, :]
        mt_ref[mine, at : at + size] = out[:HEAD, :] * inverse
        inv.ref[h : h + 1, at : at + size] = inverse
    mixed = mt_ref[...].T[:pair]
    first.ref[...] = mixed[: pair // 2, :MINE].astype(BF)
    first.send()
    second.ref[...] = mixed[pair // 2 :, :MINE].astype(BF)
    second.send()
    inv.send()


def attend_outs(total):
    pair, heads = total // 2, MINE // HEAD
    wide = -(-pair // 128) * 128
    part = ((pair // 2, MINE), BF)
    return [((heads, total, pair), BF), part, part, ((8, wide), F32)]


def attend_scratch(total):
    wide = -(-(total // 2) // 128) * 128
    return [pltpu.VMEM((PAD, total), BF), pltpu.VMEM((PAD, wide), F32)]


def attend_body(_, ins, outs, *scratch):
    q, k, v = ins
    attend_rows(q(), k, v, outs, *scratch)


def attend(q, k, v):
    total = k.shape[0]
    pair = total // 2
    return staged(
        attend_body,
        [home(q, cut=(pl.ds(0, pair),), shape=(pair, PAD)), home(k), home(v)],
        attend_outs(total),
        name="attend",
        mib=32,
        us=8,
        scratch=attend_scratch(total),
    )


def second_body(_, ins, outs, hold_ref, *scratch):
    xa, xb, cams, embedding, gain, shift, weight = ins
    pair = hold_ref.shape[0]
    keys_ref, values_ref, sems, *scratch = scratch
    first = pl.ds(0, pair)
    k, v = (
        Incoming(out.target.at[first], ref.at[first], sems.at[i], ref)
        for i, (out, ref) in enumerate(((outs[4], keys_ref), (outs[5], values_ref)))
    )
    there = (pl.ds(pair, pair),)
    triple = [(outs[3].ref, 0, outs[3]), (k.buffer, pair, outs[4]), (v.buffer, pair, outs[5])]
    outs[4].ref, outs[5].ref = k.buffer, v.buffer
    project_rows((xa, xb), cams, embedding, gain, shift, weight, [*outs[:3], *triple], there, hold_ref)
    attend_rows(outs[3].ref, k, v, outs[6:], *scratch)
    k()
    v()


def second_half(xa, xb, cams, embedding, gain, shift, weight, held):
    rows, width = xa.shape[-2:]
    pair, total = 2 * rows, 4 * rows
    outs = project_outs(total, width)
    buffers = {i: (pair, o[0][1]) for i, o in enumerate(outs)}
    buffers[4] = buffers[5] = (16, PAD)
    return staged(
        second_body,
        [xa, ready(xb), ready(cams), embedding, gain, shift, weight],
        [*outs, *attend_outs(total)],
        name="second_half",
        mib=44,
        us=10,
        scratch=[
            pltpu.VMEM((pair, width), F32),
            pltpu.VMEM((total, PAD), BF),
            pltpu.VMEM((total, PAD), BF),
            pltpu.SemaphoreType.DMA((2,)),
            *attend_scratch(total),
        ],
        held=held,
        buffers=buffers,
    )


def back_body(code, ins, outs, g_ref, kt_ref, delta_ref, dq_ref, dk_ref, dv_ref, hold_ref, piece_ref):
    q, k, v, *ins = ins
    grads, mixes, invs, expos, normed = ins[:4], ins[4:8], ins[8:10], ins[10:-1], ins[-1]
    dqk, dv, keep, send = outs
    total = q.buffer.shape[0]
    heads = len(expos) // 2
    pair, rows = total // 2, grads[0].buffer.shape[0]
    for arrival in (q, k, v, *grads, *mixes, *invs, *expos[:2]):
        arrival()
    hold_ref[...] = jnp.zeros_like(hold_ref)
    for i, grad in enumerate(grads):
        hold_ref[i * rows : (i + 1) * rows, :MINE] = grad()[...].astype(F32)
    lane = lax.broadcasted_iota(jnp.int32, (8, PAD), 1) // HEAD
    pick = (lane == lax.broadcasted_iota(jnp.int32, (8, PAD), 0)).astype(F32).astype(BF)
    for i in range(2):
        here = slice(i * pair, (i + 1) * pair)
        inverse = invs[i]()[...].T[:pair, :]
        lane = lax.broadcasted_iota(jnp.int32, (pair, PAD), 1) // HEAD
        scale = jnp.zeros((pair, PAD), F32)
        for h in range(heads):
            scale = jnp.where(lane == h, inverse[:, h : h + 1], scale)
        g_ref[here, :] = (hold_ref[here, :] * scale).astype(BF)
        for j in range(2):
            rows_here = slice(i * pair + j * rows, i * pair + (j + 1) * rows)
            hold_ref[rows_here, :MINE] = mixes[2 * i + j]()[...].astype(F32)
        prod = g_ref[here, :].astype(F32) * hold_ref[here, :]
        high = prod.astype(BF)
        low = (prod - high.astype(F32)).astype(BF)
        delta_ref[i, :, :pair] = dott(pick, high) + dott(pick, low)
    kt_ref[...] = k()[...].astype(F32).T.astype(BF)
    dq_ref[...] = jnp.zeros_like(dq_ref)
    work = [(h, i, at, size) for h in range(heads) for i in range(2) for at, size in blocks_of(pair)]

    def cut(ref, h, i, at, size):
        return one_head(ref[i * pair + at : i * pair + at + size, tile_of(h)], h)

    ahead_grad = cut(g_ref, *work[0])
    ahead = dott(v()[:, tile_of(0)], ahead_grad)
    begun = set()
    for n, (h, i, at, size) in enumerate(work):
        if i == at == 0:
            expos[2 * h]()
            expos[2 * h + 1]()
        grad, prob_grad = ahead_grad, ahead
        if n + 1 < len(work):
            ahead_grad = cut(g_ref, *work[n + 1])
            ahead = dott(v()[:, tile_of(work[n + 1][0])], ahead_grad)
        expo = expos[2 * h + i]()[:, at : at + size]
        delta = delta_ref[i, h : h + 1, at : at + size]
        score_grad = (expo.astype(F32) * (prob_grad - delta)).astype(BF)
        value_part = dot(expo, grad)
        key_part = dot(score_grad, cut(q(), h, i, at, size))
        t = h * HEAD // TILE
        if t in begun:
            value_part += dv_ref[t]
            key_part += dk_ref[t]
        begun.add(t)
        dv_ref[t] = value_part
        dk_ref[t] = key_part
        mine = slice(h * HEAD, (h + 1) * HEAD)
        dq_ref[i, mine, at : at + size] = dot(kt_ref[mine, :], score_grad)
    for i in range(2):
        dq = dq_ref[i].T[:pair] * HEAD**-0.5
        dqk.ref[i * pair : (i + 1) * pair, :MINE] = dq[:, :MINE].astype(BF)
    rest = MINE - TILE
    dqk.ref[:, MINE : MINE + TILE] = dk_ref[0].astype(BF)
    dqk.ref[:, MINE + TILE :] = dk_ref[1][:, :rest].astype(BF)
    dv.ref[:, :TILE] = dv_ref[0].astype(BF)
    dv.ref[:, TILE:] = dv_ref[1][:, :rest].astype(BF)
    weight_grad(code, normed, dqk.ref, dv.ref, keep, send, piece_ref)
    dqk.send()
    dv.send()


PIECES = 8


def weight_grad(code, normed, dqk_ref, dv_ref, keep, send, hold_ref):
    width = normed().shape[1]
    rows = width // PIECES
    piece = rows + rows // 2
    mine = code[0]
    qk = tdot(normed()[...], dqk_ref[...]).astype(BF)
    v = tdot(normed()[...], dv_ref[...]).astype(BF)
    for p in range(PIECES):
        at = pl.multiple_of((p ^ mine) * piece, 16)
        hold_ref[pl.ds(at, rows), :] = qk[p * rows : (p + 1) * rows]
        at = pl.multiple_of((p ^ mine) * piece + rows, 16)
        top = v[p * rows : p * rows + rows // 2]
        low = v[p * rows + rows // 2 : (p + 1) * rows]
        hold_ref[pl.ds(at, rows // 2), :] = jnp.concatenate([top, low], 1)
    half = PIECES * piece // 2
    send.ref[...] = hold_ref[half:, :]
    send.send()
    keep.ref[...] = hold_ref[:half, :]
    keep.send()


def attend_back(codes, q, k, v, e0, e1, grads, mixes, inv0, inv1, normed):
    total, heads = k.shape[0], MINE // HEAD
    pair, width = total // 2, normed.shape[1]
    wide = -(-pair // 128) * 128
    piece = width // PIECES * 3 // 2
    half = ((PIECES * piece // 2, 2 * MINE), BF)
    args = [q, k, v, grads[0], *map(ready, grads[1:]), *mixes, inv0, inv1]
    for h in range(heads):
        args += [home(e, cut=(h,), shape=(total, pair)) for e in (e0, e1)]
    return staged(
        back_body,
        [*args, normed],
        [((total, 2 * MINE), BF), ((total, MINE), BF), half, half],
        name="attend_back",
        mib=48,
        us=20,
        scratch=[
            pltpu.VMEM((total, PAD), BF),
            pltpu.VMEM((PAD, total), BF),
            pltpu.VMEM((2, 8, wide), F32),
            pltpu.VMEM((2, PAD, wide), F32),
            pltpu.VMEM((2, total, TILE), F32),
            pltpu.VMEM((2, total, TILE), F32),
            pltpu.VMEM((total, PAD), F32),
            pltpu.VMEM((PIECES * piece, 2 * MINE), BF),
        ],
        code=codes,
    )


STEP = 512


def feed_forward_body(code, ins, outs):
    summed, own, near, far, rest, combiner, baseline, gain, shift, expander, priming, squeezer, tangent = ins
    residual, own_wide, wide, own_slim, slim = outs
    me = code[2]
    first = code[3] == 0
    total = summed()[...] + baseline()[...]
    for r, block in ((2, far), (3, rest), (0, own), (1, near)):
        at = pl.multiple_of((me ^ r) * MINE, 16)
        total += dot(block()[...], combiner()[pl.ds(at, MINE), :])
    residual.ref[...] = total
    residual.send()
    unit, _ = normalise(total)
    low = (unit * gain()[...] + shift()[...]).astype(BF)
    own_slim.ref[...] = jnp.where(first, tangent()[...], low)
    own_slim.send()
    slim.ref[...] = jnp.where(first, low, tangent()[...])
    slim.send()
    for at in range(0, expander().shape[1], STEP):
        cut = slice(at, at + STEP)
        hidden = dot(low, expander()[:, cut]) + priming()[cut]
        back = dott(tangent()[...], squeezer()[cut, :])
        phi = 0.5 * (1.0 + lax.erf(hidden * (2.0**-0.5)))
        density = jnp.exp(-0.5 * hidden * hidden) * 0.3989422804014327
        active = (hidden * phi).astype(BF)
        grad = (back * (phi + hidden * density)).astype(BF)
        own_wide.ref[:, cut] = jnp.where(first, active, grad)
        wide.ref[:, cut] = jnp.where(first, grad, active)
        part = (slice(None), pl.ds(at, STEP))
        own_wide.send(part, part)
        wide.send(part, part)


def feed_forward(codes, summed, own, near, far, rest, combiner, baseline, gain, shift, expander, priming, squeezer, tangent):
    rows, width = summed.shape
    hid = expander.shape[1]
    weights = [combiner, baseline, gain, shift, expander, priming, squeezer, tangent]
    return staged(
        feed_forward_body,
        [home(summed), own, ready(near), ready(far), ready(rest), *weights],
        [((rows, width), F32), ((rows, hid), BF), ((rows, hid), BF), ((rows, width), BF), ((rows, width), BF)],
        name="feed_forward",
        mib=24,
        us=6,
        code=codes,
    )


def feed_back_body(code, ins, outs, grad_ref, sem):
    residual, tangent, expander, gain, combiner, own_wide, wide = ins
    residual_grad, low, *grads, rows = outs
    me = code[2]

    for core, source in enumerate((wide, own_wide)):

        @pl.when(code[3] == core)
        def _():
            pltpu.make_async_copy(source(), grad_ref, sem.at[0]).start()

    pltpu.make_async_copy(wide(), grad_ref, sem.at[0]).wait()
    second_grad = dott(grad_ref[...], expander()[...])
    unit, rstd = normalise(residual()[...])
    slope = tangent()[...].astype(F32)
    total = slope + norm_back(second_grad * gain()[...], unit, rstd)
    low.ref[...] = total.astype(BF)
    low.send()
    for r in (2, 3, 1, 0):
        at = pl.multiple_of((me ^ r) * MINE, 16)
        grads[r].ref[...] = dott(low.ref[...], combiner()[pl.ds(at, MINE), :]).astype(BF)
        grads[r].send()
    residual_grad.ref[...] = total
    residual_grad.send()
    width = total.shape[1]
    rows.ref[0:1, :] = jnp.sum(slope, 0, keepdims=True)
    rows.ref[1:2, :] = jnp.sum(low.ref[...].astype(F32), 0, keepdims=True)
    rows.ref[2:3, :] = jnp.sum(second_grad * unit, 0, keepdims=True)
    rows.ref[3:4, :] = jnp.sum(second_grad, 0, keepdims=True)
    for j in range(grad_ref.shape[1] // width):
        block = grad_ref[:, j * width : (j + 1) * width].astype(F32)
        rows.ref[4 + j : 5 + j, :] = jnp.sum(block, 0, keepdims=True)
    rows.ref[6:8, :] = jnp.zeros((2, width), F32)
    rows.send()


def feed_back(codes, residual, own_wide, wide, tangent, expander, gain, combiner):
    rows, width = residual.shape
    return staged(
        feed_back_body,
        [home(residual), tangent, expander, gain, combiner, apart(own_wide), apart(wide)],
        [((rows, width), F32), ((rows, width), BF)] + [((rows, MINE), BF)] * 4 + [((8, width), F32)],
        name="feed_back",
        mib=24,
        us=6,
        scratch=[pltpu.VMEM(wide.shape, BF), pltpu.SemaphoreType.DMA((1,))],
        code=codes,
    )


def outcome_body(code, ins, outs, active_ref, sem):
    residual, squeezer, leveling, own_wide, wide = ins

    for core, source in enumerate((own_wide, wide)):

        @pl.when(code[3] == core)
        def _():
            pltpu.make_async_copy(source(), active_ref, sem.at[0]).start()

    pltpu.make_async_copy(wide(), active_ref, sem.at[0]).wait()
    outs[0].ref[...] = (residual()[...] + dot(active_ref[...], squeezer()[...]) + leveling()[...]).astype(BF)
    outs[0].send()


def outcome_of(codes, residual, own_wide, wide, squeezer, leveling):
    rows, width = residual.shape
    return staged(
        outcome_body,
        [home(residual), squeezer, leveling, apart(own_wide), apart(wide)],
        [((rows, width), BF)],
        name="outcome",
        mib=16,
        us=4,
        scratch=[pltpu.VMEM(wide.shape, BF), pltpu.SemaphoreType.DMA((1,))],
        code=codes,
    )[0]


PARTS = 16


def place(code, piece, size):
    return pl.multiple_of((piece ^ code) * size, 8)


def segments(first, rows, low, size):
    out, at = [], first
    while at < first + rows:
        piece, offset = divmod(at - low, size)
        count = min(size - offset, first + rows - at)
        out.append((piece, offset, at - first, count))
        at += count
    return out


def spread(hold_ref, block, first, low, size, code):
    for piece, offset, start, count in segments(first, block.shape[0], low, size):
        at = pl.multiple_of(place(code, piece, size) + offset, 8)
        hold_ref[pl.ds(at, count), :] = block[start : start + count]


def feed_grad_body(sizes, code, ins, outs, mine_ref, peer_ref, sems, *holds):
    own_wide, own_slim, wide, slim, own, far, near, rest, resid, other = ins
    hid, width = own_wide().shape[1], own_slim().shape[1]
    assert hid == 2 * width
    bulk = PARTS * sizes[0]
    loads = []
    for n, (hold_ref, big, small) in enumerate(((mine_ref, own_wide, own_slim), (peer_ref, wide, slim))):
        for j in range(hid // width):
            loads.append(pltpu.make_async_copy(big().at[:, pl.ds(j * width, width)], hold_ref.at[j], sems.at[3 * n + j]))
        loads.append(pltpu.make_async_copy(small(), hold_ref.at[2], sems.at[3 * n + 2]))
    for load in loads:
        load.start()
    for load in loads:
        load.wait()

    def put(block, row):
        for part, low, high in ((0, 0, bulk), (1, bulk, bulk + PARTS * sizes[1])):
            first, last = max(row, low), min(row + block.shape[0], high)
            if first < last:
                spread(holds[part], block[first - row : last - row], first, low, sizes[part], code[4 + 2 * part])

    for j in range(hid // width):
        left = jnp.where(code[3] == 0, j, 2)
        right = jnp.where(code[3] == 0, 2, j)
        block = tdot(mine_ref[left], mine_ref[right]) + tdot(peer_ref[left], peer_ref[right])
        put(block, j * width)

    upper = code[2] < 2
    for i in range(2):
        here = jnp.where(upper, (own, far)[i]()[...], (far, own)[i]()[...])
        peer = jnp.where(upper, (near, rest)[i]()[...], (rest, near)[i]()[...])
        put(tdot(here, resid()[...]) + tdot(peer, other()[...]), hid + i * MINE)
    for part, hold_ref in enumerate(holds):
        keep, send = outs[2 * part : 2 * part + 2]
        half = hold_ref.shape[0] // 2
        send.ref[...] = hold_ref[half:, :].astype(BF)
        send.send()
        keep.ref[...] = hold_ref[:half, :].astype(BF)
        keep.send()


def feed_grad(codes, sizes, feed, mixed):
    rows, width = feed[1].shape
    halves = [((PARTS * size // 2, width), BF) for size in sizes]
    return staged(
        functools.partial(feed_grad_body, sizes),
        [apart(feed[0]), apart(feed[1]), *map(ready, feed[2:]), mixed[0], *map(ready, mixed[1:4]), mixed[4], ready(mixed[5])],
        [halves[0], halves[0], halves[1], halves[1]],
        name="feed_grad",
        mib=40,
        us=7,
        scratch=[
            pltpu.VMEM((3, rows, width), BF),
            pltpu.VMEM((3, rows, width), BF),
            pltpu.SemaphoreType.DMA((6,)),
            *[pltpu.VMEM((PARTS * size, width), F32) for size in sizes],
        ],
        code=codes,
    )


def feed_assemble_body(half, sizes, code, ins, outs, sems, *holds):
    squeezer, expander, combiner = (out.target for out in outs)
    hid, width = squeezer.shape

    def targets(core, row, count):
        out = []
        while count:
            if row < hid and core == 0:
                take = min(count, hid - row)
                out.append((squeezer.at[pl.ds(row, take), :], take))
            elif row < hid:
                j = row // width
                take = min(count, (j + 1) * width - row)
                cut = pl.ds(row - j * width, take), pl.ds(j * width, width)
                out.append((expander.at[cut], take))
            else:
                view, at = divmod(row - hid, MINE)
                take = min(count, MINE - at)
                out.append((combiner.at[pl.ds((core + 2 * view) * MINE + at, take), :], take))
            row, count = row + take, count - take
        return out

    for hold_ref, block in zip(holds, ins, strict=True):
        hold_ref[...] = block()[...].astype(F32)
    for action in ("start", "wait"):
        for me in range(2):
            number = 0
            for side in range(2):
                core = me if side == 0 else 1 - me
                low = 0
                for part, size in enumerate(sizes):
                    for piece in range(PARTS):
                        there = piece ^ code[4 + 2 * part + side]
                        moves, at = [], 0
                        for target, count in targets(core, low + piece * size, size):
                            moves.append((at, count, target, number))
                            at, number = at + count, number + 1

                        @pl.when((code[3] == me) & (there // 8 == half))
                        def _():
                            for at, count, target, n in moves:
                                start = pl.multiple_of(there % 8 * size + at, 8)
                                source = holds[2 * side + part].at[pl.ds(start, count), :]
                                getattr(pltpu.make_async_copy(source, target, sems.at[n]), action)()

                    low += PARTS * size


def feed_assemble(codes, half, blocks, hid, held=()):
    width = blocks[0].shape[1]
    sizes = [blocks[0].shape[0] // 8, blocks[1].shape[0] // 8]
    return staged(
        functools.partial(feed_assemble_body, half, sizes),
        blocks,
        [((hid, width), F32), ((width, hid), F32), ((width, width), F32)],
        name="feed_assemble",
        mib=24,
        us=6,
        scratch=[pltpu.SemaphoreType.DMA((96,))] + [pltpu.VMEM(b.shape, F32) for b in blocks],
        code=codes,
        held=held,
        buffers={0: (8, 128), 1: (8, 128), 2: (8, 128)},
    )


def input_grad_body(_, ins, outs, hold_ref):
    dqk, dv, weight, unit, rstd, gain, *rest = ins
    near_cams, far_cams, resid = rest
    small = outs[4]
    patches = resid.buffer.shape[0]
    groups = small.ref.shape[0] - 2
    slope = dott(dqk()[:, :MINE], weight()[:, :MINE]) + dott(dqk()[:, MINE:], weight()[:, PAD : PAD + MINE])
    slope += dott(dv()[...], weight()[:, 2 * PAD : 2 * PAD + MINE])
    values = unit()[...].astype(F32)
    small.ref[groups : groups + 1, :] = jnp.sum(slope * values, 0, keepdims=True)
    small.ref[groups + 1 : groups + 2, :] = jnp.sum(slope, 0, keepdims=True)
    hold_ref[...] = norm_back(slope * gain()[...], values, rstd()[...])
    table = jnp.zeros((groups, slope.shape[1]), F32)
    for r in (1, 3, 0, 2):
        part = hold_ref[r * patches : (r + 1) * patches, :]
        outs[r].ref[...] = part.astype(outs[r].ref.dtype)
        outs[r].send()
        if r == 0:
            part = part + resid()[...]
        hot = onehot_t((near_cams, far_cams)[r // 2]()[r % 2 : r % 2 + 1, :], groups)
        for piece in split3(part):
            table += dot(hot, piece)
    small.ref[:groups, :] = table
    small.send()


def input_grad(dqk, dv, weight, unit, rstd, gain, cams, resid, groups):
    total, width = unit.shape
    patches = resid.shape[0]
    low, full = ((patches, width), BF), ((patches, width), F32)
    return staged(
        input_grad_body,
        [home(dqk), home(dv), home(weight), home(unit), home(rstd), gain, *cams, home(resid)],
        [full, low, full, low, ((groups + 2, width), F32)],
        name="input_grad",
        mib=48,
        us=9,
        scratch=[pltpu.VMEM((total, width), F32)],
    )


def assemble_kernel(code_ref, *refs):
    refs, out_ref = refs[:-1], refs[-1]
    me, p = code_ref[2], pl.program_id(0)
    rows = out_ref.shape[0]
    width = out_ref.shape[1] // 3
    blocks = []
    for i in range(4):
        upper = (p ^ code_ref[i % 2]) >= PIECES // 2
        blocks.append(jnp.where(upper, refs[2 * i + 1][...], refs[2 * i][...]).astype(F32))
    for v, block in enumerate(by_view(blocks, me)):
        at = v * MINE
        out_ref[:, at : at + MINE] = block[:rows, :MINE]
        out_ref[:, width + at : width + at + MINE] = block[:rows, MINE:]
        out_ref[: rows // 2, 2 * width + at : 2 * width + at + MINE] = block[rows:, :MINE]
        out_ref[rows // 2 :, 2 * width + at : 2 * width + at + MINE] = block[rows:, MINE:]


def assemble(codes, blocks, width):
    rows = width // PIECES
    piece = rows * 3 // 2

    def part(which, far):
        def place(p, code):
            r = (p ^ code[which]) % 4
            core = code[3] if which == 0 else 1 - code[3]
            middle = jnp.where(core == 0, r // 2 * 2 + far, far * 2 + r // 2)
            return (middle * 2 + r % 2, 0)

        return [pl.BlockSpec((piece, 2 * MINE), place)] * 2

    own, own_got, near, near_got = blocks
    return pl.pallas_call(
        assemble_kernel,
        grid_spec=pltpu.PrefetchScalarGridSpec(
            num_scalar_prefetch=1,
            grid=(PIECES,),
            in_specs=[*part(0, 0), *part(1, 0), *part(0, 1), *part(1, 1)],
            out_specs=pl.BlockSpec((rows, 3 * width), lambda p, code: (p, 0)),
        ),
        out_shape=jax.ShapeDtypeStruct((width, 3 * width), F32),
        compiler_params=pltpu.CompilerParams(vmem_limit_bytes=24 * MIB),
        cost_estimate=pl.CostEstimate(flops=0, bytes_accessed=0, transcendentals=0),
        name="assemble",
    )(codes, own, own_got, near, near_got, own, own_got, near, near_got)


def small_kernel(here_ref, there_ref, table_ref, *refs):
    groups, width = table_ref.shape
    total = here_ref[...].astype(F32) + there_ref[...].astype(F32)
    rows, half = total.shape[0] // 2, width // 2
    table_ref[:, :half] = total[:groups, :]
    table_ref[:, half:] = total[rows : rows + groups, :]
    row = groups
    for ref in refs:
        for at in range(0, ref.shape[0], width):
            ref[at : at + half] = total[row, :]
            ref[at + half : at + width] = total[rows + row, :]
            row += 1


def small_outputs(here, there, groups, sizes):
    shapes = [(groups, 2 * here.shape[1])] + [(n,) for n in sizes]
    return pl.pallas_call(
        small_kernel,
        out_shape=[jax.ShapeDtypeStruct(s, F32) for s in shapes],
        cost_estimate=pl.CostEstimate(flops=0, bytes_accessed=0, transcendentals=0),
        name="small_outputs",
    )(here, there)


def turned(block):
    half = block.shape[0] // 2
    return jnp.concatenate([block[half:], block[:half]], 0)


def after(values, *others):
    out = lax.optimization_barrier((*values, *others))
    return out[: len(values)]


def on_device(
    inputs,
    cameras,
    embedding,
    scaling,
    shifting,
    projector,
    combiner,
    baseline,
    rescaling,
    reshifting,
    expander,
    priming,
    squeezer,
    leveling,
    cotangent,
):
    me = lax.axis_index("view")
    core = me % 2
    patches, width = inputs.shape[2], inputs.shape[3]
    groups, hid = embedding.shape[0], expander.shape[1]
    codes = [code_of(SCENE, core), code_of(SCENE, 1 - core), me, core]
    codes += [code_of(WIDE, core), code_of(WIDE, 1 - core), code_of(THIN, core), code_of(THIN, core)]
    codes = jnp.stack(codes).astype(jnp.int32)
    tangent = cotangent.reshape(patches, width)
    x0 = inputs.reshape(patches, width)
    c0 = cameras.reshape(1, patches)
    x2 = swap(x0, "view", 2)
    x1, c1 = swap(x0, "view", 1), swap(c0, "view", 1)
    near_cams = jnp.concatenate([c0, c1], 0)
    far_cams = swap(near_cams, "view", 2)
    hole = jnp.zeros((width, PAD - MINE), BF)
    padded = []
    for part in range(3):
        padded += [lax.dynamic_slice_in_dim(projector, part * width + me * MINE, MINE, 1), hole]
    padded = jnp.concatenate(padded, 1)
    *held, summed = project(x0, x1, near_cams, embedding, scaling, shifting, padded)
    x2, far_cams = after((x2, far_cams), *held)
    x3 = swap(x2, "view", 1)
    normed, unit1, rstd1, q, k, v, e1, far, rest, inv1 = second_half(
        x2, x3, far_cams, embedding, scaling, shifting, padded, held
    )
    mine_far, mine_rest = far, rest
    far, rest = swap(far, "view", 2), swap(rest, "view", 3)
    e0, own, near, inv0 = attend(q, k, v)
    mixes = [own, near, mine_far, mine_rest]
    near, own, far, rest = after((near, own, far, rest))
    near, peer_rest = swap(near, "view", 1), swap(rest, "view", 1)

    residual, own_wide, wide, own_slim, slim = feed_forward(
        codes, summed, own, near, far, rest, combiner, baseline, rescaling, reshifting, expander, priming,
        squeezer, tangent,
    )
    peer_near = swap(near, "view", 1)
    peer_wide, peer_slim = swap(wide, "view", 1), swap(slim, "view", 1)
    residual_grad, resid_low, *grads, rows = feed_back(
        codes, residual, own_wide, wide, tangent, expander, rescaling, combiner
    )
    grads = [grads[0]] + [swap(grads[r], "view", r) for r in (1, 2, 3)]
    other = swap(resid_low, "view", 1)
    sizes = [(hid + width // 2) // 24, (hid + width // 2) // 48]
    keep0, send0, keep1, send1 = feed_grad(
        codes, sizes, [own_wide, own_slim, peer_wide, peer_slim],
        [own, far, peer_near, peer_rest, resid_low, other],
    )
    *grads, keep0, send0, keep1, send1 = after((*grads, keep0, send0, keep1, send1))
    got0, got1 = swap_by_core(send0, WIDE[0]), swap_by_core(send1, THIN[0])
    dqk, dv, keep, send = attend_back(codes, q, k, v, e0, e1, grads, mixes, inv0, inv1, normed)
    got0, got1, dqk, dv, keep, send = after((got0, got1, dqk, dv, keep, send))

    def split(keep, got):
        cut = keep.shape[0] // 2
        return keep[:cut] + got[:cut], keep[cut:] + got[cut:]

    got = swap_by_core(send, SCENE[0])
    keep0, send0 = split(keep0, got0)
    keep1, send1 = split(keep1, got1)
    got0, got1 = swap_by_core(send0, WIDE[1]), swap_by_core(send1, THIN[1])
    own, near, far, rest, small = input_grad(
        dqk, dv, padded, unit1, rstd1, scaling, (near_cams, far_cams), residual_grad, groups
    )
    near, rest, got, small = after((near, rest, got, small))
    near, rest = swap(near, "view", 1), swap(rest, "view", 1)
    keep, send = split(keep, got)
    got = swap_by_core(send, SCENE[1])
    keep0, got0, keep1, got1, keep = after((keep0, got0, keep1, got1, keep))
    keep0, send0 = split(keep0, got0)
    keep1, send1 = split(keep1, got1)
    got0, got1 = swap_by_core(send0, WIDE[2]), swap_by_core(send1, THIN[2])
    small = jnp.concatenate([small, rows[:6]], 0)
    small = rounded(jnp.concatenate([small[:, : width // 2], small[:, width // 2 :]], 0))
    small = whole_slice(small)
    extra = small.shape[0]
    got, got0, got1, small, near, rest = after((got, got0, got1, small, near, rest))
    joint = jnp.concatenate([whole_slice(keep0 + got0), whole_slice(keep1 + got1)], 0)
    joint = lax.optimization_barrier(joint)
    got0 = swap_by_core(joint, WIDE[3])
    message = jnp.concatenate([whole_slice(keep + got), small], 0)
    message = lax.optimization_barrier(message)
    got = swap_by_core(message, SCENE[2])
    far = swap((far + rest.astype(F32)).astype(BF), "view", 2)

    def grow(message, got):
        small = rounded(message[-extra:].astype(F32) + got[-extra:].astype(F32))
        return jnp.concatenate([message[:-extra], got[:-extra], small], 0)

    joint, got0, message, far = after((joint, got0, message, far))
    cut = keep0.shape[0]
    all0 = joint[:cut] + turned(got0[:cut])
    all1 = joint[cut:] + turned(got0[cut:])
    all0, all1 = lax.optimization_barrier((all0, all1))
    got0, got1 = swap_by_core(all0, WIDE[2]), swap_by_core(all1, THIN[2])
    inputs_grad = (residual_grad + own + near.astype(F32) + far.astype(F32)).astype(BF)
    got, message, all0, all1 = after((got, message, all0, all1))
    got = jnp.concatenate([turned(got[:-extra]), got[-extra:]], 0)
    message = rounded(message.astype(F32) + got.astype(F32))
    got = swap_by_core(message, LATE[0])
    got0, got1, message = after((got0, got1, message))
    all0 = jnp.concatenate([all0, got0], 0)
    all1 = jnp.concatenate([all1, got1], 0)
    got0, got1 = swap_by_core(all0, WIDE[1]), swap_by_core(all1, THIN[1])
    got, all0, all1 = after((got, all0, all1))
    message = grow(message, got)
    got = swap_by_core(message, LATE[1])
    got0, got1, message = after((got0, got1, message))
    all0 = jnp.concatenate([all0, got0], 0)
    all1 = jnp.concatenate([all1, got1], 0)
    got0, got1 = swap_by_core(all0, WIDE[0]), swap_by_core(all1, THIN[0])
    peer0, peer1 = swap(all0, "view", 1), swap(all1, "view", 1)
    got, all0, all1 = after((got, all0, all1))
    message = grow(message, got)
    got = swap_by_core(message, LATE[2])
    near_keep = swap(message[:-extra], "view", 1)
    peer0, peer1 = after((peer0, peer1))
    feed_grads = feed_assemble(codes, 0, [all0, all1, peer0, peer1], hid)
    got0, got1, inputs_grad, *feed_grads = after((got0, got1, inputs_grad, *feed_grads))
    peer0, peer1 = swap(got0, "view", 1), swap(got1, "view", 1)
    outcome = outcome_of(codes, residual, own_wide, wide, squeezer, leveling)
    peer0, peer1, got0, got1, outcome = after((peer0, peer1, got0, got1, outcome))
    grad_squeezer, grad_expander, grad_combiner = feed_assemble(
        codes, 1, [got0, got1, peer0, peer1], hid, feed_grads
    )
    got, near_keep, grad_squeezer = after((got, near_keep, grad_squeezer))
    near_got = swap(got, "view", 1)
    small = rounded(message[-extra:].astype(F32) + got[-extra:].astype(F32))
    other = swap(small, "view", 1)
    grad_projector = assemble(codes, [message, got, near_keep, near_got], width)
    vectors = [width] * 6 + [hid]
    table, *vectors = small_outputs(
        small, other, groups, vectors
    )
    grad_scaling, grad_shifting, grad_leveling, grad_baseline, grad_rescaling, grad_reshifting, grad_priming = vectors

    return (
        outcome.reshape(inputs.shape),
        inputs_grad.reshape(inputs.shape),
        table,
        grad_scaling,
        grad_shifting,
        grad_projector,
        grad_combiner,
        grad_baseline,
        grad_rescaling,
        grad_reshifting,
        grad_expander,
        grad_priming,
        grad_squeezer,
        grad_leveling,
    )


def solution(mesh):
    tokens = P("scene", "view", None, None)
    placed = (tokens, P("scene", "view", None)) + (P(),) * 12 + (tokens,)
    return jax.shard_map(
        on_device,
        mesh=mesh,
        in_specs=placed,
        out_specs=(tokens, tokens) + (P(),) * 12,
        check_vma=False,
    )
```

```python
import functools

import jax
import jax.numpy as jnp
from jax import lax
from jax.experimental import pallas as pl
from jax.experimental.pallas import tpu as pltpu
from jax.sharding import PartitionSpec as P

HEADS = 12
HEAD = 64
BF = jnp.bfloat16
F32 = jnp.float32
BOTH = ("scene", "view")
MINE = HEADS // 4 * HEAD
PAD = 256
MIB = 1 << 20


def swap(value, axis, mask):
    count = lax.axis_size(axis)
    return lax.ppermute(value, axis, [(i, i ^ mask) for i in range(count)])


def swap_by_core(value, masks):
    scenes, views = lax.axis_size("scene"), lax.axis_size("view")
    pairs = []
    for s in range(scenes):
        for v in range(views):
            ds, dv = masks[v % 2]
            pairs.append((s * views + v, (s ^ ds) * views + (v ^ dv)))
    return lax.ppermute(value, BOTH, pairs)


def side_of(masks, core):
    scene, view = lax.axis_index("scene"), lax.axis_index("view")
    bits = [((scene & ds) + (view & dv) > 0).astype(jnp.int32) for ds, dv in masks]
    return jnp.where(core == 0, bits[0], bits[1])


def code_of(stages, core):
    total = 0
    for masks in stages:
        total = 2 * total + side_of(masks, core)
    return total


X, Y, Z1, Z2 = (1, 0), (0, 2), (2, 0), (4, 0)
WIDE = ((X, Z1), (Y, X), (Z1, Y), (Z2, Z2))
THIN = ((Y, Y), (Z1, Z1), (X, X), (Z2, Z2))
SCENE = ((X, Z1), (Z1, X), (Z2, Z2))
LATE = ((Y, X), (Z1, Y), (X, Z1))


def rounded(value):
    return lax.optimization_barrier(lax.reduce_precision(value, 8, 7).astype(BF))


def whole_slice(value):
    bit = 8
    while bit < lax.axis_size("scene"):
        value = rounded(value.astype(F32) + swap(value, "scene", bit).astype(F32))
        bit *= 2
    return value


def by_view(blocks, me):
    a, b, c, d = blocks
    one = (me & 1) == 1
    a, b = jnp.where(one, b, a), jnp.where(one, a, b)
    c, d = jnp.where(one, d, c), jnp.where(one, c, d)
    two = (me & 2) == 2
    a, c = jnp.where(two, c, a), jnp.where(two, a, c)
    b, d = jnp.where(two, d, b), jnp.where(two, b, d)
    return a, b, c, d


def normalise(values):
    centre = values - jnp.mean(values, axis=-1, keepdims=True)
    rstd = lax.rsqrt(jnp.mean(centre * centre, axis=-1, keepdims=True) + 1e-05)
    return centre * rstd, rstd


def norm_back(grad, unit, rstd):
    return (
        grad
        - jnp.mean(grad, axis=-1, keepdims=True)
        - unit * jnp.mean(grad * unit, axis=-1, keepdims=True)
    ) * rstd


def dot(a, b):
    return jnp.dot(a, b, preferred_element_type=F32)


def tdot(a, b):
    return lax.dot_general(a, b, (((0,), (0,)), ((), ())), preferred_element_type=F32)


def dott(a, b):
    return lax.dot_general(a, b, (((1,), (1,)), ((), ())), preferred_element_type=F32)


def split3(values):
    high = values.astype(BF)
    rest = values - high.astype(F32)
    middle = rest.astype(BF)
    return high, middle, (rest - middle.astype(F32)).astype(BF)


def onehot_t(cameras, groups):
    rows = lax.broadcasted_iota(jnp.int32, (groups, cameras.shape[1]), 0)
    return (rows == cameras).astype(F32).astype(BF)


class Incoming:
    def __init__(self, source, buffer, sem, whole=None):
        self.copy, self.there = pltpu.make_async_copy(source, buffer, sem), False
        self.buffer = buffer if whole is None else whole
        self.copy.start()

    def __call__(self):
        if not self.there:
            self.copy.wait()
            self.there = True
        return self.buffer


class Present:
    def __init__(self, ref):
        self.buffer = ref

    def __call__(self):
        return self.buffer


class Outgoing:
    def __init__(self, target, buffer, sems, moves):
        self.target, self.ref, self.sems, self.moves = target, buffer, sems, moves

    def send(self, here=None, there=None):
        source = self.ref if here is None else self.ref.at[here]
        target = self.target if there is None else self.target.at[there]
        move = pltpu.make_async_copy(source, target, self.sems.at[len(self.moves)])
        move.start()
        self.moves.append(move)


class Operand:
    def __init__(self, array, *, home=False, ready=False, cut=None, shape=None):
        self.array, self.ready, self.cut, self.apart = array, ready, cut, False
        if home:
            self.array = pltpu.with_memory_space_constraint(array, pltpu.HBM)
        self.shape = array.shape if shape is None else shape


def apart(array):
    operand = Operand(array, home=True)
    operand.apart = True
    return operand


def home(array, **more):
    return Operand(array, home=True, **more)


def ready(array):
    return Operand(array, ready=True)


def staged(body, args, outs, *, name, mib, us, scratch=(), code=None, held=(), buffers=None, early=None):
    buffers = buffers or {}
    args = [a if isinstance(a, Operand) else home(a) for a in args]
    n_code, n_in, n_held, n_out = int(code is not None), len(args), len(held), len(outs)
    loads = [i for i, a in enumerate(args) if not (a.ready or a.apart)]

    def kernel(*refs):
        code_ref = refs[0] if n_code else None
        refs = refs[n_code:]
        ins, refs = refs[:n_in], refs[n_in + n_held :]
        targets, refs = refs[:n_out], refs[n_out:]
        in_bufs, refs = refs[: len(loads)], refs[len(loads) :]
        out_bufs, refs = refs[:n_out], refs[n_out:]
        in_sems, out_sems, rest = refs[0], refs[1], refs[2:]
        arrivals = [Present(ref) for ref in ins]
        if early is not None:
            early(code_ref, ins, rest)
        for n, i in enumerate(loads):
            source = ins[i] if args[i].cut is None else ins[i].at[args[i].cut]
            arrivals[i] = Incoming(source, in_bufs[n], in_sems.at[n])
        moves = []
        leaving = [Outgoing(t, b, out_sems, moves) for t, b in zip(targets, out_bufs, strict=True)]
        body(code_ref, arrivals, leaving, *rest)
        for arrival in arrivals:
            arrival()
        for move in moves:
            move.wait()

    anywhere, vmem = pl.BlockSpec(memory_space=pl.ANY), pl.BlockSpec(memory_space=pltpu.VMEM)
    specs = [pl.BlockSpec(memory_space=pltpu.SMEM)] * n_code
    specs += [vmem if a.ready else anywhere for a in args] + [anywhere] * n_held
    operands = ([code] if n_code else []) + [a.array for a in args]
    operands += [pltpu.with_memory_space_constraint(a, pltpu.HBM) for a in held]
    bufs = [pltpu.VMEM(args[i].shape, args[i].array.dtype) for i in loads]
    return pl.pallas_call(
        kernel,
        in_specs=specs,
        out_specs=[anywhere] * n_out,
        out_shape=[pltpu.HBM(shape, dtype) for shape, dtype in outs],
        scratch_shapes=bufs
        + [pltpu.VMEM(buffers.get(i, o[0]), o[1]) for i, o in enumerate(outs)]
        + [pltpu.SemaphoreType.DMA((max(len(loads), 1),)), pltpu.SemaphoreType.DMA((48,))]
        + list(scratch),
        input_output_aliases={n_code + n_in + i: i for i in range(n_held)},
        compiler_params=pltpu.CompilerParams(vmem_limit_bytes=mib * MIB),
        cost_estimate=pl.CostEstimate(flops=0, bytes_accessed=0, transcendentals=0),
        name=name,
    )(*operands)


def project_rows(tokens, cams, embedding, gain, shift, weight, outs, there, hold_ref, summed=None):
    normed, unit, rstd, *triple = outs
    rows = tokens[0].buffer.shape[0]
    pair = 2 * rows
    table = jnp.concatenate(split3(embedding()[...]), 0)
    hot = onehot_t(cams()[...], embedding().shape[0])
    hold_ref[...] = tdot(jnp.concatenate([hot] * 3, 0), table)
    for at, x in enumerate(tokens):
        here = slice(at * rows, (at + 1) * rows)
        values = x()[...].astype(F32) + hold_ref[here, :]
        if at == 0 and summed is not None:
            summed.ref[...] = values
            summed.send()
        values, scale = normalise(values)
        hold_ref[here, :] = values
        rstd.ref[here, :] = scale
    values = hold_ref[...]
    low = (values * gain()[...] + shift()[...]).astype(BF)
    normed.ref[...] = low
    lane = lax.broadcasted_iota(jnp.int32, (pair, PAD), 1)
    for i, (ref, first, out) in enumerate(triple):
        block = dot(low, weight()[:, i * PAD : (i + 1) * PAD])
        if i == 0:
            block = block * HEAD**-0.5
        if i == 2:
            block = jnp.where(lane < MINE, block, 1.0)
        ref[first : first + pair, :] = block.astype(BF)
        out.send((pl.ds(first, pair),), there)
    normed.send(None, there)
    unit.ref[...] = values.astype(BF)
    unit.send(None, there)
    rstd.send(None, there)


def project_outs(total, width):
    outs = [((total, width), BF), ((total, width), BF), ((total, 1), F32)]
    return outs + [((total, PAD), BF)] * 3


def project_body(_, ins, outs, hold_ref):
    xa, xb, cams, embedding, gain, shift, weight = ins
    there = (pl.ds(0, hold_ref.shape[0]),)
    triple = [(out.ref, 0, out) for out in outs[3:6]]
    project_rows((xa, xb), cams, embedding, gain, shift, weight, [*outs[:3], *triple], there, hold_ref, outs[6])


def project(xa, xb, cams, embedding, gain, shift, weight):
    rows, width = xa.shape[-2:]
    pair, total = 2 * rows, 4 * rows
    outs = project_outs(total, width)
    return staged(
        project_body,
        [xa, ready(xb), cams, embedding, gain, shift, weight],
        [*outs, ((rows, width), F32)],
        name="project",
        mib=32,
        us=5,
        scratch=[pltpu.VMEM((pair, width), F32)],
        buffers={i: (pair, o[0][1]) for i, o in enumerate(outs)},
    )


def blocks_of(total):
    return [(at, min(256, total - at)) for at in range(0, total, 256)]


TILE = 128


def tile_of(head):
    at = head * HEAD // TILE * TILE
    return slice(at, at + TILE)


def one_head(block, head):
    lane = lax.broadcasted_iota(jnp.int32, block.shape, 1) // HEAD
    return jnp.where(lane == head % (TILE // HEAD), block, jnp.zeros_like(block))


def attend_rows(q_ref, keys, values_of, outs, vt_ref, mt_ref):
    e, first, second, inv = outs
    pair, heads = q_ref.shape[0], e.ref.shape[0]
    work = [(h, at, size) for h in range(heads) for at, size in blocks_of(pair)]

    def scores(h, at, size):
        return dott(keys()[:, tile_of(h)], one_head(q_ref[at : at + size, tile_of(h)], h))

    keys(), values_of()
    ahead = scores(*work[0])
    vt_ref[...] = values_of()[...].astype(F32).T.astype(BF)
    mt_ref[...] = jnp.zeros_like(mt_ref)
    inv.ref[...] = jnp.zeros_like(inv.ref)
    for i, (h, at, size) in enumerate(work):
        here = ahead
        if i + 1 < len(work):
            ahead = scores(*work[i + 1])
        mine = slice(h * HEAD, (h + 1) * HEAD)
        expo = jnp.exp(here - jnp.max(here, 0, keepdims=True)).astype(BF)
        cut = (h, slice(None), slice(at, at + size))
        e.ref[cut] = expo
        if at + size == pair:
            e.send((h,), (h,))
        values = jnp.concatenate([vt_ref[mine, :], vt_ref[MINE : MINE + 16, :]], 0)
        out = dot(values, expo)
        inverse = 1.0 / out[HEAD : HEAD + 1, :]
        mt_ref[mine, at : at + size] = out[:HEAD, :] * inverse
        inv.ref[h : h + 1, at : at + size] = inverse
    mixed = mt_ref[...].T[:pair]
    first.ref[...] = mixed[: pair // 2, :MINE].astype(BF)
    first.send()
    second.ref[...] = mixed[pair // 2 :, :MINE].astype(BF)
    second.send()
    inv.send()


def attend_outs(total):
    pair, heads = total // 2, MINE // HEAD
    wide = -(-pair // 128) * 128
    part = ((pair // 2, MINE), BF)
    return [((heads, total, pair), BF), part, part, ((8, wide), F32)]


def attend_scratch(total):
    wide = -(-(total // 2) // 128) * 128
    return [pltpu.VMEM((PAD, total), BF), pltpu.VMEM((PAD, wide), F32)]


def attend_body(_, ins, outs, *scratch):
    q, k, v = ins
    attend_rows(q(), k, v, outs, *scratch)


def attend(q, k, v):
    total = k.shape[0]
    pair = total // 2
    return staged(
        attend_body,
        [home(q, cut=(pl.ds(0, pair),), shape=(pair, PAD)), home(k), home(v)],
        attend_outs(total),
        name="attend",
        mib=32,
        us=8,
        scratch=attend_scratch(total),
    )


def second_body(_, ins, outs, hold_ref, *scratch):
    xa, xb, cams, embedding, gain, shift, weight = ins
    pair = hold_ref.shape[0]
    keys_ref, values_ref, sems, *scratch = scratch
    first = pl.ds(0, pair)
    k, v = (
        Incoming(out.target.at[first], ref.at[first], sems.at[i], ref)
        for i, (out, ref) in enumerate(((outs[4], keys_ref), (outs[5], values_ref)))
    )
    there = (pl.ds(pair, pair),)
    triple = [(outs[3].ref, 0, outs[3]), (k.buffer, pair, outs[4]), (v.buffer, pair, outs[5])]
    outs[4].ref, outs[5].ref = k.buffer, v.buffer
    project_rows((xa, xb), cams, embedding, gain, shift, weight, [*outs[:3], *triple], there, hold_ref)
    attend_rows(outs[3].ref, k, v, outs[6:], *scratch)
    k()
    v()


def second_half(xa, xb, cams, embedding, gain, shift, weight, held):
    rows, width = xa.shape[-2:]
    pair, total = 2 * rows, 4 * rows
    outs = project_outs(total, width)
    buffers = {i: (pair, o[0][1]) for i, o in enumerate(outs)}
    buffers[4] = buffers[5] = (16, PAD)
    return staged(
        second_body,
        [xa, ready(xb), ready(cams), embedding, gain, shift, weight],
        [*outs, *attend_outs(total)],
        name="second_half",
        mib=44,
        us=10,
        scratch=[
            pltpu.VMEM((pair, width), F32),
            pltpu.VMEM((total, PAD), BF),
            pltpu.VMEM((total, PAD), BF),
            pltpu.SemaphoreType.DMA((2,)),
            *attend_scratch(total),
        ],
        held=held,
        buffers=buffers,
    )


def back_heads(heads, q_ref, v_ref, g_ref, kt_ref, delta_of, expos, dq_ref, dk_ref, dv_ref):
    pair = q_ref.shape[0] // 2
    work = [(h, i, at, size) for h in heads for i in range(2) for at, size in blocks_of(pair)]
    dq_ref[...] = jnp.zeros_like(dq_ref)

    def cut(ref, h, i, at, size):
        return one_head(ref[i * pair + at : i * pair + at + size, :], h)

    ahead_grad = cut(g_ref, *work[0])
    ahead = dott(v_ref[...], ahead_grad)
    for n, (h, i, at, size) in enumerate(work):
        if i == at == 0:
            expos[2 * heads.index(h)]()
            expos[2 * heads.index(h) + 1]()
        grad, prob_grad = ahead_grad, ahead
        if n + 1 < len(work):
            ahead_grad = cut(g_ref, *work[n + 1])
            ahead = dott(v_ref[...], ahead_grad)
        expo = expos[2 * heads.index(h) + i]()[:, at : at + size]
        score_grad = (expo.astype(F32) * (prob_grad - delta_of(h, i, at, size))).astype(BF)
        value_part = dot(expo, grad)
        key_part = dot(score_grad, cut(q_ref, h, i, at, size))
        if n:
            value_part += dv_ref[...]
            key_part += dk_ref[...]
        dv_ref[...] = value_part
        dk_ref[...] = key_part
        mine = slice(h * HEAD % TILE, h * HEAD % TILE + HEAD)
        dq_ref[i, mine, at : at + size] = dot(kt_ref[mine, :], score_grad)


def back_first_body(code, ins, outs, g_ref, kt_ref, dq_ref, dk_ref, dv_ref, hold_ref):
    q, k, v, *ins = ins
    grads, invs, mixes, expos = ins[:4], ins[4:6], ins[6:10], ins[10:]
    dq, dk, dv, g_rest, delta = outs
    total = q.buffer.shape[0]
    pair, rows = total // 2, grads[0].buffer.shape[0]
    for arrival in (q, k, v, *grads, *invs, *mixes, *expos[:2]):
        arrival()
    hold_ref[...] = jnp.zeros_like(hold_ref)
    for i, grad in enumerate(grads):
        hold_ref[i * rows : (i + 1) * rows, :MINE] = grad()[...].astype(F32)
    lane = lax.broadcasted_iota(jnp.int32, (8, PAD), 1) // HEAD
    pick = (lane == lax.broadcasted_iota(jnp.int32, (8, PAD), 0)).astype(F32).astype(BF)
    for i in range(2):
        here = slice(i * pair, (i + 1) * pair)
        inverse = invs[i]()[...].T[:pair, :]
        lane = lax.broadcasted_iota(jnp.int32, (pair, PAD), 1) // HEAD
        scale = jnp.zeros((pair, PAD), F32)
        for h in range(MINE // HEAD):
            scale = jnp.where(lane == h, inverse[:, h : h + 1], scale)
        scaled = (hold_ref[here, :] * scale).astype(BF)
        g_ref[here, :] = scaled[:, :TILE]
        g_rest.ref[here, :] = scaled[:, TILE:]
        for j in range(2):
            rows_here = slice(i * pair + j * rows, i * pair + (j + 1) * rows)
            hold_ref[rows_here, :MINE] = mixes[2 * i + j]()[...].astype(F32)
        prod = scaled.astype(F32) * hold_ref[here, :]
        high = prod.astype(BF)
        low = (prod - high.astype(F32)).astype(BF)
        delta.ref[8 * i : 8 * i + 8, :pair] = dott(pick, high) + dott(pick, low)
        delta.ref[8 * i : 8 * i + 8, pair:] = jnp.zeros((8, delta.ref.shape[1] - pair), F32)
    g_rest.send()
    delta.send()
    kt_ref[...] = k()[...].astype(F32).T.astype(BF)

    def delta_of(h, i, at, size):
        return delta.ref[8 * i + h : 8 * i + h + 1, at : at + size]

    back_heads((0, 1), q(), v(), g_ref, kt_ref, delta_of, expos, dq_ref, dk_ref, dv_ref)
    for i in range(2):
        dq.ref[i * pair : (i + 1) * pair, :] = (dq_ref[i].T[:pair] * HEAD**-0.5).astype(BF)
    dq.send()
    dk.ref[...] = dk_ref[...].astype(BF)
    dk.send()
    dv.ref[...] = dv_ref[...].astype(BF)
    dv.send()


def back_last_body(code, ins, outs, kt_ref, dq_ref, dk_ref, dv_ref, piece_ref):
    q, k, v, g, delta, *expos = ins[:7]
    dq0, dk0, dv0, normed = ins[7:]
    dqk, dv, keep, send = outs
    pair = q.buffer.shape[0] // 2
    for arrival in (q, k, v, g, delta, *expos):
        arrival()
    kt_ref[...] = k()[...].astype(F32).T.astype(BF)

    def delta_of(h, i, at, size):
        return delta()[8 * i + h : 8 * i + h + 1, at : at + size]

    back_heads((2,), q(), v(), g(), kt_ref, delta_of, expos, dq_ref, dk_ref, dv_ref)
    rest = MINE - TILE
    dqk.ref[:, :TILE] = dq0()[...]
    for i in range(2):
        dq = (dq_ref[i].T[:pair] * HEAD**-0.5).astype(BF)
        dqk.ref[i * pair : (i + 1) * pair, TILE:MINE] = dq[:, :rest]
    dqk.ref[:, MINE : MINE + TILE] = dk0()[...]
    dqk.ref[:, MINE + TILE :] = dk_ref[:, :rest].astype(BF)
    dv.ref[:, :TILE] = dv0()[...]
    dv.ref[:, TILE:] = dv_ref[:, :rest].astype(BF)
    weight_grad(code, normed, dqk.ref, dv.ref, keep, send, piece_ref)
    dqk.send()
    dv.send()


PIECES = 8


def weight_grad(code, normed, dqk_ref, dv_ref, keep, send, hold_ref):
    width = normed().shape[1]
    rows = width // PIECES
    piece = rows + rows // 2
    mine = code[0]
    qk = tdot(normed()[...], dqk_ref[...]).astype(BF)
    v = tdot(normed()[...], dv_ref[...]).astype(BF)
    for p in range(PIECES):
        at = pl.multiple_of((p ^ mine) * piece, 16)
        hold_ref[pl.ds(at, rows), :] = qk[p * rows : (p + 1) * rows]
        at = pl.multiple_of((p ^ mine) * piece + rows, 16)
        top = v[p * rows : p * rows + rows // 2]
        low = v[p * rows + rows // 2 : (p + 1) * rows]
        hold_ref[pl.ds(at, rows // 2), :] = jnp.concatenate([top, low], 1)
    half = PIECES * piece // 2
    send.ref[...] = hold_ref[half:, :]
    send.send()
    keep.ref[...] = hold_ref[:half, :]
    keep.send()


def back_scratch(total):
    wide = -(-(total // 2) // 128) * 128
    return [
        pltpu.VMEM((TILE, total), BF),
        pltpu.VMEM((2, TILE, wide), F32),
        pltpu.VMEM((total, TILE), F32),
        pltpu.VMEM((total, TILE), F32),
    ]


def tile_cut(array, tile):
    return home(array, cut=(slice(None), pl.ds(tile * TILE, TILE)), shape=(array.shape[0], TILE))


def back_first(q, k, v, e0, e1, grads, mixes, inv0, inv1):
    total = k.shape[0]
    pair = total // 2
    wide = -(-pair // 128) * 128
    args = [tile_cut(a, 0) for a in (q, k, v)] + [grads[0], *map(ready, grads[1:]), inv0, inv1, *mixes]
    args += [home(e, cut=(h,), shape=(total, pair)) for h in range(2) for e in (e0, e1)]
    return staged(
        back_first_body,
        args,
        [((total, TILE), BF)] * 4 + [((16, wide), F32)],
        name="back_first",
        mib=40,
        us=12,
        scratch=[pltpu.VMEM((total, TILE), BF), *back_scratch(total), pltpu.VMEM((total, PAD), F32)],
    )


def back_last(codes, q, k, v, e0, e1, first, normed):
    total, width = k.shape[0], normed.shape[1]
    pair = total // 2
    dq, dk, dv, g, delta = first
    piece = width // PIECES * 3 // 2
    half = ((PIECES * piece // 2, 2 * MINE), BF)
    args = [tile_cut(a, 1) for a in (q, k, v)] + [g, delta]
    args += [home(e, cut=(2,), shape=(total, pair)) for e in (e0, e1)]
    return staged(
        back_last_body,
        [*args, dq, dk, dv, normed],
        [((total, 2 * MINE), BF), ((total, MINE), BF), half, half],
        name="back_last",
        mib=40,
        us=10,
        scratch=[*back_scratch(total), pltpu.VMEM((PIECES * piece, 2 * MINE), BF)],
        code=codes,
    )


STEP = 512


def feed_forward_body(code, ins, outs):
    summed, own, near, far, rest, combiner, baseline, gain, shift, expander, priming, squeezer, tangent = ins
    residual, own_wide, wide, own_slim, slim = outs
    me = code[2]
    first = code[3] == 0
    total = summed()[...] + baseline()[...]
    for r, block in ((2, far), (3, rest), (0, own), (1, near)):
        at = pl.multiple_of((me ^ r) * MINE, 16)
        total += dot(block()[...], combiner()[pl.ds(at, MINE), :])
    residual.ref[...] = total
    residual.send()
    unit, _ = normalise(total)
    low = (unit * gain()[...] + shift()[...]).astype(BF)
    own_slim.ref[...] = jnp.where(first, tangent()[...], low)
    own_slim.send()
    slim.ref[...] = jnp.where(first, low, tangent()[...])
    slim.send()
    for at in range(0, expander().shape[1], STEP):
        cut = slice(at, at + STEP)
        hidden = dot(low, expander()[:, cut]) + priming()[cut]
        back = dott(tangent()[...], squeezer()[cut, :])
        phi = 0.5 * (1.0 + lax.erf(hidden * (2.0**-0.5)))
        density = jnp.exp(-0.5 * hidden * hidden) * 0.3989422804014327
        active = (hidden * phi).astype(BF)
        grad = (back * (phi + hidden * density)).astype(BF)
        own_wide.ref[:, cut] = jnp.where(first, active, grad)
        wide.ref[:, cut] = jnp.where(first, grad, active)
        part = (slice(None), pl.ds(at, STEP))
        own_wide.send(part, part)
        wide.send(part, part)


def feed_forward(codes, summed, own, near, far, rest, combiner, baseline, gain, shift, expander, priming, squeezer, tangent):
    rows, width = summed.shape
    hid = expander.shape[1]
    weights = [combiner, baseline, gain, shift, expander, priming, squeezer, tangent]
    return staged(
        feed_forward_body,
        [home(summed), own, ready(near), ready(far), ready(rest), *weights],
        [((rows, width), F32), ((rows, hid), BF), ((rows, hid), BF), ((rows, width), BF), ((rows, width), BF)],
        name="feed_forward",
        mib=24,
        us=6,
        code=codes,
    )


def feed_back_body(code, ins, outs, grad_ref, sem):
    expander, residual, gain, tangent, combiner, own_wide, wide = ins
    residual_grad, low, *grads, rows = outs
    me = code[2]
    pltpu.make_async_copy(wide(), grad_ref, sem.at[0]).wait()
    second_grad = dott(grad_ref[...], expander()[...])
    unit, rstd = normalise(residual()[...])
    slope = tangent()[...].astype(F32)
    total = slope + norm_back(second_grad * gain()[...], unit, rstd)
    low.ref[...] = total.astype(BF)
    low.send()
    for r in (2, 3, 1, 0):
        at = pl.multiple_of((me ^ r) * MINE, 16)
        grads[r].ref[...] = dott(low.ref[...], combiner()[pl.ds(at, MINE), :]).astype(BF)
        grads[r].send()
    residual_grad.ref[...] = total
    residual_grad.send()
    width = total.shape[1]
    rows.ref[0:1, :] = jnp.sum(slope, 0, keepdims=True)
    rows.ref[1:2, :] = jnp.sum(low.ref[...].astype(F32), 0, keepdims=True)
    rows.ref[2:3, :] = jnp.sum(second_grad * unit, 0, keepdims=True)
    rows.ref[3:4, :] = jnp.sum(second_grad, 0, keepdims=True)
    for j in range(grad_ref.shape[1] // width):
        block = grad_ref[:, j * width : (j + 1) * width].astype(F32)
        rows.ref[4 + j : 5 + j, :] = jnp.sum(block, 0, keepdims=True)
    rows.ref[6:8, :] = jnp.zeros((2, width), F32)
    rows.send()


def pick_wide(on_zero, on_one):
    def early(code, operands, scratch):
        for core, place in enumerate((on_zero, on_one)):

            @pl.when(code[3] == core)
            def _():
                pltpu.make_async_copy(operands[place], scratch[0], scratch[1].at[0]).start()

    return early


def feed_back(codes, residual, own_wide, wide, tangent, expander, gain, combiner):
    rows, width = residual.shape
    return staged(
        feed_back_body,
        [expander, home(residual), gain, tangent, combiner, apart(own_wide), apart(wide)],
        [((rows, width), F32), ((rows, width), BF)] + [((rows, MINE), BF)] * 4 + [((8, width), F32)],
        early=pick_wide(6, 5),
        name="feed_back",
        mib=24,
        us=6,
        scratch=[pltpu.VMEM(wide.shape, BF), pltpu.SemaphoreType.DMA((1,))],
        code=codes,
    )


def outcome_body(code, ins, outs, active_ref, sem):
    squeezer, residual, leveling, own_wide, wide = ins
    pltpu.make_async_copy(wide(), active_ref, sem.at[0]).wait()
    outs[0].ref[...] = (residual()[...] + dot(active_ref[...], squeezer()[...]) + leveling()[...]).astype(BF)
    outs[0].send()


def outcome_of(codes, residual, own_wide, wide, squeezer, leveling):
    rows, width = residual.shape
    return staged(
        outcome_body,
        [squeezer, home(residual), leveling, apart(own_wide), apart(wide)],
        [((rows, width), BF)],
        early=pick_wide(3, 4),
        name="outcome",
        mib=16,
        us=4,
        scratch=[pltpu.VMEM(wide.shape, BF), pltpu.SemaphoreType.DMA((1,))],
        code=codes,
    )[0]


PARTS = 16


def place(code, piece, size):
    return pl.multiple_of((piece ^ code) * size, 8)


def segments(first, rows, low, size):
    out, at = [], first
    while at < first + rows:
        piece, offset = divmod(at - low, size)
        count = min(size - offset, first + rows - at)
        out.append((piece, offset, at - first, count))
        at += count
    return out


def spread(hold_ref, block, first, low, size, code):
    for piece, offset, start, count in segments(first, block.shape[0], low, size):
        at = pl.multiple_of(place(code, piece, size) + offset, 8)
        hold_ref[pl.ds(at, count), :] = block[start : start + count]


def feed_grad_body(sizes, code, ins, outs, tokens_ref, sems, *holds):
    own_wide, own_slim, wide, slim, own, far, near, rest, resid, other = ins
    hid, width = own_wide().shape[1], own_slim().shape[1]
    assert hid == 2 * width
    bulk = PARTS * sizes[0]
    rows = own_slim().shape[0]
    room = tokens_ref.shape[1] // 2
    gap = rows // 16 * 16
    loads = []
    for n, (big, small) in enumerate(((own_wide, own_slim), (wide, slim))):
        first = n * room
        for j in range(3):
            tokens_ref[j, first + gap : first + room, :] = jnp.zeros((room - gap, width), BF)
    for n, (big, small) in enumerate(((own_wide, own_slim), (wide, slim))):
        there = pl.ds(n * room, rows)
        for j in range(hid // width):
            source = big().at[:, pl.ds(j * width, width)]
            loads.append(pltpu.make_async_copy(source, tokens_ref.at[j, there], sems.at[3 * n + j]))
        loads.append(pltpu.make_async_copy(small(), tokens_ref.at[2, there], sems.at[3 * n + 2]))
    for load in loads:
        load.start()
    for load in loads:
        load.wait()

    def put(block, row):
        for part, low, high in ((0, 0, bulk), (1, bulk, bulk + PARTS * sizes[1])):
            first, last = max(row, low), min(row + block.shape[0], high)
            if first < last:
                spread(holds[part], block[first - row : last - row], first, low, sizes[part], code[4 + 2 * part])

    for j in range(hid // width):
        left = jnp.where(code[3] == 0, j, 2)
        right = jnp.where(code[3] == 0, 2, j)
        block = tdot(tokens_ref[left], tokens_ref[right])
        put(block, j * width)

    upper = code[2] < 2
    for i in range(2):
        here = jnp.where(upper, (own, far)[i]()[...], (far, own)[i]()[...])
        peer = jnp.where(upper, (near, rest)[i]()[...], (rest, near)[i]()[...])
        put(tdot(here, resid()[...]) + tdot(peer, other()[...]), hid + i * MINE)
    for part, hold_ref in enumerate(holds):
        keep, send = outs[2 * part : 2 * part + 2]
        half = hold_ref.shape[0] // 2
        send.ref[...] = hold_ref[half:, :].astype(BF)
        send.send()
        keep.ref[...] = hold_ref[:half, :].astype(BF)
        keep.send()


def feed_grad(codes, sizes, feed, mixed):
    rows, width = feed[1].shape
    halves = [((PARTS * size // 2, width), BF) for size in sizes]
    return staged(
        functools.partial(feed_grad_body, sizes),
        [apart(feed[0]), apart(feed[1]), *map(ready, feed[2:]), mixed[0], *map(ready, mixed[1:4]), mixed[4], ready(mixed[5])],
        [halves[0], halves[0], halves[1], halves[1]],
        name="feed_grad",
        mib=40,
        us=7,
        scratch=[
            pltpu.VMEM((3, 2 * (-(-rows // 16) * 16), width), BF),
            pltpu.SemaphoreType.DMA((6,)),
            *[pltpu.VMEM((PARTS * size, width), F32) for size in sizes],
        ],
        code=codes,
    )


def feed_assemble_body(half, sizes, code, ins, outs, sems, *holds):
    squeezer, expander, combiner = (out.target for out in outs)
    hid, width = squeezer.shape

    def targets(core, row, count):
        out = []
        while count:
            if row < hid and core == 0:
                take = min(count, hid - row)
                out.append((squeezer.at[pl.ds(row, take), :], take))
            elif row < hid:
                j = row // width
                take = min(count, (j + 1) * width - row)
                cut = pl.ds(row - j * width, take), pl.ds(j * width, width)
                out.append((expander.at[cut], take))
            else:
                view, at = divmod(row - hid, MINE)
                take = min(count, MINE - at)
                out.append((combiner.at[pl.ds((core + 2 * view) * MINE + at, take), :], take))
            row, count = row + take, count - take
        return out

    for hold_ref, block in zip(holds, ins, strict=True):
        hold_ref[...] = block()[...].astype(F32)
    for action in ("start", "wait"):
        for me in range(2):
            number = 0
            for side in range(2):
                core = me if side == 0 else 1 - me
                low = 0
                for part, size in enumerate(sizes):
                    for piece in range(PARTS):
                        there = piece ^ code[4 + 2 * part + side]
                        moves, at = [], 0
                        for target, count in targets(core, low + piece * size, size):
                            moves.append((at, count, target, number))
                            at, number = at + count, number + 1

                        @pl.when((code[3] == me) & (there // 8 == half))
                        def _():
                            for at, count, target, n in moves:
                                start = pl.multiple_of(there % 8 * size + at, 8)
                                source = holds[2 * side + part].at[pl.ds(start, count), :]
                                getattr(pltpu.make_async_copy(source, target, sems.at[n]), action)()

                    low += PARTS * size


def feed_assemble(codes, half, blocks, hid, held=()):
    width = blocks[0].shape[1]
    sizes = [blocks[0].shape[0] // 8, blocks[1].shape[0] // 8]
    return staged(
        functools.partial(feed_assemble_body, half, sizes),
        [Operand(b) for b in blocks],
        [((hid, width), F32), ((width, hid), F32), ((width, width), F32)],
        name="feed_assemble",
        mib=24,
        us=6,
        scratch=[pltpu.SemaphoreType.DMA((96,))] + [pltpu.VMEM(b.shape, F32) for b in blocks],
        code=codes,
        held=held,
        buffers={0: (8, 128), 1: (8, 128), 2: (8, 128)},
    )


def input_grad_body(_, ins, outs, hold_ref):
    dqk, dv, weight, unit, rstd, gain, *rest = ins
    near_cams, far_cams, resid = rest
    small = outs[4]
    patches = resid.buffer.shape[0]
    groups = small.ref.shape[0] - 2
    slope = dott(dqk()[:, :MINE], weight()[:, :MINE]) + dott(dqk()[:, MINE:], weight()[:, PAD : PAD + MINE])
    slope += dott(dv()[...], weight()[:, 2 * PAD : 2 * PAD + MINE])
    values = unit()[...].astype(F32)
    small.ref[groups : groups + 1, :] = jnp.sum(slope * values, 0, keepdims=True)
    small.ref[groups + 1 : groups + 2, :] = jnp.sum(slope, 0, keepdims=True)
    hold_ref[...] = norm_back(slope * gain()[...], values, rstd()[...])
    for r in (1, 3, 0, 2):
        part = hold_ref[r * patches : (r + 1) * patches, :]
        outs[r].ref[...] = part.astype(outs[r].ref.dtype)
        outs[r].send()
    hold_ref[:patches, :] = hold_ref[:patches, :] + resid()[...]
    table = jnp.zeros((groups, slope.shape[1]), F32)
    for i, cams in enumerate((near_cams, far_cams)):
        part = hold_ref[2 * i * patches : 2 * (i + 1) * patches, :]
        hot = onehot_t(cams()[...], groups)
        for piece in split3(part)[:2]:
            table += dot(hot, piece)
    small.ref[:groups, :] = table
    small.send()


def input_grad(dqk, dv, weight, unit, rstd, gain, cams, resid, groups):
    total, width = unit.shape
    patches = resid.shape[0]
    low, full = ((patches, width), BF), ((patches, width), F32)
    return staged(
        input_grad_body,
        [home(dqk), home(dv), home(weight), home(unit), home(rstd), gain, *cams, home(resid)],
        [full, low, full, low, ((groups + 2, width), F32)],
        name="input_grad",
        mib=48,
        us=9,
        scratch=[pltpu.VMEM((total, width), F32)],
    )


def assemble_body(code, ins, outs):
    out, table, *vectors = outs
    rows, width = out.ref.shape[0] // PIECES, out.ref.shape[1] // 3
    piece = rows * 3 // 2
    blocks = [arrival() for arrival in ins[:4]]
    for p in range(PIECES):
        cut = []
        for i, which in enumerate((0, 1, 0, 1)):
            r = (p ^ code[which]) % 4
            core = code[3] if which == 0 else 1 - code[3]
            far = i // 2
            middle = jnp.where(core == 0, r // 2 * 2 + far, far * 2 + r // 2)
            at = pl.multiple_of((middle * 2 + r % 2) * piece, 16)
            upper = (p ^ code[which]) >= PIECES // 2
            lower_block = blocks[2 * which][pl.ds(at, piece), :]
            upper_block = blocks[2 * which + 1][pl.ds(at, piece), :]
            cut.append(jnp.where(upper, upper_block, lower_block).astype(F32))
        low = p * rows
        for v, block in enumerate(by_view(cut, code[2])):
            at = v * MINE
            out.ref[low : low + rows, at : at + MINE] = block[:rows, :MINE]
            out.ref[low : low + rows, width + at : width + at + MINE] = block[:rows, MINE:]
            at += 2 * width
            out.ref[low : low + rows // 2, at : at + MINE] = block[rows:, :MINE]
            out.ref[low + rows // 2 : low + rows, at : at + MINE] = block[rows:, MINE:]
        out.send((pl.ds(low, rows),), (pl.ds(low, rows),))
    total = ins[4]()[...].astype(F32) + ins[5]()[...].astype(F32)
    count, half, groups = total.shape[0] // 2, width // 2, table.ref.shape[0]
    table.ref[:, :half] = total[:groups, :]
    table.ref[:, half:] = total[count : count + groups, :]
    table.send()
    row = groups
    for vector in vectors:
        for at in range(0, vector.ref.shape[0], width):
            vector.ref[at : at + half] = total[row, :]
            vector.ref[at + half : at + width] = total[count + row, :]
            row += 1
        vector.send()


def assemble(codes, blocks, smalls, groups, sizes, width):
    return staged(
        assemble_body,
        [Operand(b) for b in (*blocks, *smalls)],
        [((width, 3 * width), F32), ((groups, width), F32)] + [((size,), F32) for size in sizes],
        name="assemble",
        mib=24,
        us=5,
        code=codes,
    )


def turned(block):
    half = block.shape[0] // 2
    return jnp.concatenate([block[half:], block[:half]], 0)


def after(values, *others):
    out = lax.optimization_barrier((*values, *others))
    return out[: len(values)]


def halve(keep, got):
    cut = keep.shape[0] // 2
    return keep[:cut] + got[:cut], keep[cut:] + got[cut:]


class Part:
    def __init__(self, keep, got, stages):
        self.value, self.got, self.stages, self.step, self.lower = keep, got, stages, 0, None

    def begin(self):
        self.value, send = halve(self.value, self.got)
        self.got = swap_by_core(send, self.stages[2])

    def advance(self, got):
        self.step += 1
        if self.step == 1:
            self.value = lax.optimization_barrier(whole_slice(self.value + got))
            self.got = swap_by_core(self.value, self.stages[3])
        elif self.step == 2:
            self.value = lax.optimization_barrier(self.value + turned(got))
            self.got = swap_by_core(self.value, self.stages[2])
        elif self.step == 3:
            self.value = jnp.concatenate([self.value, got], 0)
            self.got = swap_by_core(self.value, self.stages[1])
        elif self.step == 4:
            self.value = jnp.concatenate([self.value, got], 0)
            self.got, peer = swap_by_core(self.value, self.stages[0]), swap(self.value, "view", 1)
            self.lower = (self.value, peer)
        else:
            self.got = got
            return []
        return [self.value]


PLAN = ("LAB", "LAG", "BI", "AO", "B", "L", "AI", "L", "B", "Lp", "PAB", "Lkq")


def on_device(
    inputs,
    cameras,
    embedding,
    scaling,
    shifting,
    projector,
    combiner,
    baseline,
    rescaling,
    reshifting,
    expander,
    priming,
    squeezer,
    leveling,
    cotangent,
):
    me = lax.axis_index("view")
    core = me % 2
    patches, width = inputs.shape[2], inputs.shape[3]
    groups, hid = embedding.shape[0], expander.shape[1]
    codes = [code_of(SCENE, core), code_of(SCENE, 1 - core), me, core]
    codes += [code_of(WIDE, core), code_of(WIDE, 1 - core), code_of(THIN, core), code_of(THIN, core)]
    codes = jnp.stack(codes).astype(jnp.int32)
    tangent = cotangent.reshape(patches, width)
    x0 = inputs.reshape(patches, width)
    c0 = cameras.reshape(1, patches)
    x2 = swap(x0, "view", 2)
    x1, c1 = swap(x0, "view", 1), swap(c0, "view", 1)
    near_cams = jnp.concatenate([c0, c1], 1)
    far_cams = swap(near_cams, "view", 2)
    hole = jnp.zeros((width, PAD - MINE), BF)
    padded = []
    for part in range(3):
        padded += [lax.dynamic_slice_in_dim(projector, part * width + me * MINE, MINE, 1), hole]
    padded = jnp.concatenate(padded, 1)
    *held, summed = project(x0, x1, near_cams, embedding, scaling, shifting, padded)
    x2, far_cams = after((x2, far_cams), *held)
    x3 = swap(x2, "view", 1)
    normed, unit1, rstd1, q, k, v, e1, far, rest, inv1 = second_half(
        x2, x3, far_cams, embedding, scaling, shifting, padded, held
    )
    mine_far, mine_rest = far, rest
    far, rest = swap(far, "view", 2), swap(rest, "view", 3)
    e0, own, near, inv0 = attend(q, k, v)
    mixes = [own, near, mine_far, mine_rest]
    near, own, far, rest = after((near, own, far, rest))
    near, peer_rest = swap(near, "view", 1), swap(rest, "view", 1)

    residual, own_wide, wide, own_slim, slim = feed_forward(
        codes, summed, own, near, far, rest, combiner, baseline, rescaling, reshifting, expander, priming,
        squeezer, tangent,
    )
    peer_near = swap(near, "view", 1)
    peer_wide, peer_slim = swap(wide, "view", 1), swap(slim, "view", 1)
    residual_grad, resid_low, *grads, rows = feed_back(
        codes, residual, own_wide, wide, tangent, expander, rescaling, combiner
    )
    grads = [grads[0]] + [swap(grads[r], "view", r) for r in (1, 2, 3)]
    other = swap(resid_low, "view", 1)
    sizes = [(hid + width // 2) // 24, (hid + width // 2) // 48]
    keep0, send0, keep1, send1 = feed_grad(
        codes, sizes, [own_wide, own_slim, peer_wide, peer_slim],
        [own, far, peer_near, peer_rest, resid_low, other],
    )
    *grads, keep0, send0, keep1, send1 = after((*grads, keep0, send0, keep1, send1))
    got0, got1 = swap_by_core(send0, WIDE[0]), swap_by_core(send1, THIN[0])
    first = back_first(q, k, v, e0, e1, grads, mixes, inv0, inv1)
    got0, got1, *first = after((got0, got1, *first))
    keep0, send0 = halve(keep0, got0)
    keep1, send1 = halve(keep1, got1)
    got0, got1 = swap_by_core(send0, WIDE[1]), swap_by_core(send1, THIN[1])
    dqk, dv, keep, send = back_last(codes, q, k, v, e0, e1, first, normed)
    got0, got1, dqk, dv, keep, send = after((got0, got1, dqk, dv, keep, send))
    wide_part = Part(keep0, got0, WIDE)
    thin_part = Part(keep1, got1, THIN)
    got_l = swap_by_core(send, SCENE[0])
    wide_part.begin()
    thin_part.begin()
    parts = dict(A=wide_part, B=thin_part)
    l_step, i_step = 0, 0
    message = near_keep = near_got = other = small = peers = None
    outcome = inputs_grad = feed_grads = None
    last = []
    gate = [codes, dqk]
    extra = 0

    def grow(message, got):
        small = rounded(message[-extra:].astype(F32) + got[-extra:].astype(F32))
        return jnp.concatenate([message[:-extra], got[:-extra], small], 0)

    for group in PLAN:
        tied = []
        if "O" in group:
            outcome = outcome_of(gate[0], residual, own_wide, wide, squeezer, leveling)
            tied.append(outcome)
        if "G" in group:
            own, near, far, rest, small = input_grad(
                gate.pop(), dv, padded, unit1, rstd1, scaling, (near_cams, far_cams), residual_grad, groups
            )
            tied += [near, rest, small]
        if "P" in group:
            (all0, peer0), (all1, peer1) = (parts[n].lower for n in "AB")
            feed_grads = feed_assemble(gate[0], 0, [all0, all1, peer0, peer1], hid)
            tied += feed_grads
        waits = []
        for name in group:
            if name in "AB":
                waits.append(parts[name].got)
            elif name == "L":
                waits.append(got_l)
            elif name == "I":
                waits += [near, rest] if i_step == 0 else [far]
            elif name == "p":
                waits += [parts["A"].lower[1], parts["B"].lower[1]]
            elif name == "k":
                waits.append(near_keep)
            elif name == "q":
                waits += peers
        bundle = list(after((*waits, *tied, *last, *gate)))
        new_waits, rest_of = bundle[: len(waits)], bundle[len(waits) :]
        new_tied, gate = rest_of[: len(tied)], rest_of[len(rest_of) - len(gate) :]
        if "O" in group:
            outcome = new_tied.pop(0)
        if "G" in group:
            near, rest, small = new_tied[:3]
            new_tied = new_tied[3:]
        if "P" in group:
            feed_grads = new_tied
        last = []
        for name in group:
            if name in "AB":
                last += parts[name].advance(new_waits.pop(0))
            elif name == "p":
                for n in "AB":
                    parts[n].lower = (parts[n].lower[0], new_waits.pop(0))
            elif name == "k":
                near_keep = new_waits.pop(0)
            elif name == "q":
                peers = [new_waits.pop(0), new_waits.pop(0)]
            elif name == "I":
                if i_step == 0:
                    near, rest = new_waits.pop(0), new_waits.pop(0)
                    far = lax.optimization_barrier((far + rest.astype(F32)).astype(BF))
                    last.append(far)
                    far = swap(far, "view", 2)
                else:
                    far = new_waits.pop(0)
                    inputs_grad = (residual_grad + own + near.astype(F32) + far.astype(F32)).astype(BF)
                    last.append(inputs_grad)
                i_step += 1
            elif name == "L":
                got = new_waits.pop(0)
                if l_step == 0:
                    keep, send = halve(keep, got)
                    got_l = swap_by_core(send, SCENE[1])
                elif l_step == 1:
                    block = jnp.concatenate([small, rows[:6]], 0)
                    block = rounded(jnp.concatenate([block[:, : width // 2], block[:, width // 2 :]], 0))
                    extra = block.shape[0]
                    message = jnp.concatenate([keep + got, block], 0)
                    message = lax.optimization_barrier(whole_slice(message))
                    got_l = swap_by_core(message, SCENE[2])
                elif l_step == 2:
                    got = jnp.concatenate([turned(got[:-extra]), got[-extra:]], 0)
                    message = rounded(message.astype(F32) + got.astype(F32))
                    got_l = swap_by_core(message, LATE[0])
                elif l_step < 5:
                    message = grow(message, got)
                    got_l = swap_by_core(message, LATE[l_step - 2])
                    if l_step == 4:
                        near_keep = swap(message[:-extra], "view", 1)
                else:
                    got_l = got
                    near_got = swap(got, "view", 1)
                    small = rounded(message[-extra:].astype(F32) + got[-extra:].astype(F32))
                    other = swap(small, "view", 1)
                if l_step:
                    last.append(message if l_step < 5 else small)
                else:
                    last += [keep, send]
                l_step += 1
            elif name == "G":
                near, rest = swap(near, "view", 1), swap(rest, "view", 1)
            elif name == "P":
                peers = [swap(parts[n].got, "view", 1) for n in "AB"]
    assert l_step == 6 and i_step == 2 and outcome is not None
    grad_squeezer, grad_expander, grad_combiner = feed_assemble(
        gate[0], 1, [parts["A"].got, parts["B"].got, *peers], hid, feed_grads
    )
    near_got, other, grad_squeezer = after((near_got, other, grad_squeezer))
    vectors = [width] * 6 + [hid]
    grad_projector, table, *vectors = assemble(
        gate[0], [message, got_l, near_keep, near_got], [small, other], groups, vectors, width
    )
    grad_scaling, grad_shifting, grad_leveling, grad_baseline, grad_rescaling, grad_reshifting, grad_priming = vectors

    return (
        outcome.reshape(inputs.shape),
        inputs_grad.reshape(inputs.shape),
        table,
        grad_scaling,
        grad_shifting,
        grad_projector,
        grad_combiner,
        grad_baseline,
        grad_rescaling,
        grad_reshifting,
        grad_expander,
        grad_priming,
        grad_squeezer,
        grad_leveling,
    )


def solution(mesh):
    tokens = P("scene", "view", None, None)
    placed = (tokens, P("scene", "view", None)) + (P(),) * 12 + (tokens,)
    return jax.shard_map(
        on_device,
        mesh=mesh,
        in_specs=placed,
        out_specs=(tokens, tokens) + (P(),) * 12,
        check_vma=False,
    )
```

```python
import functools

import jax
import jax.numpy as jnp
from jax import lax
from jax.experimental import pallas as pl
from jax.experimental.pallas import tpu as pltpu
from jax.sharding import PartitionSpec as P

HEADS = 12
HEAD = 64
BF = jnp.bfloat16
F32 = jnp.float32
BOTH = ("scene", "view")
MINE = HEADS // 4 * HEAD
PAD = 256
MIB = 1 << 20


def swap(value, axis, mask):
    count = lax.axis_size(axis)
    return lax.ppermute(value, axis, [(i, i ^ mask) for i in range(count)])


def swap_by_core(value, masks):
    scenes, views = lax.axis_size("scene"), lax.axis_size("view")
    pairs = []
    for s in range(scenes):
        for v in range(views):
            ds, dv = masks[v % 2]
            pairs.append((s * views + v, (s ^ ds) * views + (v ^ dv)))
    return lax.ppermute(value, BOTH, pairs)


def side_of(masks, core):
    scene, view = lax.axis_index("scene"), lax.axis_index("view")
    bits = [((scene & ds) + (view & dv) > 0).astype(jnp.int32) for ds, dv in masks]
    return jnp.where(core == 0, bits[0], bits[1])


def code_of(stages, core):
    total = 0
    for masks in stages:
        total = 2 * total + side_of(masks, core)
    return total


X, Y, Z1, Z2 = (1, 0), (0, 2), (2, 0), (4, 0)
WIDE = ((X, Z1), (Y, X), (Z1, Y), (Z2, Z2))
THIN = ((Y, Y), (Z1, Z1), (X, X), (Z2, Z2))
SCENE = ((X, Z1), (Z1, X), (Z2, Z2))
LATE = ((Y, X), (Z1, Y), (X, Z1))


def rounded(value):
    return lax.optimization_barrier(lax.reduce_precision(value, 8, 7).astype(BF))


def whole_slice(value):
    bit = 8
    while bit < lax.axis_size("scene"):
        value = rounded(value.astype(F32) + swap(value, "scene", bit).astype(F32))
        bit *= 2
    return value


def by_view(blocks, me):
    a, b, c, d = blocks
    one = (me & 1) == 1
    a, b = jnp.where(one, b, a), jnp.where(one, a, b)
    c, d = jnp.where(one, d, c), jnp.where(one, c, d)
    two = (me & 2) == 2
    a, c = jnp.where(two, c, a), jnp.where(two, a, c)
    b, d = jnp.where(two, d, b), jnp.where(two, b, d)
    return a, b, c, d


def normalise(values):
    centre = values - jnp.mean(values, axis=-1, keepdims=True)
    rstd = lax.rsqrt(jnp.mean(centre * centre, axis=-1, keepdims=True) + 1e-05)
    return centre * rstd, rstd


def norm_back(grad, unit, rstd):
    return (
        grad
        - jnp.mean(grad, axis=-1, keepdims=True)
        - unit * jnp.mean(grad * unit, axis=-1, keepdims=True)
    ) * rstd


def dot(a, b):
    return jnp.dot(a, b, preferred_element_type=F32)


def tdot(a, b):
    return lax.dot_general(a, b, (((0,), (0,)), ((), ())), preferred_element_type=F32)


def dott(a, b):
    return lax.dot_general(a, b, (((1,), (1,)), ((), ())), preferred_element_type=F32)


def split3(values):
    high = values.astype(BF)
    rest = values - high.astype(F32)
    middle = rest.astype(BF)
    return high, middle, (rest - middle.astype(F32)).astype(BF)


def onehot_t(cameras, groups):
    rows = lax.broadcasted_iota(jnp.int32, (groups, cameras.shape[1]), 0)
    return (rows == cameras).astype(F32).astype(BF)


class Incoming:
    def __init__(self, source, buffer, sem, whole=None):
        self.copy, self.there = pltpu.make_async_copy(source, buffer, sem), False
        self.buffer = buffer if whole is None else whole
        self.copy.start()

    def __call__(self):
        if not self.there:
            self.copy.wait()
            self.there = True
        return self.buffer


class Present:
    def __init__(self, ref):
        self.buffer = ref

    def __call__(self):
        return self.buffer


class Outgoing:
    def __init__(self, target, buffer, sems, moves):
        self.target, self.ref, self.sems, self.moves = target, buffer, sems, moves

    def send(self, here=None, there=None):
        source = self.ref if here is None else self.ref.at[here]
        target = self.target if there is None else self.target.at[there]
        move = pltpu.make_async_copy(source, target, self.sems.at[len(self.moves)])
        move.start()
        self.moves.append(move)


class Operand:
    def __init__(self, array, *, home=False, ready=False, cut=None, shape=None):
        self.array, self.ready, self.cut, self.apart = array, ready, cut, False
        if home:
            self.array = pltpu.with_memory_space_constraint(array, pltpu.HBM)
        self.shape = array.shape if shape is None else shape


def apart(array):
    operand = Operand(array, home=True)
    operand.apart = True
    return operand


def home(array, **more):
    return Operand(array, home=True, **more)


def ready(array):
    return Operand(array, ready=True)


def staged(body, args, outs, *, name, mib, us, scratch=(), code=None, held=(), buffers=None, early=None):
    buffers = buffers or {}
    args = [a if isinstance(a, Operand) else home(a) for a in args]
    n_code, n_in, n_held, n_out = int(code is not None), len(args), len(held), len(outs)
    loads = [i for i, a in enumerate(args) if not (a.ready or a.apart)]

    def kernel(*refs):
        code_ref = refs[0] if n_code else None
        refs = refs[n_code:]
        ins, refs = refs[:n_in], refs[n_in + n_held :]
        targets, refs = refs[:n_out], refs[n_out:]
        in_bufs, refs = refs[: len(loads)], refs[len(loads) :]
        out_bufs, refs = refs[:n_out], refs[n_out:]
        in_sems, out_sems, rest = refs[0], refs[1], refs[2:]
        arrivals = [Present(ref) for ref in ins]
        if early is not None:
            early(code_ref, ins, rest)
        for n, i in enumerate(loads):
            source = ins[i] if args[i].cut is None else ins[i].at[args[i].cut]
            arrivals[i] = Incoming(source, in_bufs[n], in_sems.at[n])
        moves = []
        leaving = [Outgoing(t, b, out_sems, moves) for t, b in zip(targets, out_bufs, strict=True)]
        body(code_ref, arrivals, leaving, *rest)
        for arrival in arrivals:
            arrival()
        for move in moves:
            move.wait()

    anywhere, vmem = pl.BlockSpec(memory_space=pl.ANY), pl.BlockSpec(memory_space=pltpu.VMEM)
    specs = [pl.BlockSpec(memory_space=pltpu.SMEM)] * n_code
    specs += [vmem if a.ready else anywhere for a in args] + [anywhere] * n_held
    operands = ([code] if n_code else []) + [a.array for a in args]
    operands += [pltpu.with_memory_space_constraint(a, pltpu.HBM) for a in held]
    bufs = [pltpu.VMEM(args[i].shape, args[i].array.dtype) for i in loads]
    return pl.pallas_call(
        kernel,
        in_specs=specs,
        out_specs=[anywhere] * n_out,
        out_shape=[pltpu.HBM(shape, dtype) for shape, dtype in outs],
        scratch_shapes=bufs
        + [pltpu.VMEM(buffers.get(i, o[0]), o[1]) for i, o in enumerate(outs)]
        + [pltpu.SemaphoreType.DMA((max(len(loads), 1),)), pltpu.SemaphoreType.DMA((48,))]
        + list(scratch),
        input_output_aliases={n_code + n_in + i: i for i in range(n_held)},
        compiler_params=pltpu.CompilerParams(vmem_limit_bytes=mib * MIB),
        cost_estimate=pl.CostEstimate(flops=0, bytes_accessed=0, transcendentals=0),
        name=name,
    )(*operands)


def project_rows(tokens, cams, embedding, gain, shift, weight, outs, there, hold_ref, summed=None):
    normed, unit, rstd, *triple = outs
    rows = tokens[0].buffer.shape[0]
    pair = 2 * rows
    table = jnp.concatenate(split3(embedding()[...]), 0)
    hot = onehot_t(cams()[...], embedding().shape[0])
    hold_ref[...] = tdot(jnp.concatenate([hot] * 3, 0), table)
    for at, x in enumerate(tokens):
        here = slice(at * rows, (at + 1) * rows)
        values = x()[...].astype(F32) + hold_ref[here, :]
        if at == 0 and summed is not None:
            summed.ref[...] = values
            summed.send()
        values, scale = normalise(values)
        hold_ref[here, :] = values
        rstd.ref[here, :] = scale
    values = hold_ref[...]
    low = (values * gain()[...] + shift()[...]).astype(BF)
    normed.ref[...] = low
    lane = lax.broadcasted_iota(jnp.int32, (pair, PAD), 1)
    for i, (ref, first, out) in enumerate(triple):
        block = dot(low, weight()[:, i * PAD : (i + 1) * PAD])
        if i == 0:
            block = block * HEAD**-0.5
        if i == 2:
            block = jnp.where(lane < MINE, block, 1.0)
        ref[first : first + pair, :] = block.astype(BF)
        out.send((pl.ds(first, pair),), there)
    normed.send(None, there)
    unit.ref[...] = values.astype(BF)
    unit.send(None, there)
    rstd.send(None, there)


def project_outs(total, width):
    outs = [((total, width), BF), ((total, width), BF), ((total, 1), F32)]
    return outs + [((total, PAD), BF)] * 3


def project_body(_, ins, outs, hold_ref):
    xa, xb, cams, embedding, gain, shift, weight = ins
    there = (pl.ds(0, hold_ref.shape[0]),)
    triple = [(out.ref, 0, out) for out in outs[3:6]]
    project_rows((xa, xb), cams, embedding, gain, shift, weight, [*outs[:3], *triple], there, hold_ref, outs[6])


def project(xa, xb, cams, embedding, gain, shift, weight):
    rows, width = xa.shape[-2:]
    pair, total = 2 * rows, 4 * rows
    outs = project_outs(total, width)
    return staged(
        project_body,
        [xa, ready(xb), cams, embedding, gain, shift, weight],
        [*outs, ((rows, width), F32)],
        name="project",
        mib=32,
        us=5,
        scratch=[pltpu.VMEM((pair, width), F32)],
        buffers={i: (pair, o[0][1]) for i, o in enumerate(outs)},
    )


def blocks_of(total):
    return [(at, min(256, total - at)) for at in range(0, total, 256)]


TILE = 128


def tile_of(head):
    at = head * HEAD // TILE * TILE
    return slice(at, at + TILE)


def one_head(block, head):
    lane = lax.broadcasted_iota(jnp.int32, block.shape, 1) // HEAD
    return jnp.where(lane == head % (TILE // HEAD), block, jnp.zeros_like(block))


def attend_rows(q_ref, keys, values_of, outs, vt_ref, mt_ref):
    e, first, second, inv = outs
    pair, heads = q_ref.shape[0], e.ref.shape[0]
    work = [(h, at, size) for h in range(heads) for at, size in blocks_of(pair)]

    def scores(h, at, size):
        return dott(keys()[:, tile_of(h)], one_head(q_ref[at : at + size, tile_of(h)], h))

    keys(), values_of()
    ahead = scores(*work[0])
    vt_ref[...] = values_of()[...].astype(F32).T.astype(BF)
    mt_ref[...] = jnp.zeros_like(mt_ref)
    inv.ref[...] = jnp.zeros_like(inv.ref)
    for i, (h, at, size) in enumerate(work):
        here = ahead
        if i + 1 < len(work):
            ahead = scores(*work[i + 1])
        mine = slice(h * HEAD, (h + 1) * HEAD)
        expo = jnp.exp(here - jnp.max(here, 0, keepdims=True)).astype(BF)
        cut = (h, slice(None), slice(at, at + size))
        e.ref[cut] = expo
        if at + size == pair:
            e.send((h,), (h,))
        values = jnp.concatenate([vt_ref[mine, :], vt_ref[MINE : MINE + 16, :]], 0)
        out = dot(values, expo)
        inverse = 1.0 / out[HEAD : HEAD + 1, :]
        mt_ref[mine, at : at + size] = out[:HEAD, :] * inverse
        inv.ref[h : h + 1, at : at + size] = inverse
    mixed = mt_ref[...].T[:pair]
    first.ref[...] = mixed[: pair // 2, :MINE].astype(BF)
    first.send()
    second.ref[...] = mixed[pair // 2 :, :MINE].astype(BF)
    second.send()
    inv.send()


def attend_outs(total):
    pair, heads = total // 2, MINE // HEAD
    wide = -(-pair // 128) * 128
    part = ((pair // 2, MINE), BF)
    return [((heads, total, pair), BF), part, part, ((8, wide), F32)]


def attend_scratch(total):
    wide = -(-(total // 2) // 128) * 128
    return [pltpu.VMEM((PAD, total), BF), pltpu.VMEM((PAD, wide), F32)]


def attend_body(_, ins, outs, *scratch):
    q, k, v = ins
    attend_rows(q(), k, v, outs, *scratch)


def attend(q, k, v):
    total = k.shape[0]
    pair = total // 2
    return staged(
        attend_body,
        [home(q, cut=(pl.ds(0, pair),), shape=(pair, PAD)), home(k), home(v)],
        attend_outs(total),
        name="attend",
        mib=32,
        us=8,
        scratch=attend_scratch(total),
    )


def second_body(_, ins, outs, hold_ref, *scratch):
    xa, xb, cams, embedding, gain, shift, weight = ins
    pair = hold_ref.shape[0]
    keys_ref, values_ref, sems, *scratch = scratch
    first = pl.ds(0, pair)
    k, v = (
        Incoming(out.target.at[first], ref.at[first], sems.at[i], ref)
        for i, (out, ref) in enumerate(((outs[4], keys_ref), (outs[5], values_ref)))
    )
    there = (pl.ds(pair, pair),)
    triple = [(outs[3].ref, 0, outs[3]), (k.buffer, pair, outs[4]), (v.buffer, pair, outs[5])]
    outs[4].ref, outs[5].ref = k.buffer, v.buffer
    project_rows((xa, xb), cams, embedding, gain, shift, weight, [*outs[:3], *triple], there, hold_ref)
    attend_rows(outs[3].ref, k, v, outs[6:], *scratch)
    k()
    v()


def second_half(xa, xb, cams, embedding, gain, shift, weight, held):
    rows, width = xa.shape[-2:]
    pair, total = 2 * rows, 4 * rows
    outs = project_outs(total, width)
    buffers = {i: (pair, o[0][1]) for i, o in enumerate(outs)}
    buffers[4] = buffers[5] = (16, PAD)
    return staged(
        second_body,
        [xa, ready(xb), ready(cams), embedding, gain, shift, weight],
        [*outs, *attend_outs(total)],
        name="second_half",
        mib=44,
        us=10,
        scratch=[
            pltpu.VMEM((pair, width), F32),
            pltpu.VMEM((total, PAD), BF),
            pltpu.VMEM((total, PAD), BF),
            pltpu.SemaphoreType.DMA((2,)),
            *attend_scratch(total),
        ],
        held=held,
        buffers=buffers,
    )


def back_heads(heads, q_ref, v_ref, g_ref, kt_ref, delta_of, expos, dq_ref, dk_ref, dv_ref):
    pair = q_ref.shape[0] // 2
    work = [(h, i, at, size) for h in heads for i in range(2) for at, size in blocks_of(pair)]
    dq_ref[...] = jnp.zeros_like(dq_ref)

    def cut(ref, h, i, at, size):
        return one_head(ref[i * pair + at : i * pair + at + size, :], h)

    ahead_grad = cut(g_ref, *work[0])
    ahead = dott(v_ref[...], ahead_grad)
    for n, (h, i, at, size) in enumerate(work):
        if i == at == 0:
            expos[2 * heads.index(h)]()
            expos[2 * heads.index(h) + 1]()
        grad, prob_grad = ahead_grad, ahead
        if n + 1 < len(work):
            ahead_grad = cut(g_ref, *work[n + 1])
            ahead = dott(v_ref[...], ahead_grad)
        expo = expos[2 * heads.index(h) + i]()[:, at : at + size]
        score_grad = (expo.astype(F32) * (prob_grad - delta_of(h, i, at, size))).astype(BF)
        value_part = dot(expo, grad)
        key_part = dot(score_grad, cut(q_ref, h, i, at, size))
        if n:
            value_part += dv_ref[...]
            key_part += dk_ref[...]
        dv_ref[...] = value_part
        dk_ref[...] = key_part
        mine = slice(h * HEAD % TILE, h * HEAD % TILE + HEAD)
        dq_ref[i, mine, at : at + size] = dot(kt_ref[mine, :], score_grad)


def back_first_body(code, ins, outs, g_ref, kt_ref, dq_ref, dk_ref, dv_ref, hold_ref):
    grads, invs, mixes, (v, k, q), expos = ins[:4], ins[4:6], ins[6:10], ins[10:13], ins[13:]
    dq, dk, dv, g_rest, delta = outs
    total = q.buffer.shape[0]
    pair, rows = total // 2, grads[0].buffer.shape[0]
    for arrival in (*grads, *invs, *mixes):
        arrival()
    hold_ref[...] = jnp.zeros_like(hold_ref)
    for i, grad in enumerate(grads):
        hold_ref[i * rows : (i + 1) * rows, :MINE] = grad()[...].astype(F32)
    lane = lax.broadcasted_iota(jnp.int32, (8, PAD), 1) // HEAD
    pick = (lane == lax.broadcasted_iota(jnp.int32, (8, PAD), 0)).astype(F32).astype(BF)
    for i in range(2):
        here = slice(i * pair, (i + 1) * pair)
        inverse = invs[i]()[...].T[:pair, :]
        lane = lax.broadcasted_iota(jnp.int32, (pair, PAD), 1) // HEAD
        scale = jnp.zeros((pair, PAD), F32)
        for h in range(MINE // HEAD):
            scale = jnp.where(lane == h, inverse[:, h : h + 1], scale)
        scaled = (hold_ref[here, :] * scale).astype(BF)
        g_ref[here, :] = scaled[:, :TILE]
        g_rest.ref[here, :] = scaled[:, TILE:]
        for j in range(2):
            rows_here = slice(i * pair + j * rows, i * pair + (j + 1) * rows)
            hold_ref[rows_here, :MINE] = mixes[2 * i + j]()[...].astype(F32)
        prod = scaled.astype(F32) * hold_ref[here, :]
        high = prod.astype(BF)
        low = (prod - high.astype(F32)).astype(BF)
        delta.ref[8 * i : 8 * i + 8, :pair] = dott(pick, high) + dott(pick, low)
        delta.ref[8 * i : 8 * i + 8, pair:] = jnp.zeros((8, delta.ref.shape[1] - pair), F32)
    g_rest.send()
    delta.send()
    for arrival in (v, k, q, *expos[:2]):
        arrival()
    kt_ref[...] = k()[...].astype(F32).T.astype(BF)

    def delta_of(h, i, at, size):
        return delta.ref[8 * i + h : 8 * i + h + 1, at : at + size]

    back_heads((0, 1), q(), v(), g_ref, kt_ref, delta_of, expos, dq_ref, dk_ref, dv_ref)
    for i in range(2):
        dq.ref[i * pair : (i + 1) * pair, :] = (dq_ref[i].T[:pair] * HEAD**-0.5).astype(BF)
    dq.send()
    dk.ref[...] = dk_ref[...].astype(BF)
    dk.send()
    dv.ref[...] = dv_ref[...].astype(BF)
    dv.send()


def back_last_body(code, ins, outs, kt_ref, dq_ref, dk_ref, dv_ref, piece_ref):
    v, g, k, q, delta, *expos = ins[:7]
    dq0, dk0, dv0, normed = ins[7:]
    dqk, dv, keep, send = outs
    pair = q.buffer.shape[0] // 2
    for arrival in (v, g, k, q, delta):
        arrival()
    kt_ref[...] = k()[...].astype(F32).T.astype(BF)

    def delta_of(h, i, at, size):
        return delta()[8 * i + h : 8 * i + h + 1, at : at + size]

    back_heads((2,), q(), v(), g(), kt_ref, delta_of, expos, dq_ref, dk_ref, dv_ref)
    rest = MINE - TILE
    dqk.ref[:, :TILE] = dq0()[...]
    for i in range(2):
        dq = (dq_ref[i].T[:pair] * HEAD**-0.5).astype(BF)
        dqk.ref[i * pair : (i + 1) * pair, TILE:MINE] = dq[:, :rest]
    dqk.ref[:, MINE : MINE + TILE] = dk0()[...]
    dqk.ref[:, MINE + TILE :] = dk_ref[:, :rest].astype(BF)
    dv.ref[:, :TILE] = dv0()[...]
    dv.ref[:, TILE:] = dv_ref[:, :rest].astype(BF)
    weight_grad(code, normed, dqk.ref, dv.ref, keep, send, piece_ref)
    dqk.send()
    dv.send()


PIECES = 8


def weight_grad(code, normed, dqk_ref, dv_ref, keep, send, hold_ref):
    width = normed().shape[1]
    rows = width // PIECES
    piece = rows + rows // 2
    mine = code[0]
    qk = tdot(normed()[...], dqk_ref[...]).astype(BF)
    v = tdot(normed()[...], dv_ref[...]).astype(BF)
    for p in range(PIECES):
        at = pl.multiple_of((p ^ mine) * piece, 16)
        hold_ref[pl.ds(at, rows), :] = qk[p * rows : (p + 1) * rows]
        at = pl.multiple_of((p ^ mine) * piece + rows, 16)
        top = v[p * rows : p * rows + rows // 2]
        low = v[p * rows + rows // 2 : (p + 1) * rows]
        hold_ref[pl.ds(at, rows // 2), :] = jnp.concatenate([top, low], 1)
    half = PIECES * piece // 2
    send.ref[...] = hold_ref[half:, :]
    send.send()
    keep.ref[...] = hold_ref[:half, :]
    keep.send()


def back_scratch(total):
    wide = -(-(total // 2) // 128) * 128
    return [
        pltpu.VMEM((TILE, total), BF),
        pltpu.VMEM((2, TILE, wide), F32),
        pltpu.VMEM((total, TILE), F32),
        pltpu.VMEM((total, TILE), F32),
    ]


def tile_cut(array, tile):
    return home(array, cut=(slice(None), pl.ds(tile * TILE, TILE)), shape=(array.shape[0], TILE))


def back_first(q, k, v, e0, e1, grads, mixes, inv0, inv1):
    total = k.shape[0]
    pair = total // 2
    wide = -(-pair // 128) * 128
    args = [grads[0], *map(ready, grads[1:]), inv0, inv1, *mixes] + [tile_cut(a, 0) for a in (v, k, q)]
    args += [home(e, cut=(h,), shape=(total, pair)) for h in range(2) for e in (e0, e1)]
    return staged(
        back_first_body,
        args,
        [((total, TILE), BF)] * 4 + [((16, wide), F32)],
        name="back_first",
        mib=40,
        us=12,
        scratch=[pltpu.VMEM((total, TILE), BF), *back_scratch(total), pltpu.VMEM((total, PAD), F32)],
    )


def back_last(codes, q, k, v, e0, e1, first, normed):
    total, width = k.shape[0], normed.shape[1]
    pair = total // 2
    dq, dk, dv, g, delta = first
    piece = width // PIECES * 3 // 2
    half = ((PIECES * piece // 2, 2 * MINE), BF)
    args = [tile_cut(v, 1), g, tile_cut(k, 1), tile_cut(q, 1), delta]
    args += [home(e, cut=(2,), shape=(total, pair)) for e in (e0, e1)]
    return staged(
        back_last_body,
        [*args, dq, dk, dv, normed],
        [((total, 2 * MINE), BF), ((total, MINE), BF), half, half],
        name="back_last",
        mib=40,
        us=10,
        scratch=[*back_scratch(total), pltpu.VMEM((PIECES * piece, 2 * MINE), BF)],
        code=codes,
    )


STEP = 512


def feed_forward_body(code, ins, outs):
    summed, own, near, far, rest, combiner, baseline, gain, shift, expander, priming, squeezer, tangent = ins
    residual, own_wide, wide, own_slim, slim = outs
    me = code[2]
    first = code[3] == 0
    total = summed()[...] + baseline()[...]
    for r, block in ((2, far), (3, rest), (0, own), (1, near)):
        at = pl.multiple_of((me ^ r) * MINE, 16)
        total += dot(block()[...], combiner()[pl.ds(at, MINE), :])
    residual.ref[...] = total
    residual.send()
    unit, _ = normalise(total)
    low = (unit * gain()[...] + shift()[...]).astype(BF)
    own_slim.ref[...] = jnp.where(first, tangent()[...], low)
    own_slim.send()
    slim.ref[...] = jnp.where(first, low, tangent()[...])
    slim.send()
    for at in range(0, expander().shape[1], STEP):
        cut = slice(at, at + STEP)
        hidden = dot(low, expander()[:, cut]) + priming()[cut]
        back = dott(tangent()[...], squeezer()[cut, :])
        phi = 0.5 * (1.0 + lax.erf(hidden * (2.0**-0.5)))
        density = jnp.exp(-0.5 * hidden * hidden) * 0.3989422804014327
        active = (hidden * phi).astype(BF)
        grad = (back * (phi + hidden * density)).astype(BF)
        own_wide.ref[:, cut] = jnp.where(first, active, grad)
        wide.ref[:, cut] = jnp.where(first, grad, active)
        part = (slice(None), pl.ds(at, STEP))
        own_wide.send(part, part)
        wide.send(part, part)


def feed_forward(codes, summed, own, near, far, rest, combiner, baseline, gain, shift, expander, priming, squeezer, tangent):
    rows, width = summed.shape
    hid = expander.shape[1]
    weights = [combiner, baseline, gain, shift, expander, priming, squeezer, tangent]
    return staged(
        feed_forward_body,
        [home(summed), own, ready(near), ready(far), ready(rest), *weights],
        [((rows, width), F32), ((rows, hid), BF), ((rows, hid), BF), ((rows, width), BF), ((rows, width), BF)],
        name="feed_forward",
        mib=24,
        us=6,
        code=codes,
    )


def feed_back_body(code, ins, outs, grad_ref, sem):
    expander, residual, gain, tangent, combiner, own_wide, wide = ins
    residual_grad, low, *grads, rows = outs
    me = code[2]
    pltpu.make_async_copy(wide(), grad_ref, sem.at[0]).wait()
    second_grad = dott(grad_ref[...], expander()[...])
    unit, rstd = normalise(residual()[...])
    slope = tangent()[...].astype(F32)
    total = slope + norm_back(second_grad * gain()[...], unit, rstd)
    low.ref[...] = total.astype(BF)
    low.send()
    for r in (2, 3, 1, 0):
        at = pl.multiple_of((me ^ r) * MINE, 16)
        grads[r].ref[...] = dott(low.ref[...], combiner()[pl.ds(at, MINE), :]).astype(BF)
        grads[r].send()
    residual_grad.ref[...] = total
    residual_grad.send()
    width = total.shape[1]
    rows.ref[0:1, :] = jnp.sum(slope, 0, keepdims=True)
    rows.ref[1:2, :] = jnp.sum(low.ref[...].astype(F32), 0, keepdims=True)
    rows.ref[2:3, :] = jnp.sum(second_grad * unit, 0, keepdims=True)
    rows.ref[3:4, :] = jnp.sum(second_grad, 0, keepdims=True)
    for j in range(grad_ref.shape[1] // width):
        block = grad_ref[:, j * width : (j + 1) * width].astype(F32)
        rows.ref[4 + j : 5 + j, :] = jnp.sum(block, 0, keepdims=True)
    rows.ref[6:8, :] = jnp.zeros((2, width), F32)
    rows.send()


def pick_wide(on_zero, on_one):
    def early(code, operands, scratch):
        for core, place in enumerate((on_zero, on_one)):

            @pl.when(code[3] == core)
            def _():
                pltpu.make_async_copy(operands[place], scratch[0], scratch[1].at[0]).start()

    return early


def feed_back(codes, residual, own_wide, wide, tangent, expander, gain, combiner):
    rows, width = residual.shape
    return staged(
        feed_back_body,
        [expander, home(residual), gain, tangent, combiner, apart(own_wide), apart(wide)],
        [((rows, width), F32), ((rows, width), BF)] + [((rows, MINE), BF)] * 4 + [((8, width), F32)],
        early=pick_wide(6, 5),
        name="feed_back",
        mib=24,
        us=6,
        scratch=[pltpu.VMEM(wide.shape, BF), pltpu.SemaphoreType.DMA((1,))],
        code=codes,
    )


def outcome_body(code, ins, outs, active_ref, sem):
    squeezer, residual, leveling, own_wide, wide = ins
    pltpu.make_async_copy(wide(), active_ref, sem.at[0]).wait()
    outs[0].ref[...] = (residual()[...] + dot(active_ref[...], squeezer()[...]) + leveling()[...]).astype(BF)
    outs[0].send()


def outcome_of(codes, residual, own_wide, wide, squeezer, leveling):
    rows, width = residual.shape
    return staged(
        outcome_body,
        [squeezer, home(residual), leveling, apart(own_wide), apart(wide)],
        [((rows, width), BF)],
        early=pick_wide(3, 4),
        name="outcome",
        mib=16,
        us=4,
        scratch=[pltpu.VMEM(wide.shape, BF), pltpu.SemaphoreType.DMA((1,))],
        code=codes,
    )[0]


PARTS = 16


def place(code, piece, size):
    return pl.multiple_of((piece ^ code) * size, 8)


def segments(first, rows, low, size):
    out, at = [], first
    while at < first + rows:
        piece, offset = divmod(at - low, size)
        count = min(size - offset, first + rows - at)
        out.append((piece, offset, at - first, count))
        at += count
    return out


def spread(hold_ref, block, first, low, size, code):
    for piece, offset, start, count in segments(first, block.shape[0], low, size):
        at = pl.multiple_of(place(code, piece, size) + offset, 8)
        hold_ref[pl.ds(at, count), :] = block[start : start + count]


def feed_grad_body(sizes, code, ins, outs, tokens_ref, sems, *holds):
    own_wide, own_slim, wide, slim, own, far, near, rest, resid, other = ins
    hid, width = own_wide().shape[1], own_slim().shape[1]
    assert hid == 2 * width
    bulk = PARTS * sizes[0]
    rows = own_slim().shape[0]
    room = tokens_ref.shape[1] // 2
    gap = rows // 16 * 16
    loads = []
    for n, (big, small) in enumerate(((own_wide, own_slim), (wide, slim))):
        first = n * room
        for j in range(3):
            tokens_ref[j, first + gap : first + room, :] = jnp.zeros((room - gap, width), BF)
    for n, (big, small) in enumerate(((own_wide, own_slim), (wide, slim))):
        there = pl.ds(n * room, rows)
        for j in range(hid // width):
            source = big().at[:, pl.ds(j * width, width)]
            loads.append(pltpu.make_async_copy(source, tokens_ref.at[j, there], sems.at[3 * n + j]))
        loads.append(pltpu.make_async_copy(small(), tokens_ref.at[2, there], sems.at[3 * n + 2]))
    for load in loads:
        load.start()
    for load in loads:
        load.wait()

    def put(block, row):
        for part, low, high in ((0, 0, bulk), (1, bulk, bulk + PARTS * sizes[1])):
            first, last = max(row, low), min(row + block.shape[0], high)
            if first < last:
                spread(holds[part], block[first - row : last - row], first, low, sizes[part], code[4 + 2 * part])

    for j in range(hid // width):
        left = jnp.where(code[3] == 0, j, 2)
        right = jnp.where(code[3] == 0, 2, j)
        block = tdot(tokens_ref[left], tokens_ref[right])
        put(block, j * width)

    upper = code[2] < 2
    for i in range(2):
        here = jnp.where(upper, (own, far)[i]()[...], (far, own)[i]()[...])
        peer = jnp.where(upper, (near, rest)[i]()[...], (rest, near)[i]()[...])
        put(tdot(here, resid()[...]) + tdot(peer, other()[...]), hid + i * MINE)
    for part, hold_ref in enumerate(holds):
        keep, send = outs[2 * part : 2 * part + 2]
        half = hold_ref.shape[0] // 2
        send.ref[...] = hold_ref[half:, :].astype(BF)
        send.send()
        keep.ref[...] = hold_ref[:half, :].astype(BF)
        keep.send()


def feed_grad(codes, sizes, feed, mixed):
    rows, width = feed[1].shape
    halves = [((PARTS * size // 2, width), BF) for size in sizes]
    return staged(
        functools.partial(feed_grad_body, sizes),
        [apart(feed[0]), apart(feed[1]), *map(ready, feed[2:]), mixed[0], *map(ready, mixed[1:4]), mixed[4], ready(mixed[5])],
        [halves[0], halves[0], halves[1], halves[1]],
        name="feed_grad",
        mib=40,
        us=7,
        scratch=[
            pltpu.VMEM((3, 2 * (-(-rows // 16) * 16), width), BF),
            pltpu.SemaphoreType.DMA((6,)),
            *[pltpu.VMEM((PARTS * size, width), F32) for size in sizes],
        ],
        code=codes,
    )


def feed_assemble_body(side, sizes, code, ins, outs, sems, *holds):
    squeezer, expander, combiner = (out.target for out in outs)
    hid, width = squeezer.shape

    def targets(core, row, count):
        out = []
        while count:
            if row < hid and core == 0:
                take = min(count, hid - row)
                out.append((squeezer.at[pl.ds(row, take), :], take))
            elif row < hid:
                j = row // width
                take = min(count, (j + 1) * width - row)
                cut = pl.ds(row - j * width, take), pl.ds(j * width, width)
                out.append((expander.at[cut], take))
            else:
                view, at = divmod(row - hid, MINE)
                take = min(count, MINE - at)
                out.append((combiner.at[pl.ds((core + 2 * view) * MINE + at, take), :], take))
            row, count = row + take, count - take
        return out

    for i, hold_ref in enumerate(holds):
        half = hold_ref.shape[0] // 2
        hold_ref[:half, :] = ins[2 * i]()[...].astype(F32)
        hold_ref[half:, :] = ins[2 * i + 1]()[...].astype(F32)
    for core in range(2):

        @pl.when(code[3] == core ^ side)
        def _():
            moves, low = [], 0
            for part, size in enumerate(sizes):
                for piece in range(PARTS):
                    start = pl.multiple_of((piece ^ code[4 + 2 * part + side]) * size, 8)
                    at = 0
                    for target, count in targets(core, low + piece * size, size):
                        source = holds[part].at[pl.ds(pl.multiple_of(start + at, 8), count), :]
                        moves.append(pltpu.make_async_copy(source, target, sems.at[len(moves)]))
                        moves[-1].start()
                        at += count
                low += PARTS * size
            for move in moves:
                move.wait()


def feed_assemble(codes, side, blocks, hid, held=()):
    width = blocks[0].shape[1]
    sizes = [blocks[0].shape[0] // 8, blocks[2].shape[0] // 8]
    return staged(
        functools.partial(feed_assemble_body, side, sizes),
        [Operand(b) for b in blocks],
        [((hid, width), F32), ((width, hid), F32), ((width, width), F32)],
        name="feed_assemble",
        mib=24,
        us=5,
        scratch=[pltpu.SemaphoreType.DMA((48,))] + [pltpu.VMEM((PARTS * n, width), F32) for n in sizes],
        code=codes,
        held=held,
        buffers={0: (8, 128), 1: (8, 128), 2: (8, 128)},
    )


def input_grad_body(_, ins, outs, hold_ref):
    dqk, dv, weight, unit, rstd, gain, *rest = ins
    near_cams, far_cams, resid = rest
    small = outs[4]
    patches = resid.buffer.shape[0]
    groups = small.ref.shape[0] - 2
    slope = dott(dqk()[:, :MINE], weight()[:, :MINE]) + dott(dqk()[:, MINE:], weight()[:, PAD : PAD + MINE])
    slope += dott(dv()[...], weight()[:, 2 * PAD : 2 * PAD + MINE])
    values = unit()[...].astype(F32)
    small.ref[groups : groups + 1, :] = jnp.sum(slope * values, 0, keepdims=True)
    small.ref[groups + 1 : groups + 2, :] = jnp.sum(slope, 0, keepdims=True)
    hold_ref[...] = norm_back(slope * gain()[...], values, rstd()[...])
    for r in (1, 3, 0, 2):
        part = hold_ref[r * patches : (r + 1) * patches, :]
        outs[r].ref[...] = part.astype(outs[r].ref.dtype)
        outs[r].send()
    hold_ref[:patches, :] = hold_ref[:patches, :] + resid()[...]
    table = jnp.zeros((groups, slope.shape[1]), F32)
    for i, cams in enumerate((near_cams, far_cams)):
        part = hold_ref[2 * i * patches : 2 * (i + 1) * patches, :]
        hot = onehot_t(cams()[...], groups)
        for piece in split3(part)[:2]:
            table += dot(hot, piece)
    small.ref[:groups, :] = table
    small.send()


def input_grad(dqk, dv, weight, unit, rstd, gain, cams, resid, groups):
    total, width = unit.shape
    patches = resid.shape[0]
    low, full = ((patches, width), BF), ((patches, width), F32)
    return staged(
        input_grad_body,
        [home(dqk), home(dv), home(weight), home(unit), home(rstd), gain, *cams, home(resid)],
        [full, low, full, low, ((groups + 2, width), F32)],
        name="input_grad",
        mib=48,
        us=9,
        scratch=[pltpu.VMEM((total, width), F32)],
    )


def assemble_body(code, ins, outs):
    out, table, *vectors = outs
    rows, width = out.ref.shape[0] // PIECES, out.ref.shape[1] // 3
    piece = rows * 3 // 2
    blocks = [arrival() for arrival in ins[:4]]
    for p in range(PIECES):
        cut = []
        for i, which in enumerate((0, 1, 0, 1)):
            r = (p ^ code[which]) % 4
            core = code[3] if which == 0 else 1 - code[3]
            far = i // 2
            middle = jnp.where(core == 0, r // 2 * 2 + far, far * 2 + r // 2)
            at = pl.multiple_of((middle * 2 + r % 2) * piece, 16)
            upper = (p ^ code[which]) >= PIECES // 2
            lower_block = blocks[2 * which][pl.ds(at, piece), :]
            upper_block = blocks[2 * which + 1][pl.ds(at, piece), :]
            cut.append(jnp.where(upper, upper_block, lower_block).astype(F32))
        low = p * rows
        for v, block in enumerate(by_view(cut, code[2])):
            at = v * MINE
            out.ref[low : low + rows, at : at + MINE] = block[:rows, :MINE]
            out.ref[low : low + rows, width + at : width + at + MINE] = block[:rows, MINE:]
            at += 2 * width
            out.ref[low : low + rows // 2, at : at + MINE] = block[rows:, :MINE]
            out.ref[low + rows // 2 : low + rows, at : at + MINE] = block[rows:, MINE:]
        out.send((pl.ds(low, rows),), (pl.ds(low, rows),))
    total = ins[4]()[...].astype(F32) + ins[5]()[...].astype(F32)
    count, half, groups = total.shape[0] // 2, width // 2, table.ref.shape[0]
    table.ref[:, :half] = total[:groups, :]
    table.ref[:, half:] = total[count : count + groups, :]
    table.send()
    row = groups
    for vector in vectors:
        for at in range(0, vector.ref.shape[0], width):
            vector.ref[at : at + half] = total[row, :]
            vector.ref[at + half : at + width] = total[count + row, :]
            row += 1
        vector.send()


def assemble(codes, blocks, smalls, groups, sizes, width):
    return staged(
        assemble_body,
        [Operand(b) for b in (*blocks, *smalls)],
        [((width, 3 * width), F32), ((groups, width), F32)] + [((size,), F32) for size in sizes],
        name="assemble",
        mib=24,
        us=5,
        code=codes,
    )


def turned(block):
    half = block.shape[0] // 2
    return jnp.concatenate([block[half:], block[:half]], 0)


def after(values, *others):
    out = lax.optimization_barrier((*values, *others))
    return out[: len(values)]


def halve(keep, got):
    cut = keep.shape[0] // 2
    return keep[:cut] + got[:cut], keep[cut:] + got[cut:]


class Part:
    def __init__(self, keep, got, stages):
        self.value, self.got, self.stages, self.step, self.lower, self.peer = keep, got, stages, 0, None, None

    def begin(self):
        self.value, send = halve(self.value, self.got)
        self.got = swap_by_core(send, self.stages[2])

    def advance(self, got):
        self.step += 1
        if self.step == 1:
            self.value = lax.optimization_barrier(whole_slice(self.value + got))
            self.got = swap_by_core(self.value, self.stages[3])
        elif self.step == 2:
            self.value = lax.optimization_barrier(self.value + turned(got))
            self.got = swap_by_core(self.value, self.stages[2])
        elif self.step == 3:
            self.value = jnp.concatenate([self.value, got], 0)
            self.got = swap_by_core(self.value, self.stages[1])
        elif self.step == 4:
            self.value = jnp.concatenate([self.value, got], 0)
            self.got, peer = swap_by_core(self.value, self.stages[0]), swap(self.value, "view", 1)
            self.lower = (self.value, peer)
        else:
            self.got, self.peer = got, swap(got, "view", 1)
            return []
        return [self.value]


PLAN = ("LAB", "LAG", "BI", "AO", "B", "L", "AI", "L", "B", "Lp", "AB", "P", "Lkq")


def on_device(
    inputs,
    cameras,
    embedding,
    scaling,
    shifting,
    projector,
    combiner,
    baseline,
    rescaling,
    reshifting,
    expander,
    priming,
    squeezer,
    leveling,
    cotangent,
):
    me = lax.axis_index("view")
    core = me % 2
    patches, width = inputs.shape[2], inputs.shape[3]
    groups, hid = embedding.shape[0], expander.shape[1]
    codes = [code_of(SCENE, core), code_of(SCENE, 1 - core), me, core]
    codes += [code_of(WIDE, core), code_of(WIDE, 1 - core), code_of(THIN, core), code_of(THIN, core)]
    codes = jnp.stack(codes).astype(jnp.int32)
    tangent = cotangent.reshape(patches, width)
    x0 = inputs.reshape(patches, width)
    c0 = cameras.reshape(1, patches)
    x2 = swap(x0, "view", 2)
    x1, c1 = swap(x0, "view", 1), swap(c0, "view", 1)
    near_cams = jnp.concatenate([c0, c1], 1)
    far_cams = swap(near_cams, "view", 2)
    hole = jnp.zeros((width, PAD - MINE), BF)
    padded = []
    for part in range(3):
        padded += [lax.dynamic_slice_in_dim(projector, part * width + me * MINE, MINE, 1), hole]
    padded = jnp.concatenate(padded, 1)
    *held, summed = project(x0, x1, near_cams, embedding, scaling, shifting, padded)
    x2, far_cams = after((x2, far_cams), *held)
    x3 = swap(x2, "view", 1)
    normed, unit1, rstd1, q, k, v, e1, far, rest, inv1 = second_half(
        x2, x3, far_cams, embedding, scaling, shifting, padded, held
    )
    mine_far, mine_rest = far, rest
    far, rest = swap(far, "view", 2), swap(rest, "view", 3)
    e0, own, near, inv0 = attend(q, k, v)
    mixes = [own, near, mine_far, mine_rest]
    near, own, far, rest = after((near, own, far, rest))
    near, peer_rest = swap(near, "view", 1), swap(rest, "view", 1)

    residual, own_wide, wide, own_slim, slim = feed_forward(
        codes, summed, own, near, far, rest, combiner, baseline, rescaling, reshifting, expander, priming,
        squeezer, tangent,
    )
    peer_near = swap(near, "view", 1)
    peer_wide, peer_slim = swap(wide, "view", 1), swap(slim, "view", 1)
    residual_grad, resid_low, *grads, rows = feed_back(
        codes, residual, own_wide, wide, tangent, expander, rescaling, combiner
    )
    peer_near, peer_rest, resid_low, *grads = after((peer_near, peer_rest, resid_low, *grads))
    grads = [grads[0]] + [swap(grads[r], "view", r) for r in (1, 2, 3)]
    other = swap(resid_low, "view", 1)
    sizes = [(hid + width // 2) // 24, (hid + width // 2) // 48]
    keep0, send0, keep1, send1 = feed_grad(
        codes, sizes, [own_wide, own_slim, peer_wide, peer_slim],
        [own, far, peer_near, peer_rest, resid_low, other],
    )
    *grads, keep0, send0, keep1, send1 = after((*grads, keep0, send0, keep1, send1))
    got0, got1 = swap_by_core(send0, WIDE[0]), swap_by_core(send1, THIN[0])
    first = back_first(q, k, v, e0, e1, grads, mixes, inv0, inv1)
    got0, got1, *first = after((got0, got1, *first))
    keep0, send0 = halve(keep0, got0)
    keep1, send1 = halve(keep1, got1)
    got0, got1 = swap_by_core(send0, WIDE[1]), swap_by_core(send1, THIN[1])
    dqk, dv, keep, send = back_last(codes, q, k, v, e0, e1, first, normed)
    got0, got1, dqk, dv, keep, send = after((got0, got1, dqk, dv, keep, send))
    wide_part = Part(keep0, got0, WIDE)
    thin_part = Part(keep1, got1, THIN)
    got_l = swap_by_core(send, SCENE[0])
    wide_part.begin()
    thin_part.begin()
    parts = dict(A=wide_part, B=thin_part)
    l_step, i_step = 0, 0
    message = near_keep = near_got = other = small = None
    outcome = inputs_grad = feed_grads = None
    last = []
    gate = [codes, dqk]
    extra = 0

    def grow(message, got):
        small = rounded(message[-extra:].astype(F32) + got[-extra:].astype(F32))
        return jnp.concatenate([message[:-extra], got[:-extra], small], 0)

    for group in PLAN:
        tied = []
        if "O" in group:
            outcome = outcome_of(gate[0], residual, own_wide, wide, squeezer, leveling)
            tied.append(outcome)
        if "G" in group:
            own, near, far, rest, small = input_grad(
                gate.pop(), dv, padded, unit1, rstd1, scaling, (near_cams, far_cams), residual_grad, groups
            )
            tied += [near, rest, small]
        if "P" in group:
            blocks = [b for n in "AB" for b in (parts[n].lower[0], parts[n].got)]
            feed_grads = feed_assemble(gate[0], 0, blocks, hid)
            tied += feed_grads
        waits = []
        for name in group:
            if name in "AB":
                waits.append(parts[name].got)
            elif name == "L":
                waits.append(got_l)
            elif name == "I":
                waits += [near, rest] if i_step == 0 else [far]
            elif name == "p":
                waits += [parts["A"].lower[1], parts["B"].lower[1]]
            elif name == "k":
                waits.append(near_keep)
            elif name == "q":
                waits += [parts[n].peer for n in "AB"]
        bundle = list(after((*waits, *tied, *last, *gate)))
        new_waits, rest_of = bundle[: len(waits)], bundle[len(waits) :]
        new_tied, gate = rest_of[: len(tied)], rest_of[len(rest_of) - len(gate) :]
        if "O" in group:
            outcome = new_tied.pop(0)
        if "G" in group:
            near, rest, small = new_tied[:3]
            new_tied = new_tied[3:]
        if "P" in group:
            feed_grads = new_tied
        last = []
        for name in group:
            if name in "AB":
                last += parts[name].advance(new_waits.pop(0))
            elif name == "p":
                for n in "AB":
                    parts[n].lower = (parts[n].lower[0], new_waits.pop(0))
            elif name == "k":
                near_keep = new_waits.pop(0)
            elif name == "q":
                for n in "AB":
                    parts[n].peer = new_waits.pop(0)
            elif name == "I":
                if i_step == 0:
                    near, rest = new_waits.pop(0), new_waits.pop(0)
                    far = lax.optimization_barrier((far + rest.astype(F32)).astype(BF))
                    last.append(far)
                    far = swap(far, "view", 2)
                else:
                    far = new_waits.pop(0)
                    inputs_grad = (residual_grad + own + near.astype(F32) + far.astype(F32)).astype(BF)
                    last.append(inputs_grad)
                i_step += 1
            elif name == "L":
                got = new_waits.pop(0)
                if l_step == 0:
                    keep, send = halve(keep, got)
                    got_l = swap_by_core(send, SCENE[1])
                elif l_step == 1:
                    block = jnp.concatenate([small, rows[:6]], 0)
                    block = rounded(jnp.concatenate([block[:, : width // 2], block[:, width // 2 :]], 0))
                    extra = block.shape[0]
                    message = jnp.concatenate([keep + got, block], 0)
                    message = lax.optimization_barrier(whole_slice(message))
                    got_l = swap_by_core(message, SCENE[2])
                elif l_step == 2:
                    got = jnp.concatenate([turned(got[:-extra]), got[-extra:]], 0)
                    message = rounded(message.astype(F32) + got.astype(F32))
                    got_l = swap_by_core(message, LATE[0])
                elif l_step < 5:
                    message = grow(message, got)
                    got_l = swap_by_core(message, LATE[l_step - 2])
                    if l_step == 4:
                        near_keep = swap(message[:-extra], "view", 1)
                else:
                    got_l = got
                    near_got = swap(got, "view", 1)
                    small = rounded(message[-extra:].astype(F32) + got[-extra:].astype(F32))
                    other = swap(small, "view", 1)
                if l_step:
                    last.append(message if l_step < 5 else small)
                else:
                    last += [keep, send]
                l_step += 1
            elif name == "G":
                near, rest = swap(near, "view", 1), swap(rest, "view", 1)
    assert l_step == 6 and i_step == 2 and outcome is not None
    blocks = [b for n in "AB" for b in (parts[n].lower[1], parts[n].peer)]
    grad_squeezer, grad_expander, grad_combiner = feed_assemble(gate[0], 1, blocks, hid, feed_grads)
    near_got, other, grad_squeezer = after((near_got, other, grad_squeezer))
    vectors = [width] * 6 + [hid]
    grad_projector, table, *vectors = assemble(
        gate[0], [message, got_l, near_keep, near_got], [small, other], groups, vectors, width
    )
    grad_scaling, grad_shifting, grad_leveling, grad_baseline, grad_rescaling, grad_reshifting, grad_priming = vectors

    return (
        outcome.reshape(inputs.shape),
        inputs_grad.reshape(inputs.shape),
        table,
        grad_scaling,
        grad_shifting,
        grad_projector,
        grad_combiner,
        grad_baseline,
        grad_rescaling,
        grad_reshifting,
        grad_expander,
        grad_priming,
        grad_squeezer,
        grad_leveling,
    )


def solution(mesh):
    tokens = P("scene", "view", None, None)
    placed = (tokens, P("scene", "view", None)) + (P(),) * 12 + (tokens,)
    return jax.shard_map(
        on_device,
        mesh=mesh,
        in_specs=placed,
        out_specs=(tokens, tokens) + (P(),) * 12,
        check_vma=False,
    )
```

```python
import functools

import jax
import jax.numpy as jnp
from jax import lax
from jax.experimental import pallas as pl
from jax.experimental.pallas import tpu as pltpu
from jax.sharding import PartitionSpec as P

HEADS = 12
HEAD = 64
BF = jnp.bfloat16
F32 = jnp.float32
BOTH = ("scene", "view")
MINE = HEADS // 4 * HEAD
PAD = 256
MIB = 1 << 20


def swap(value, axis, mask):
    count = lax.axis_size(axis)
    return lax.ppermute(value, axis, [(i, i ^ mask) for i in range(count)])


def swap_by_core(value, masks):
    scenes, views = lax.axis_size("scene"), lax.axis_size("view")
    pairs = []
    for s in range(scenes):
        for v in range(views):
            ds, dv = masks[v % 2]
            pairs.append((s * views + v, (s ^ ds) * views + (v ^ dv)))
    return lax.ppermute(value, BOTH, pairs)


def side_of(masks, core):
    scene, view = lax.axis_index("scene"), lax.axis_index("view")
    bits = [((scene & ds) + (view & dv) > 0).astype(jnp.int32) for ds, dv in masks]
    return jnp.where(core == 0, bits[0], bits[1])


def code_of(stages, core):
    total = 0
    for masks in stages:
        total = 2 * total + side_of(masks, core)
    return total


X, Y, Z1, Z2 = (1, 0), (0, 2), (2, 0), (4, 0)
WIDE = ((X, Z1), (Y, X), (Z1, Y), (Z2, Z2))
THIN = ((Y, Y), (Z1, Z1), (X, X), (Z2, Z2))
SCENE = ((X, Z1), (Z1, X), (Z2, Z2))
LATE = ((Y, X), (Z1, Y), (X, Z1))


def rounded(value):
    return lax.optimization_barrier(lax.reduce_precision(value, 8, 7).astype(BF))


def whole_slice(value):
    bit = 8
    while bit < lax.axis_size("scene"):
        value = rounded(value.astype(F32) + swap(value, "scene", bit).astype(F32))
        bit *= 2
    return value


def by_view(blocks, me):
    a, b, c, d = blocks
    one = (me & 1) == 1
    a, b = jnp.where(one, b, a), jnp.where(one, a, b)
    c, d = jnp.where(one, d, c), jnp.where(one, c, d)
    two = (me & 2) == 2
    a, c = jnp.where(two, c, a), jnp.where(two, a, c)
    b, d = jnp.where(two, d, b), jnp.where(two, b, d)
    return a, b, c, d


def normalise(values):
    centre = values - jnp.mean(values, axis=-1, keepdims=True)
    rstd = lax.rsqrt(jnp.mean(centre * centre, axis=-1, keepdims=True) + 1e-05)
    return centre * rstd, rstd


def norm_back(grad, unit, rstd):
    return (
        grad
        - jnp.mean(grad, axis=-1, keepdims=True)
        - unit * jnp.mean(grad * unit, axis=-1, keepdims=True)
    ) * rstd


def dot(a, b):
    return jnp.dot(a, b, preferred_element_type=F32)


def tdot(a, b):
    return lax.dot_general(a, b, (((0,), (0,)), ((), ())), preferred_element_type=F32)


def dott(a, b):
    return lax.dot_general(a, b, (((1,), (1,)), ((), ())), preferred_element_type=F32)


def split3(values):
    high = values.astype(BF)
    rest = values - high.astype(F32)
    middle = rest.astype(BF)
    return high, middle, (rest - middle.astype(F32)).astype(BF)


def onehot_t(cameras, groups):
    rows = lax.broadcasted_iota(jnp.int32, (groups, cameras.shape[1]), 0)
    return (rows == cameras).astype(F32).astype(BF)


class Incoming:
    def __init__(self, source, buffer, sem, whole=None):
        self.copy, self.there = pltpu.make_async_copy(source, buffer, sem), False
        self.buffer = buffer if whole is None else whole
        self.copy.start()

    def __call__(self):
        if not self.there:
            self.copy.wait()
            self.there = True
        return self.buffer


class Present:
    def __init__(self, ref):
        self.buffer = ref

    def __call__(self):
        return self.buffer


class Outgoing:
    def __init__(self, target, buffer, sems, moves):
        self.target, self.ref, self.sems, self.moves = target, buffer, sems, moves

    def send(self, here=None, there=None):
        if self.ref is self.target:
            return
        source = self.ref if here is None else self.ref.at[here]
        target = self.target if there is None else self.target.at[there]
        move = pltpu.make_async_copy(source, target, self.sems.at[len(self.moves)])
        move.start()
        self.moves.append(move)


class Operand:
    def __init__(self, array, *, home=False, ready=False, cut=None, shape=None):
        self.array, self.ready, self.cut, self.apart = array, ready, cut, False
        if home:
            self.array = pltpu.with_memory_space_constraint(array, pltpu.HBM)
        self.shape = array.shape if shape is None else shape


def apart(array):
    operand = Operand(array)
    operand.apart = True
    return operand


def home(array, **more):
    return Operand(array, home=True, **more)


def ready(array):
    return Operand(array, ready=True)


def staged(body, args, outs, *, name, mib, us, scratch=(), code=None, held=(), buffers=None, early=None, near=()):
    buffers = buffers or {}
    args = [a if isinstance(a, Operand) else home(a) for a in args]
    n_code, n_in, n_held, n_out = int(code is not None), len(args), len(held), len(outs)
    loads = [i for i, a in enumerate(args) if not (a.ready or a.apart)]

    def kernel(*refs):
        code_ref = refs[0] if n_code else None
        refs = refs[n_code:]
        ins, refs = refs[:n_in], refs[n_in + n_held :]
        targets, refs = refs[:n_out], refs[n_out:]
        in_bufs, refs = refs[: len(loads)], refs[len(loads) :]
        out_bufs, refs = list(refs[: n_out - len(near)]), refs[n_out - len(near) :]
        for i in sorted(near):
            out_bufs.insert(i, targets[i])
        in_sems, out_sems, rest = refs[0], refs[1], refs[2:]
        arrivals = [Present(ref) for ref in ins]
        if early is not None:
            early(code_ref, ins, rest)
        for n, i in enumerate(loads):
            source = ins[i] if args[i].cut is None else ins[i].at[args[i].cut]
            arrivals[i] = Incoming(source, in_bufs[n], in_sems.at[n])
        moves = []
        leaving = [Outgoing(t, b, out_sems, moves) for t, b in zip(targets, out_bufs, strict=True)]
        body(code_ref, arrivals, leaving, *rest)
        for arrival in arrivals:
            arrival()
        for move in moves:
            move.wait()

    anywhere, vmem = pl.BlockSpec(memory_space=pl.ANY), pl.BlockSpec(memory_space=pltpu.VMEM)
    specs = [pl.BlockSpec(memory_space=pltpu.SMEM)] * n_code
    specs += [vmem if a.ready else anywhere for a in args] + [anywhere] * n_held
    operands = ([code] if n_code else []) + [a.array for a in args]
    operands += [pltpu.with_memory_space_constraint(a, pltpu.HBM) for a in held]
    bufs = [pltpu.VMEM(args[i].shape, args[i].array.dtype) for i in loads]
    return pl.pallas_call(
        kernel,
        in_specs=specs,
        out_specs=[vmem if i in near else anywhere for i in range(n_out)],
        out_shape=[(jax.ShapeDtypeStruct if i in near else pltpu.HBM)(*o) for i, o in enumerate(outs)],
        scratch_shapes=bufs
        + [pltpu.VMEM(buffers.get(i, o[0]), o[1]) for i, o in enumerate(outs) if i not in near]
        + [pltpu.SemaphoreType.DMA((max(len(loads), 1),)), pltpu.SemaphoreType.DMA((48,))]
        + list(scratch),
        input_output_aliases={n_code + n_in + i: i for i in range(n_held)},
        compiler_params=pltpu.CompilerParams(vmem_limit_bytes=mib * MIB),
        cost_estimate=pl.CostEstimate(flops=0, bytes_accessed=0, transcendentals=0),
        name=name,
    )(*operands)


def project_rows(tokens, cams, embedding, gain, shift, weight, outs, there, hold_ref, summed=None):
    normed, unit, rstd, *triple = outs
    rows = tokens[0].buffer.shape[0]
    pair = 2 * rows
    table = jnp.concatenate(split3(embedding()[...]), 0)
    hot = onehot_t(cams()[...], embedding().shape[0])
    hold_ref[...] = tdot(jnp.concatenate([hot] * 3, 0), table)
    for at, x in enumerate(tokens):
        here = slice(at * rows, (at + 1) * rows)
        values = x()[...].astype(F32) + hold_ref[here, :]
        if at == 0 and summed is not None:
            summed.ref[...] = values
            summed.send()
        values, scale = normalise(values)
        hold_ref[here, :] = values
        rstd.ref[here, :] = scale
    values = hold_ref[...]
    low = (values * gain()[...] + shift()[...]).astype(BF)
    normed.ref[...] = low
    lane = lax.broadcasted_iota(jnp.int32, (pair, PAD), 1)
    for i, (ref, first, out) in enumerate(triple):
        block = dot(low, weight()[:, i * PAD : (i + 1) * PAD])
        if i == 0:
            block = block * HEAD**-0.5
        if i == 2:
            block = jnp.where(lane < MINE, block, 1.0)
        ref[first : first + pair, :] = block.astype(BF)
        out.send((pl.ds(first, pair),), there)
    normed.send(None, there)
    unit.ref[...] = values.astype(BF)
    unit.send(None, there)
    rstd.send(None, there)


def project_outs(total, width):
    outs = [((total, width), BF), ((total, width), BF), ((total, 1), F32)]
    return outs + [((total, PAD), BF)] * 3


def project_body(_, ins, outs, hold_ref):
    xa, xb, cams, embedding, gain, shift, weight = ins
    there = (pl.ds(0, hold_ref.shape[0]),)
    triple = [(out.ref, 0, out) for out in outs[3:6]]
    project_rows((xa, xb), cams, embedding, gain, shift, weight, [*outs[:3], *triple], there, hold_ref, outs[6])


def project(xa, xb, cams, embedding, gain, shift, weight):
    rows, width = xa.shape[-2:]
    pair, total = 2 * rows, 4 * rows
    outs = project_outs(total, width)
    return staged(
        project_body,
        [xa, ready(xb), cams, embedding, gain, shift, weight],
        [*outs, ((rows, width), F32)],
        near=(6,),
        name="project",
        mib=32,
        us=5,
        scratch=[pltpu.VMEM((pair, width), F32)],
        buffers={i: (pair, o[0][1]) for i, o in enumerate(outs)},
    )


def blocks_of(total):
    return [(at, min(256, total - at)) for at in range(0, total, 256)]


TILE = 128


def tile_of(head):
    at = head * HEAD // TILE * TILE
    return slice(at, at + TILE)


def one_head(block, head):
    lane = lax.broadcasted_iota(jnp.int32, block.shape, 1) // HEAD
    return jnp.where(lane == head % (TILE // HEAD), block, jnp.zeros_like(block))


def attend_rows(q_ref, keys, values_of, outs, vt_ref, mt_ref):
    e, first, second, inv = outs
    pair, heads = q_ref.shape[0], e.ref.shape[0]
    work = [(h, at, size) for h in range(heads) for at, size in blocks_of(pair)]

    def scores(h, at, size):
        return dott(keys()[:, tile_of(h)], one_head(q_ref[at : at + size, tile_of(h)], h))

    keys(), values_of()
    ahead = scores(*work[0])
    vt_ref[...] = values_of()[...].astype(F32).T.astype(BF)
    mt_ref[...] = jnp.zeros_like(mt_ref)
    inv.ref[...] = jnp.zeros_like(inv.ref)
    for i, (h, at, size) in enumerate(work):
        here = ahead
        if i + 1 < len(work):
            ahead = scores(*work[i + 1])
        mine = slice(h * HEAD, (h + 1) * HEAD)
        expo = jnp.exp(here - jnp.max(here, 0, keepdims=True)).astype(BF)
        cut = (h, slice(None), slice(at, at + size))
        e.ref[cut] = expo
        if at + size == pair:
            e.send((h,), (h,))
        values = jnp.concatenate([vt_ref[mine, :], vt_ref[MINE : MINE + 16, :]], 0)
        out = dot(values, expo)
        inverse = 1.0 / out[HEAD : HEAD + 1, :]
        mt_ref[mine, at : at + size] = out[:HEAD, :] * inverse
        inv.ref[h : h + 1, at : at + size] = inverse
    mixed = mt_ref[...].T[:pair]
    first.ref[...] = mixed[: pair // 2, :MINE].astype(BF)
    first.send()
    second.ref[...] = mixed[pair // 2 :, :MINE].astype(BF)
    second.send()
    inv.send()


def attend_outs(total):
    pair, heads = total // 2, MINE // HEAD
    wide = -(-pair // 128) * 128
    part = ((pair // 2, MINE), BF)
    return [((heads, total, pair), BF), part, part, ((8, wide), F32)]


def attend_scratch(total):
    wide = -(-(total // 2) // 128) * 128
    return [pltpu.VMEM((PAD, total), BF), pltpu.VMEM((PAD, wide), F32)]


def attend_body(_, ins, outs, *scratch):
    q, k, v = ins
    attend_rows(q(), k, v, outs, *scratch)


def attend(q, k, v):
    total = k.shape[0]
    pair = total // 2
    return staged(
        attend_body,
        [home(q, cut=(pl.ds(0, pair),), shape=(pair, PAD)), ready(k), ready(v)],
        attend_outs(total),
        near=(1, 2),
        name="attend",
        mib=32,
        us=8,
        scratch=attend_scratch(total),
    )


def second_body(_, ins, outs, hold_ref, *scratch):
    xa, xb, cams, embedding, gain, shift, weight = ins
    pair = hold_ref.shape[0]
    keys_ref, values_ref = outs[10].ref, outs[11].ref
    sems, *scratch = scratch
    first = pl.ds(0, pair)
    k, v = (
        Incoming(out.target.at[first], ref.at[first], sems.at[i], ref)
        for i, (out, ref) in enumerate(((outs[4], keys_ref), (outs[5], values_ref)))
    )
    there = (pl.ds(pair, pair),)
    triple = [(outs[3].ref, 0, outs[3]), (k.buffer, pair, outs[4]), (v.buffer, pair, outs[5])]
    outs[4].ref, outs[5].ref = k.buffer, v.buffer
    project_rows((xa, xb), cams, embedding, gain, shift, weight, [*outs[:3], *triple], there, hold_ref)
    attend_rows(outs[3].ref, k, v, outs[6:10], *scratch)
    k()
    v()


def second_half(xa, xb, cams, embedding, gain, shift, weight, held):
    rows, width = xa.shape[-2:]
    pair, total = 2 * rows, 4 * rows
    outs = project_outs(total, width)
    buffers = {i: (pair, o[0][1]) for i, o in enumerate(outs)}
    buffers[4] = buffers[5] = (16, PAD)
    return staged(
        second_body,
        [xa, ready(xb), ready(cams), embedding, gain, shift, weight],
        [*outs, *attend_outs(total), ((total, PAD), BF), ((total, PAD), BF)],
        near=(7, 8, 10, 11),
        name="second_half",
        mib=44,
        us=10,
        scratch=[
            pltpu.VMEM((pair, width), F32),
            pltpu.SemaphoreType.DMA((2,)),
            *attend_scratch(total),
        ],
        held=held,
        buffers=buffers,
    )


def back_heads(heads, q_ref, v_ref, g_ref, kt_ref, delta_of, expos, dq_ref, dk_ref, dv_ref):
    pair = q_ref.shape[0] // 2
    work = [(h, i, at, size) for h in heads for i in range(2) for at, size in blocks_of(pair)]
    dq_ref[...] = jnp.zeros_like(dq_ref)

    def cut(ref, h, i, at, size):
        return one_head(ref[i * pair + at : i * pair + at + size, :], h)

    ahead_grad = cut(g_ref, *work[0])
    ahead = dott(v_ref[...], ahead_grad)
    for n, (h, i, at, size) in enumerate(work):
        if i == at == 0:
            expos[2 * heads.index(h)]()
            expos[2 * heads.index(h) + 1]()
        grad, prob_grad = ahead_grad, ahead
        if n + 1 < len(work):
            ahead_grad = cut(g_ref, *work[n + 1])
            ahead = dott(v_ref[...], ahead_grad)
        expo = expos[2 * heads.index(h) + i]()[:, at : at + size]
        score_grad = (expo.astype(F32) * (prob_grad - delta_of(h, i, at, size))).astype(BF)
        value_part = dot(expo, grad)
        key_part = dot(score_grad, cut(q_ref, h, i, at, size))
        if n:
            value_part += dv_ref[...]
            key_part += dk_ref[...]
        dv_ref[...] = value_part
        dk_ref[...] = key_part
        mine = slice(h * HEAD % TILE, h * HEAD % TILE + HEAD)
        dq_ref[i, mine, at : at + size] = dot(kt_ref[mine, :], score_grad)


def back_first_body(code, ins, outs, g_ref, kt_ref, dq_ref, dk_ref, dv_ref, hold_ref):
    grads, invs, mixes, (v, k, q), expos = ins[:4], ins[4:6], ins[6:10], ins[10:13], ins[13:]
    dq, dk, dv, g_rest, delta = outs
    total = q.buffer.shape[0]
    pair, rows = total // 2, grads[0].buffer.shape[0]
    for arrival in (*grads, *invs, *mixes):
        arrival()
    hold_ref[...] = jnp.zeros_like(hold_ref)
    for i, grad in enumerate(grads):
        hold_ref[i * rows : (i + 1) * rows, :MINE] = grad()[...].astype(F32)
    lane = lax.broadcasted_iota(jnp.int32, (8, PAD), 1) // HEAD
    pick = (lane == lax.broadcasted_iota(jnp.int32, (8, PAD), 0)).astype(F32).astype(BF)
    for i in range(2):
        here = slice(i * pair, (i + 1) * pair)
        inverse = invs[i]()[...].T[:pair, :]
        lane = lax.broadcasted_iota(jnp.int32, (pair, PAD), 1) // HEAD
        scale = jnp.zeros((pair, PAD), F32)
        for h in range(MINE // HEAD):
            scale = jnp.where(lane == h, inverse[:, h : h + 1], scale)
        scaled = (hold_ref[here, :] * scale).astype(BF)
        g_ref[here, :] = scaled[:, :TILE]
        g_rest.ref[here, :] = scaled[:, TILE:]
        for j in range(2):
            rows_here = slice(i * pair + j * rows, i * pair + (j + 1) * rows)
            hold_ref[rows_here, :MINE] = mixes[2 * i + j]()[...].astype(F32)
        prod = scaled.astype(F32) * hold_ref[here, :]
        high = prod.astype(BF)
        low = (prod - high.astype(F32)).astype(BF)
        delta.ref[8 * i : 8 * i + 8, :pair] = dott(pick, high) + dott(pick, low)
        delta.ref[8 * i : 8 * i + 8, pair:] = jnp.zeros((8, delta.ref.shape[1] - pair), F32)
    g_rest.send()
    delta.send()
    for arrival in (v, k, q, *expos[:2]):
        arrival()
    kt_ref[...] = k()[...].astype(F32).T.astype(BF)

    def delta_of(h, i, at, size):
        return delta.ref[8 * i + h : 8 * i + h + 1, at : at + size]

    back_heads((0, 1), q(), v(), g_ref, kt_ref, delta_of, expos, dq_ref, dk_ref, dv_ref)
    for i in range(2):
        dq.ref[i * pair : (i + 1) * pair, :] = (dq_ref[i].T[:pair] * HEAD**-0.5).astype(BF)
    dq.send()
    dk.ref[...] = dk_ref[...].astype(BF)
    dk.send()
    dv.ref[...] = dv_ref[...].astype(BF)
    dv.send()


def back_last_body(code, ins, outs, kt_ref, dq_ref, dk_ref, dv_ref, piece_ref):
    v, g, k, q, delta, *expos = ins[:7]
    dq0, dk0, dv0, normed = ins[7:]
    dqk, dv, keep, send = outs
    pair = q.buffer.shape[0] // 2
    for arrival in (v, g, k, q, delta):
        arrival()
    kt_ref[...] = k()[...].astype(F32).T.astype(BF)

    def delta_of(h, i, at, size):
        return delta()[8 * i + h : 8 * i + h + 1, at : at + size]

    back_heads((2,), q(), v(), g(), kt_ref, delta_of, expos, dq_ref, dk_ref, dv_ref)
    rest = MINE - TILE
    dqk.ref[:, :TILE] = dq0()[...]
    for i in range(2):
        dq = (dq_ref[i].T[:pair] * HEAD**-0.5).astype(BF)
        dqk.ref[i * pair : (i + 1) * pair, TILE:MINE] = dq[:, :rest]
    dqk.ref[:, MINE : MINE + TILE] = dk0()[...]
    dqk.ref[:, MINE + TILE :] = dk_ref[:, :rest].astype(BF)
    dv.ref[:, :TILE] = dv0()[...]
    dv.ref[:, TILE:] = dv_ref[:, :rest].astype(BF)
    weight_grad(code, normed, dqk.ref, dv.ref, keep, send, piece_ref)
    dqk.send()
    dv.send()


PIECES = 8


def weight_grad(code, normed, dqk_ref, dv_ref, keep, send, hold_ref):
    width = normed().shape[1]
    rows = width // PIECES
    piece = rows + rows // 2
    mine = code[0]
    qk = tdot(normed()[...], dqk_ref[...]).astype(BF)
    v = tdot(normed()[...], dv_ref[...]).astype(BF)
    for p in range(PIECES):
        at = pl.multiple_of((p ^ mine) * piece, 16)
        hold_ref[pl.ds(at, rows), :] = qk[p * rows : (p + 1) * rows]
        at = pl.multiple_of((p ^ mine) * piece + rows, 16)
        top = v[p * rows : p * rows + rows // 2]
        low = v[p * rows + rows // 2 : (p + 1) * rows]
        hold_ref[pl.ds(at, rows // 2), :] = jnp.concatenate([top, low], 1)
    half = PIECES * piece // 2
    send.ref[...] = hold_ref[half:, :]
    send.send()
    keep.ref[...] = hold_ref[:half, :]
    keep.send()


def back_scratch(total):
    wide = -(-(total // 2) // 128) * 128
    return [
        pltpu.VMEM((TILE, total), BF),
        pltpu.VMEM((2, TILE, wide), F32),
        pltpu.VMEM((total, TILE), F32),
        pltpu.VMEM((total, TILE), F32),
    ]


def tile_cut(array, tile):
    return home(array, cut=(slice(None), pl.ds(tile * TILE, TILE)), shape=(array.shape[0], TILE))


def back_first(q, k, v, e0, e1, grads, mixes, inv0, inv1):
    total = k.shape[0]
    pair = total // 2
    wide = -(-pair // 128) * 128
    args = [*map(ready, grads), inv0, inv1, *map(ready, mixes)] + [tile_cut(a, 0) for a in (v, k, q)]
    args += [home(e, cut=(h,), shape=(total, pair)) for h in range(2) for e in (e0, e1)]
    return staged(
        back_first_body,
        args,
        [((total, TILE), BF)] * 4 + [((16, wide), F32)],
        near=(0, 1, 2, 3, 4),
        name="back_first",
        mib=40,
        us=12,
        scratch=[pltpu.VMEM((total, TILE), BF), *back_scratch(total), pltpu.VMEM((total, PAD), F32)],
    )


def back_last(codes, q, k, v, e0, e1, first, normed):
    total, width = k.shape[0], normed.shape[1]
    pair = total // 2
    dq, dk, dv, g, delta = first
    piece = width // PIECES * 3 // 2
    half = ((PIECES * piece // 2, 2 * MINE), BF)
    args = [tile_cut(v, 1), ready(g), tile_cut(k, 1), tile_cut(q, 1), ready(delta)]
    args += [home(e, cut=(2,), shape=(total, pair)) for e in (e0, e1)]
    return staged(
        back_last_body,
        [*args, *map(ready, (dq, dk, dv)), normed],
        [((total, 2 * MINE), BF), ((total, MINE), BF), half, half],
        near=(0, 1, 2, 3),
        name="back_last",
        mib=40,
        us=10,
        scratch=[*back_scratch(total), pltpu.VMEM((PIECES * piece, 2 * MINE), BF)],
        code=codes,
    )


STEP = 512


def feed_forward_body(code, ins, outs):
    summed, own, near, far, rest, combiner, baseline, gain, shift, expander, priming, squeezer, tangent = ins
    residual, own_wide, wide, own_slim, slim = outs
    me = code[2]
    first = code[3] == 0
    total = summed()[...] + baseline()[...]
    for r, block in ((2, far), (3, rest), (0, own), (1, near)):
        at = pl.multiple_of((me ^ r) * MINE, 16)
        total += dot(block()[...], combiner()[pl.ds(at, MINE), :])
    residual.ref[...] = total
    residual.send()
    unit, _ = normalise(total)
    low = (unit * gain()[...] + shift()[...]).astype(BF)
    own_slim.ref[...] = jnp.where(first, tangent()[...], low)
    own_slim.send()
    slim.ref[...] = jnp.where(first, low, tangent()[...])
    slim.send()
    for at in range(0, expander().shape[1], STEP):
        cut = slice(at, at + STEP)
        hidden = dot(low, expander()[:, cut]) + priming()[cut]
        back = dott(tangent()[...], squeezer()[cut, :])
        phi = 0.5 * (1.0 + lax.erf(hidden * (2.0**-0.5)))
        density = jnp.exp(-0.5 * hidden * hidden) * 0.3989422804014327
        active = (hidden * phi).astype(BF)
        grad = (back * (phi + hidden * density)).astype(BF)
        own_wide.ref[:, cut] = jnp.where(first, active, grad)
        wide.ref[:, cut] = jnp.where(first, grad, active)
        part = (slice(None), pl.ds(at, STEP))
        own_wide.send(part, part)
        wide.send(part, part)


def feed_forward(codes, summed, own, near, far, rest, combiner, baseline, gain, shift, expander, priming, squeezer, tangent):
    rows, width = summed.shape
    hid = expander.shape[1]
    weights = [combiner, baseline, gain, shift, expander, priming, squeezer, tangent]
    return staged(
        feed_forward_body,
        [*map(ready, (summed, own, near, far, rest)), *weights],
        [((rows, width), F32), ((rows, hid), BF), ((rows, hid), BF), ((rows, width), BF), ((rows, width), BF)],
        near=(0, 1, 2, 3, 4),
        name="feed_forward",
        mib=24,
        us=6,
        code=codes,
    )


def feed_back_body(code, ins, outs, grad_ref, sem):
    expander, residual, gain, tangent, combiner, own_wide, wide = ins
    residual_grad, low, *grads, rows = outs
    me = code[2]
    pltpu.make_async_copy(wide(), grad_ref, sem.at[0]).wait()
    second_grad = dott(grad_ref[...], expander()[...])
    unit, rstd = normalise(residual()[...])
    slope = tangent()[...].astype(F32)
    total = slope + norm_back(second_grad * gain()[...], unit, rstd)
    low.ref[...] = total.astype(BF)
    low.send()
    for r in (2, 3, 1, 0):
        at = pl.multiple_of((me ^ r) * MINE, 16)
        grads[r].ref[...] = dott(low.ref[...], combiner()[pl.ds(at, MINE), :]).astype(BF)
        grads[r].send()
    residual_grad.ref[...] = total
    residual_grad.send()
    width = total.shape[1]
    rows.ref[0:1, :] = jnp.sum(slope, 0, keepdims=True)
    rows.ref[1:2, :] = jnp.sum(low.ref[...].astype(F32), 0, keepdims=True)
    rows.ref[2:3, :] = jnp.sum(second_grad * unit, 0, keepdims=True)
    rows.ref[3:4, :] = jnp.sum(second_grad, 0, keepdims=True)
    for j in range(grad_ref.shape[1] // width):
        block = grad_ref[:, j * width : (j + 1) * width].astype(F32)
        rows.ref[4 + j : 5 + j, :] = jnp.sum(block, 0, keepdims=True)
    rows.ref[6:8, :] = jnp.zeros((2, width), F32)
    rows.send()


def pick_wide(on_zero, on_one):
    def early(code, operands, scratch):
        for core, place in enumerate((on_zero, on_one)):

            @pl.when(code[3] == core)
            def _():
                pltpu.make_async_copy(operands[place], scratch[0], scratch[1].at[0]).start()

    return early


def feed_back(codes, residual, own_wide, wide, tangent, expander, gain, combiner):
    rows, width = residual.shape
    return staged(
        feed_back_body,
        [expander, ready(residual), gain, tangent, combiner, apart(own_wide), apart(wide)],
        [((rows, width), F32), ((rows, width), BF)] + [((rows, MINE), BF)] * 4 + [((8, width), F32)],
        early=pick_wide(6, 5),
        near=(1, 2, 3, 4, 5),
        name="feed_back",
        mib=24,
        us=6,
        scratch=[pltpu.VMEM(wide.shape, BF), pltpu.SemaphoreType.DMA((1,))],
        code=codes,
    )


def outcome_body(code, ins, outs, active_ref, sem):
    squeezer, residual, leveling, own_wide, wide = ins
    pltpu.make_async_copy(wide(), active_ref, sem.at[0]).wait()
    outs[0].ref[...] = (residual()[...] + dot(active_ref[...], squeezer()[...]) + leveling()[...]).astype(BF)
    outs[0].send()


def outcome_of(codes, residual, own_wide, wide, squeezer, leveling):
    rows, width = residual.shape
    return staged(
        outcome_body,
        [squeezer, home(residual), leveling, apart(own_wide), apart(wide)],
        [((rows, width), BF)],
        early=pick_wide(3, 4),
        name="outcome",
        mib=16,
        us=4,
        scratch=[pltpu.VMEM(wide.shape, BF), pltpu.SemaphoreType.DMA((1,))],
        code=codes,
    )[0]


PARTS = 16


def place(code, piece, size):
    return pl.multiple_of((piece ^ code) * size, 8)


def segments(first, rows, low, size):
    out, at = [], first
    while at < first + rows:
        piece, offset = divmod(at - low, size)
        count = min(size - offset, first + rows - at)
        out.append((piece, offset, at - first, count))
        at += count
    return out


def spread(hold_ref, block, first, low, size, code):
    for piece, offset, start, count in segments(first, block.shape[0], low, size):
        at = pl.multiple_of(place(code, piece, size) + offset, 8)
        hold_ref[pl.ds(at, count), :] = block[start : start + count]


def feed_grad_body(sizes, code, ins, outs, tokens_ref, sems, *holds):
    own_wide, own_slim, wide, slim, own, far, near, rest, resid, other = ins
    hid, width = own_wide().shape[1], own_slim().shape[1]
    assert hid == 2 * width
    bulk = PARTS * sizes[0]
    rows = own_slim().shape[0]
    room = tokens_ref.shape[1] // 2
    gap = rows // 16 * 16
    loads = []
    for n, (big, small) in enumerate(((own_wide, own_slim), (wide, slim))):
        first = n * room
        for j in range(3):
            tokens_ref[j, first + gap : first + room, :] = jnp.zeros((room - gap, width), BF)
    for n, (big, small) in enumerate(((own_wide, own_slim), (wide, slim))):
        there = pl.ds(n * room, rows)
        for j in range(hid // width):
            source = big().at[:, pl.ds(j * width, width)]
            loads.append(pltpu.make_async_copy(source, tokens_ref.at[j, there], sems.at[3 * n + j]))
        loads.append(pltpu.make_async_copy(small(), tokens_ref.at[2, there], sems.at[3 * n + 2]))
    for load in loads:
        load.start()
    for load in loads:
        load.wait()

    def put(block, row):
        for part, low, high in ((0, 0, bulk), (1, bulk, bulk + PARTS * sizes[1])):
            first, last = max(row, low), min(row + block.shape[0], high)
            if first < last:
                spread(holds[part], block[first - row : last - row], first, low, sizes[part], code[4 + 2 * part])

    for j in range(hid // width):
        left = jnp.where(code[3] == 0, j, 2)
        right = jnp.where(code[3] == 0, 2, j)
        block = tdot(tokens_ref[left], tokens_ref[right])
        put(block, j * width)

    upper = code[2] < 2
    for i in range(2):
        here = jnp.where(upper, (own, far)[i]()[...], (far, own)[i]()[...])
        peer = jnp.where(upper, (near, rest)[i]()[...], (rest, near)[i]()[...])
        put(tdot(here, resid()[...]) + tdot(peer, other()[...]), hid + i * MINE)
    for part, hold_ref in enumerate(holds):
        keep, send = outs[2 * part : 2 * part + 2]
        half = hold_ref.shape[0] // 2
        send.ref[...] = hold_ref[half:, :].astype(BF)
        send.send()
        keep.ref[...] = hold_ref[:half, :].astype(BF)
        keep.send()


def feed_grad(codes, sizes, feed, mixed):
    rows, width = feed[1].shape
    halves = [((PARTS * size // 2, width), BF) for size in sizes]
    return staged(
        functools.partial(feed_grad_body, sizes),
        [apart(feed[0]), apart(feed[1]), *map(ready, feed[2:]), *map(ready, mixed)],
        [halves[0], halves[0], halves[1], halves[1]],
        near=(0, 1, 2, 3),
        name="feed_grad",
        mib=40,
        us=7,
        scratch=[
            pltpu.VMEM((3, 2 * (-(-rows // 16) * 16), width), BF),
            pltpu.SemaphoreType.DMA((6,)),
            *[pltpu.VMEM((PARTS * size, width), F32) for size in sizes],
        ],
        code=codes,
    )


def feed_assemble_body(side, sizes, code, ins, outs, sems, *holds):
    squeezer, expander, combiner = (out.target for out in outs)
    hid, width = squeezer.shape

    def targets(core, row, count):
        out = []
        while count:
            if row < hid and core == 0:
                take = min(count, hid - row)
                out.append((squeezer.at[pl.ds(row, take), :], take))
            elif row < hid:
                j = row // width
                take = min(count, (j + 1) * width - row)
                cut = pl.ds(row - j * width, take), pl.ds(j * width, width)
                out.append((expander.at[cut], take))
            else:
                view, at = divmod(row - hid, MINE)
                take = min(count, MINE - at)
                out.append((combiner.at[pl.ds((core + 2 * view) * MINE + at, take), :], take))
            row, count = row + take, count - take
        return out

    for i, hold_ref in enumerate(holds):
        half = hold_ref.shape[0] // 2
        hold_ref[:half, :] = ins[2 * i]()[...].astype(F32)
        hold_ref[half:, :] = ins[2 * i + 1]()[...].astype(F32)
    for core in range(2):

        @pl.when(code[3] == core ^ side)
        def _():
            moves, low = [], 0
            for part, size in enumerate(sizes):
                for piece in range(PARTS):
                    start = pl.multiple_of((piece ^ code[4 + 2 * part + side]) * size, 8)
                    at = 0
                    for target, count in targets(core, low + piece * size, size):
                        source = holds[part].at[pl.ds(pl.multiple_of(start + at, 8), count), :]
                        moves.append(pltpu.make_async_copy(source, target, sems.at[len(moves)]))
                        moves[-1].start()
                        at += count
                low += PARTS * size
            for move in moves:
                move.wait()


def feed_assemble(codes, side, blocks, hid, held=()):
    width = blocks[0].shape[1]
    sizes = [blocks[0].shape[0] // 8, blocks[2].shape[0] // 8]
    return staged(
        functools.partial(feed_assemble_body, side, sizes),
        [ready(b) for b in blocks],
        [((hid, width), F32), ((width, hid), F32), ((width, width), F32)],
        name="feed_assemble",
        mib=24,
        us=5,
        scratch=[pltpu.SemaphoreType.DMA((48,))] + [pltpu.VMEM((PARTS * n, width), F32) for n in sizes],
        code=codes,
        held=held,
        buffers={0: (8, 128), 1: (8, 128), 2: (8, 128)},
    )


def input_grad_body(_, ins, outs, hold_ref):
    dqk, dv, weight, unit, rstd, gain, *rest = ins
    near_cams, far_cams, resid = rest
    small = outs[4]
    patches = resid.buffer.shape[0]
    groups = small.ref.shape[0] - 2
    slope = dott(dqk()[:, :MINE], weight()[:, :MINE]) + dott(dqk()[:, MINE:], weight()[:, PAD : PAD + MINE])
    slope += dott(dv()[...], weight()[:, 2 * PAD : 2 * PAD + MINE])
    values = unit()[...].astype(F32)
    small.ref[groups : groups + 1, :] = jnp.sum(slope * values, 0, keepdims=True)
    small.ref[groups + 1 : groups + 2, :] = jnp.sum(slope, 0, keepdims=True)
    hold_ref[...] = norm_back(slope * gain()[...], values, rstd()[...])
    for r in (1, 3, 0, 2):
        part = hold_ref[r * patches : (r + 1) * patches, :]
        outs[r].ref[...] = part.astype(outs[r].ref.dtype)
        outs[r].send()
    hold_ref[:patches, :] = hold_ref[:patches, :] + resid()[...]
    table = jnp.zeros((groups, slope.shape[1]), F32)
    for i, cams in enumerate((near_cams, far_cams)):
        part = hold_ref[2 * i * patches : 2 * (i + 1) * patches, :]
        hot = onehot_t(cams()[...], groups)
        for piece in split3(part)[:2]:
            table += dot(hot, piece)
    small.ref[:groups, :] = table
    small.send()


def input_grad(dqk, dv, weight, unit, rstd, gain, cams, resid, groups):
    total, width = unit.shape
    patches = resid.shape[0]
    low, full = ((patches, width), BF), ((patches, width), F32)
    return staged(
        input_grad_body,
        [ready(dqk), ready(dv), home(weight), home(unit), home(rstd), gain, *cams, home(resid)],
        [full, low, full, low, ((groups + 2, width), F32)],
        near=(1, 3),
        name="input_grad",
        mib=48,
        us=9,
        scratch=[pltpu.VMEM((total, width), F32)],
    )


def assemble_body(code, ins, outs):
    out, table, *vectors = outs
    rows, width = out.ref.shape[0] // PIECES, out.ref.shape[1] // 3
    piece = rows * 3 // 2
    blocks = [arrival() for arrival in ins[:4]]
    for p in range(PIECES):
        cut = []
        for i, which in enumerate((0, 1, 0, 1)):
            r = (p ^ code[which]) % 4
            core = code[3] if which == 0 else 1 - code[3]
            far = i // 2
            middle = jnp.where(core == 0, r // 2 * 2 + far, far * 2 + r // 2)
            at = pl.multiple_of((middle * 2 + r % 2) * piece, 16)
            upper = (p ^ code[which]) >= PIECES // 2
            lower_block = blocks[2 * which][pl.ds(at, piece), :]
            upper_block = blocks[2 * which + 1][pl.ds(at, piece), :]
            cut.append(jnp.where(upper, upper_block, lower_block).astype(F32))
        low = p * rows
        for v, block in enumerate(by_view(cut, code[2])):
            at = v * MINE
            out.ref[low : low + rows, at : at + MINE] = block[:rows, :MINE]
            out.ref[low : low + rows, width + at : width + at + MINE] = block[:rows, MINE:]
            at += 2 * width
            out.ref[low : low + rows // 2, at : at + MINE] = block[rows:, :MINE]
            out.ref[low + rows // 2 : low + rows, at : at + MINE] = block[rows:, MINE:]
        out.send((pl.ds(low, rows),), (pl.ds(low, rows),))
    total = ins[4]()[...].astype(F32) + ins[5]()[...].astype(F32)
    count, half, groups = total.shape[0] // 2, width // 2, table.ref.shape[0]
    table.ref[:, :half] = total[:groups, :]
    table.ref[:, half:] = total[count : count + groups, :]
    table.send()
    row = groups
    for vector in vectors:
        for at in range(0, vector.ref.shape[0], width):
            vector.ref[at : at + half] = total[row, :]
            vector.ref[at + half : at + width] = total[count + row, :]
            row += 1
        vector.send()


def assemble(codes, blocks, smalls, groups, sizes, width):
    return staged(
        assemble_body,
        [ready(b) for b in (*blocks, *smalls)],
        [((width, 3 * width), F32), ((groups, width), F32)] + [((size,), F32) for size in sizes],
        name="assemble",
        mib=24,
        us=5,
        code=codes,
    )


def turned(block):
    half = block.shape[0] // 2
    return jnp.concatenate([block[half:], block[:half]], 0)


def after(values, *others):
    out = lax.optimization_barrier((*values, *others))
    return out[: len(values)]


def halve(keep, got):
    cut = keep.shape[0] // 2
    return keep[:cut] + got[:cut], keep[cut:] + got[cut:]


class Part:
    def __init__(self, keep, got, stages):
        self.value, self.got, self.stages, self.step, self.lower, self.peer = keep, got, stages, 0, None, None

    def begin(self):
        self.value, send = halve(self.value, self.got)
        self.got = swap_by_core(send, self.stages[2])

    def advance(self, got):
        self.step += 1
        if self.step == 1:
            self.value = lax.optimization_barrier(whole_slice(self.value + got))
            self.got = swap_by_core(self.value, self.stages[3])
        elif self.step == 2:
            self.value = lax.optimization_barrier(self.value + turned(got))
            self.got = swap_by_core(self.value, self.stages[2])
        elif self.step == 3:
            self.value = jnp.concatenate([self.value, got], 0)
            self.got = swap_by_core(self.value, self.stages[1])
        elif self.step == 4:
            self.value = jnp.concatenate([self.value, got], 0)
            self.got, peer = swap_by_core(self.value, self.stages[0]), swap(self.value, "view", 1)
            self.lower = (self.value, peer)
        else:
            self.got, self.peer = got, swap(got, "view", 1)
            return []
        return [self.value]


PLAN = ("LAB", "LAG", "BI", "AO", "B", "L", "AI", "L", "B", "Lp", "AB", "P", "Lkq")


def on_device(
    inputs,
    cameras,
    embedding,
    scaling,
    shifting,
    projector,
    combiner,
    baseline,
    rescaling,
    reshifting,
    expander,
    priming,
    squeezer,
    leveling,
    cotangent,
):
    me = lax.axis_index("view")
    core = me % 2
    patches, width = inputs.shape[2], inputs.shape[3]
    groups, hid = embedding.shape[0], expander.shape[1]
    codes = [code_of(SCENE, core), code_of(SCENE, 1 - core), me, core]
    codes += [code_of(WIDE, core), code_of(WIDE, 1 - core), code_of(THIN, core), code_of(THIN, core)]
    codes = jnp.stack(codes).astype(jnp.int32)
    tangent = cotangent.reshape(patches, width)
    x0 = inputs.reshape(patches, width)
    c0 = cameras.reshape(1, patches)
    x2 = swap(x0, "view", 2)
    x1, c1 = swap(x0, "view", 1), swap(c0, "view", 1)
    near_cams = jnp.concatenate([c0, c1], 1)
    far_cams = swap(near_cams, "view", 2)
    hole = jnp.zeros((width, PAD - MINE), BF)
    padded = []
    for part in range(3):
        padded += [lax.dynamic_slice_in_dim(projector, part * width + me * MINE, MINE, 1), hole]
    padded = jnp.concatenate(padded, 1)
    *held, summed = project(x0, x1, near_cams, embedding, scaling, shifting, padded)
    x2, far_cams = after((x2, far_cams), *held)
    x3 = swap(x2, "view", 1)
    normed, unit1, rstd1, q, k, v, e1, far, rest, inv1, near_k, near_v = second_half(
        x2, x3, far_cams, embedding, scaling, shifting, padded, held
    )
    mine_far, mine_rest = far, rest
    far, rest = swap(far, "view", 2), swap(rest, "view", 3)
    e0, own, near, inv0 = attend(q, near_k, near_v)
    mixes = [own, near, mine_far, mine_rest]
    near, own, far, rest = after((near, own, far, rest))
    near, peer_rest = swap(near, "view", 1), swap(rest, "view", 1)

    residual, own_wide, wide, own_slim, slim = feed_forward(
        codes, summed, own, near, far, rest, combiner, baseline, rescaling, reshifting, expander, priming,
        squeezer, tangent,
    )
    peer_near = swap(near, "view", 1)
    peer_wide, peer_slim = swap(wide, "view", 1), swap(slim, "view", 1)
    residual_grad, resid_low, *grads, rows = feed_back(
        codes, residual, own_wide, wide, tangent, expander, rescaling, combiner
    )
    peer_near, peer_rest, resid_low, *grads = after((peer_near, peer_rest, resid_low, *grads))
    grads = [grads[0]] + [swap(grads[r], "view", r) for r in (1, 2, 3)]
    other = swap(resid_low, "view", 1)
    sizes = [(hid + width // 2) // 24, (hid + width // 2) // 48]
    keep0, send0, keep1, send1 = feed_grad(
        codes, sizes, [own_wide, own_slim, peer_wide, peer_slim],
        [own, far, peer_near, peer_rest, resid_low, other],
    )
    *grads, keep0, send0, keep1, send1 = after((*grads, keep0, send0, keep1, send1))
    got0, got1 = swap_by_core(send0, WIDE[0]), swap_by_core(send1, THIN[0])
    first = back_first(q, k, v, e0, e1, grads, mixes, inv0, inv1)
    got0, got1, *first = after((got0, got1, *first))
    keep0, send0 = halve(keep0, got0)
    keep1, send1 = halve(keep1, got1)
    got0, got1 = swap_by_core(send0, WIDE[1]), swap_by_core(send1, THIN[1])
    dqk, dv, keep, send = back_last(codes, q, k, v, e0, e1, first, normed)
    got0, got1, dqk, dv, keep, send = after((got0, got1, dqk, dv, keep, send))
    wide_part = Part(keep0, got0, WIDE)
    thin_part = Part(keep1, got1, THIN)
    got_l = swap_by_core(send, SCENE[0])
    wide_part.begin()
    thin_part.begin()
    parts = dict(A=wide_part, B=thin_part)
    l_step, i_step = 0, 0
    message = near_keep = near_got = other = small = None
    outcome = inputs_grad = feed_grads = None
    last = []
    gate = [codes, dqk]
    extra = 0

    def grow(message, got):
        small = rounded(message[-extra:].astype(F32) + got[-extra:].astype(F32))
        return jnp.concatenate([message[:-extra], got[:-extra], small], 0)

    for group in PLAN:
        tied = []
        if "O" in group:
            outcome = outcome_of(gate[0], residual, own_wide, wide, squeezer, leveling)
            tied.append(outcome)
        if "G" in group:
            own, near, far, rest, small = input_grad(
                gate.pop(), dv, padded, unit1, rstd1, scaling, (near_cams, far_cams), residual_grad, groups
            )
            tied += [near, rest, small]
        if "P" in group:
            blocks = [b for n in "AB" for b in (parts[n].lower[0], parts[n].got)]
            feed_grads = feed_assemble(gate[0], 0, blocks, hid)
            tied += feed_grads
        waits = []
        for name in group:
            if name in "AB":
                waits.append(parts[name].got)
            elif name == "L":
                waits.append(got_l)
            elif name == "I":
                waits += [near, rest] if i_step == 0 else [far]
            elif name == "p":
                waits += [parts["A"].lower[1], parts["B"].lower[1]]
            elif name == "k":
                waits.append(near_keep)
            elif name == "q":
                waits += [parts[n].peer for n in "AB"]
        bundle = list(after((*waits, *tied, *last, *gate)))
        new_waits, rest_of = bundle[: len(waits)], bundle[len(waits) :]
        new_tied, gate = rest_of[: len(tied)], rest_of[len(rest_of) - len(gate) :]
        if "O" in group:
            outcome = new_tied.pop(0)
        if "G" in group:
            near, rest, small = new_tied[:3]
            new_tied = new_tied[3:]
        if "P" in group:
            feed_grads = new_tied
        last = []
        for name in group:
            if name in "AB":
                last += parts[name].advance(new_waits.pop(0))
            elif name == "p":
                for n in "AB":
                    parts[n].lower = (parts[n].lower[0], new_waits.pop(0))
            elif name == "k":
                near_keep = new_waits.pop(0)
            elif name == "q":
                for n in "AB":
                    parts[n].peer = new_waits.pop(0)
            elif name == "I":
                if i_step == 0:
                    near, rest = new_waits.pop(0), new_waits.pop(0)
                    far = lax.optimization_barrier((far + rest.astype(F32)).astype(BF))
                    last.append(far)
                    far = swap(far, "view", 2)
                else:
                    far = new_waits.pop(0)
                    inputs_grad = (residual_grad + own + near.astype(F32) + far.astype(F32)).astype(BF)
                    last.append(inputs_grad)
                i_step += 1
            elif name == "L":
                got = new_waits.pop(0)
                if l_step == 0:
                    keep, send = halve(keep, got)
                    got_l = swap_by_core(send, SCENE[1])
                elif l_step == 1:
                    block = jnp.concatenate([small, rows[:6]], 0)
                    block = rounded(jnp.concatenate([block[:, : width // 2], block[:, width // 2 :]], 0))
                    extra = block.shape[0]
                    message = jnp.concatenate([keep + got, block], 0)
                    message = lax.optimization_barrier(whole_slice(message))
                    got_l = swap_by_core(message, SCENE[2])
                elif l_step == 2:
                    got = jnp.concatenate([turned(got[:-extra]), got[-extra:]], 0)
                    message = rounded(message.astype(F32) + got.astype(F32))
                    got_l = swap_by_core(message, LATE[0])
                elif l_step < 5:
                    message = grow(message, got)
                    got_l = swap_by_core(message, LATE[l_step - 2])
                    if l_step == 4:
                        near_keep = swap(message[:-extra], "view", 1)
                else:
                    got_l = got
                    near_got = swap(got, "view", 1)
                    small = rounded(message[-extra:].astype(F32) + got[-extra:].astype(F32))
                    other = swap(small, "view", 1)
                if l_step:
                    last.append(message if l_step < 5 else small)
                else:
                    last += [keep, send]
                l_step += 1
            elif name == "G":
                near, rest = swap(near, "view", 1), swap(rest, "view", 1)
    assert l_step == 6 and i_step == 2 and outcome is not None
    blocks = [b for n in "AB" for b in (parts[n].lower[1], parts[n].peer)]
    grad_squeezer, grad_expander, grad_combiner = feed_assemble(gate[0], 1, blocks, hid, feed_grads)
    near_got, other, grad_squeezer = after((near_got, other, grad_squeezer))
    vectors = [width] * 6 + [hid]
    grad_projector, table, *vectors = assemble(
        gate[0], [message, got_l, near_keep, near_got], [small, other], groups, vectors, width
    )
    grad_scaling, grad_shifting, grad_leveling, grad_baseline, grad_rescaling, grad_reshifting, grad_priming = vectors

    return (
        outcome.reshape(inputs.shape),
        inputs_grad.reshape(inputs.shape),
        table,
        grad_scaling,
        grad_shifting,
        grad_projector,
        grad_combiner,
        grad_baseline,
        grad_rescaling,
        grad_reshifting,
        grad_expander,
        grad_priming,
        grad_squeezer,
        grad_leveling,
    )


def solution(mesh):
    tokens = P("scene", "view", None, None)
    placed = (tokens, P("scene", "view", None)) + (P(),) * 12 + (tokens,)
    return jax.shard_map(
        on_device,
        mesh=mesh,
        in_specs=placed,
        out_specs=(tokens, tokens) + (P(),) * 12,
        check_vma=False,
    )
```

```python
import functools

import jax
import jax.numpy as jnp
from jax import lax
from jax.experimental import pallas as pl
from jax.experimental.pallas import tpu as pltpu
from jax.sharding import PartitionSpec as P

HEADS = 12
HEAD = 64
BF = jnp.bfloat16
F32 = jnp.float32
BOTH = ("scene", "view")
MINE = HEADS // 4 * HEAD
PAD = 256
MIB = 1 << 20


def swap(value, axis, mask):
    count = lax.axis_size(axis)
    return lax.ppermute(value, axis, [(i, i ^ mask) for i in range(count)])


def swap_by_core(value, masks):
    scenes, views = lax.axis_size("scene"), lax.axis_size("view")
    pairs = []
    for s in range(scenes):
        for v in range(views):
            ds, dv = masks[v % 2]
            pairs.append((s * views + v, (s ^ ds) * views + (v ^ dv)))
    return lax.ppermute(value, BOTH, pairs)


def side_of(masks, core):
    scene, view = lax.axis_index("scene"), lax.axis_index("view")
    bits = [((scene & ds) + (view & dv) > 0).astype(jnp.int32) for ds, dv in masks]
    return jnp.where(core == 0, bits[0], bits[1])


def code_of(stages, core):
    total = 0
    for masks in stages:
        total = 2 * total + side_of(masks, core)
    return total


X, Y, Z1, Z2 = (1, 0), (0, 2), (2, 0), (4, 0)
WIDE = ((X, Z1), (Y, X), (Z1, Y), (Z2, Z2))
THIN = ((Y, Y), (Z1, Z1), (X, X), (Z2, Z2))
SCENE = ((X, Z1), (Z1, X), (Z2, Z2))
LATE = ((Y, X), (Z1, Y), (X, Z1))


def rounded(value):
    return lax.optimization_barrier(lax.reduce_precision(value, 8, 7).astype(BF))


def whole_slice(value):
    bit = 8
    while bit < lax.axis_size("scene"):
        value = rounded(value.astype(F32) + swap(value, "scene", bit).astype(F32))
        bit *= 2
    return value


def by_view(blocks, me):
    a, b, c, d = blocks
    one = (me & 1) == 1
    a, b = jnp.where(one, b, a), jnp.where(one, a, b)
    c, d = jnp.where(one, d, c), jnp.where(one, c, d)
    two = (me & 2) == 2
    a, c = jnp.where(two, c, a), jnp.where(two, a, c)
    b, d = jnp.where(two, d, b), jnp.where(two, b, d)
    return a, b, c, d


def normalise(values):
    centre = values - jnp.mean(values, axis=-1, keepdims=True)
    rstd = lax.rsqrt(jnp.mean(centre * centre, axis=-1, keepdims=True) + 1e-05)
    return centre * rstd, rstd


def norm_back(grad, unit, rstd):
    return (
        grad
        - jnp.mean(grad, axis=-1, keepdims=True)
        - unit * jnp.mean(grad * unit, axis=-1, keepdims=True)
    ) * rstd


def dot(a, b):
    return jnp.dot(a, b, preferred_element_type=F32)


def tdot(a, b):
    return lax.dot_general(a, b, (((0,), (0,)), ((), ())), preferred_element_type=F32)


def dott(a, b):
    return lax.dot_general(a, b, (((1,), (1,)), ((), ())), preferred_element_type=F32)


def split3(values):
    high = values.astype(BF)
    rest = values - high.astype(F32)
    middle = rest.astype(BF)
    return high, middle, (rest - middle.astype(F32)).astype(BF)


def onehot_t(cameras, groups):
    rows = lax.broadcasted_iota(jnp.int32, (groups, cameras.shape[1]), 0)
    return (rows == cameras).astype(F32).astype(BF)


class Incoming:
    def __init__(self, source, buffer, sem, whole=None):
        self.copy, self.there = pltpu.make_async_copy(source, buffer, sem), False
        self.buffer = buffer if whole is None else whole
        self.copy.start()

    def __call__(self):
        if not self.there:
            self.copy.wait()
            self.there = True
        return self.buffer


class Present:
    def __init__(self, ref):
        self.buffer = ref

    def __call__(self):
        return self.buffer


class Outgoing:
    def __init__(self, target, buffer, sems, moves):
        self.target, self.ref, self.sems, self.moves = target, buffer, sems, moves

    def send(self, here=None, there=None):
        if self.ref is self.target:
            return
        source = self.ref if here is None else self.ref.at[here]
        target = self.target if there is None else self.target.at[there]
        move = pltpu.make_async_copy(source, target, self.sems.at[len(self.moves)])
        move.start()
        self.moves.append(move)


class Operand:
    def __init__(self, array, *, home=False, ready=False, cut=None, shape=None):
        self.array, self.ready, self.cut, self.apart = array, ready, cut, False
        if home:
            self.array = pltpu.with_memory_space_constraint(array, pltpu.HBM)
        self.shape = array.shape if shape is None else shape


def apart(array):
    operand = Operand(array)
    operand.apart = True
    return operand


def home(array, **more):
    return Operand(array, home=True, **more)


def ready(array):
    return Operand(array, ready=True)


def staged(body, args, outs, *, name, mib, us, scratch=(), code=None, held=(), buffers=None, early=None, near=()):
    buffers = buffers or {}
    args = [a if isinstance(a, Operand) else home(a) for a in args]
    n_code, n_in, n_held, n_out = int(code is not None), len(args), len(held), len(outs)
    loads = [i for i, a in enumerate(args) if not (a.ready or a.apart)]

    def kernel(*refs):
        code_ref = refs[0] if n_code else None
        refs = refs[n_code:]
        ins, refs = refs[:n_in], refs[n_in + n_held :]
        targets, refs = refs[:n_out], refs[n_out:]
        in_bufs, refs = refs[: len(loads)], refs[len(loads) :]
        out_bufs, refs = list(refs[: n_out - len(near)]), refs[n_out - len(near) :]
        for i in sorted(near):
            out_bufs.insert(i, targets[i])
        in_sems, out_sems, rest = refs[0], refs[1], refs[2:]
        arrivals = [Present(ref) for ref in ins]
        if early is not None:
            early(code_ref, ins, rest)
        for n, i in enumerate(loads):
            source = ins[i] if args[i].cut is None else ins[i].at[args[i].cut]
            arrivals[i] = Incoming(source, in_bufs[n], in_sems.at[n])
        moves = []
        leaving = [Outgoing(t, b, out_sems, moves) for t, b in zip(targets, out_bufs, strict=True)]
        body(code_ref, arrivals, leaving, *rest)
        for arrival in arrivals:
            arrival()
        for move in moves:
            move.wait()

    anywhere, vmem = pl.BlockSpec(memory_space=pl.ANY), pl.BlockSpec(memory_space=pltpu.VMEM)
    specs = [pl.BlockSpec(memory_space=pltpu.SMEM)] * n_code
    specs += [vmem if a.ready else anywhere for a in args] + [anywhere] * n_held
    operands = ([code] if n_code else []) + [a.array for a in args]
    operands += [pltpu.with_memory_space_constraint(a, pltpu.HBM) for a in held]
    bufs = [pltpu.VMEM(args[i].shape, args[i].array.dtype) for i in loads]
    return pl.pallas_call(
        kernel,
        in_specs=specs,
        out_specs=[vmem if i in near else anywhere for i in range(n_out)],
        out_shape=[(jax.ShapeDtypeStruct if i in near else pltpu.HBM)(*o) for i, o in enumerate(outs)],
        scratch_shapes=bufs
        + [pltpu.VMEM(buffers.get(i, o[0]), o[1]) for i, o in enumerate(outs) if i not in near]
        + [pltpu.SemaphoreType.DMA((max(len(loads), 1),)), pltpu.SemaphoreType.DMA((48,))]
        + list(scratch),
        input_output_aliases={n_code + n_in + i: i for i in range(n_held)},
        compiler_params=pltpu.CompilerParams(vmem_limit_bytes=mib * MIB),
        cost_estimate=pl.CostEstimate(flops=0, bytes_accessed=0, transcendentals=0),
        name=name,
    )(*operands)


def project_rows(tokens, cams, embedding, gain, shift, weight, outs, there, hold_ref, summed=None):
    normed, unit, rstd, *triple = outs
    rows = tokens[0].buffer.shape[0]
    pair = 2 * rows
    table = jnp.concatenate(split3(embedding()[...]), 0)
    hot = onehot_t(cams()[...], embedding().shape[0])
    hold_ref[...] = tdot(jnp.concatenate([hot] * 3, 0), table)
    for at, x in enumerate(tokens):
        here = slice(at * rows, (at + 1) * rows)
        values = x()[...].astype(F32) + hold_ref[here, :]
        if at == 0 and summed is not None:
            summed.ref[...] = values
            summed.send()
        values, scale = normalise(values)
        hold_ref[here, :] = values
        rstd.ref[here, :] = scale
    values = hold_ref[...]
    low = (values * gain()[...] + shift()[...]).astype(BF)
    normed.ref[...] = low
    lane = lax.broadcasted_iota(jnp.int32, (pair, PAD), 1)
    for i, (ref, first, out) in enumerate(triple):
        block = dot(low, weight()[:, i * PAD : (i + 1) * PAD])
        if i == 0:
            block = block * HEAD**-0.5
        if i == 2:
            block = jnp.where(lane < MINE, block, 1.0)
        ref[first : first + pair, :] = block.astype(BF)
        out.send((pl.ds(first, pair),), there)
    normed.send(None, there)
    unit.ref[...] = values.astype(BF)
    unit.send(None, there)
    rstd.send(None, there)


def project_outs(total, width):
    outs = [((total, width), BF), ((total, width), BF), ((total, 1), F32)]
    return outs + [((total, PAD), BF)] * 3


def project_body(_, ins, outs, hold_ref):
    xa, xb, cams, embedding, gain, shift, weight = ins
    there = (pl.ds(0, hold_ref.shape[0]),)
    triple = [(out.ref, 0, out) for out in outs[3:6]]
    project_rows((xa, xb), cams, embedding, gain, shift, weight, [*outs[:3], *triple], there, hold_ref, outs[6])


def project(xa, xb, cams, embedding, gain, shift, weight):
    rows, width = xa.shape[-2:]
    pair, total = 2 * rows, 4 * rows
    outs = project_outs(total, width)
    return staged(
        project_body,
        [xa, ready(xb), cams, embedding, gain, shift, weight],
        [*outs, ((rows, width), F32)],
        near=(6,),
        name="project",
        mib=32,
        us=5,
        scratch=[pltpu.VMEM((pair, width), F32)],
        buffers={i: (pair, o[0][1]) for i, o in enumerate(outs)},
    )


def blocks_of(total):
    return [(at, min(256, total - at)) for at in range(0, total, 256)]


TILE = 128


def tile_of(head):
    at = head * HEAD // TILE * TILE
    return slice(at, at + TILE)


def one_head(block, head):
    lane = lax.broadcasted_iota(jnp.int32, block.shape, 1) // HEAD
    return jnp.where(lane == head % (TILE // HEAD), block, jnp.zeros_like(block))


def attend_rows(q_ref, keys, values_of, outs, vt_ref, mt_ref):
    e, first, second, inv = outs
    pair, heads = q_ref.shape[0], e.ref.shape[0]
    work = [(h, at, size) for h in range(heads) for at, size in blocks_of(pair)]

    def scores(h, at, size):
        return dott(keys()[:, tile_of(h)], one_head(q_ref[at : at + size, tile_of(h)], h))

    keys(), values_of()
    ahead = scores(*work[0])
    vt_ref[...] = values_of()[...].astype(F32).T.astype(BF)
    mt_ref[...] = jnp.zeros_like(mt_ref)
    inv.ref[...] = jnp.zeros_like(inv.ref)
    for i, (h, at, size) in enumerate(work):
        here = ahead
        if i + 1 < len(work):
            ahead = scores(*work[i + 1])
        mine = slice(h * HEAD, (h + 1) * HEAD)
        expo = jnp.exp(here - jnp.max(here, 0, keepdims=True)).astype(BF)
        cut = (h, slice(None), slice(at, at + size))
        e.ref[cut] = expo
        if at + size == pair:
            e.send((h,), (h,))
        values = jnp.concatenate([vt_ref[mine, :], vt_ref[MINE : MINE + 16, :]], 0)
        out = dot(values, expo)
        inverse = 1.0 / out[HEAD : HEAD + 1, :]
        mt_ref[mine, at : at + size] = out[:HEAD, :] * inverse
        inv.ref[h : h + 1, at : at + size] = inverse
    mixed = mt_ref[...].T[:pair]
    first.ref[...] = mixed[: pair // 2, :MINE].astype(BF)
    first.send()
    second.ref[...] = mixed[pair // 2 :, :MINE].astype(BF)
    second.send()
    inv.send()


def attend_outs(total):
    pair, heads = total // 2, MINE // HEAD
    wide = -(-pair // 128) * 128
    part = ((pair // 2, MINE), BF)
    return [((heads, total, pair), BF), part, part, ((8, wide), F32)]


def attend_scratch(total):
    wide = -(-(total // 2) // 128) * 128
    return [pltpu.VMEM((PAD, total), BF), pltpu.VMEM((PAD, wide), F32)]


def attend_body(_, ins, outs, *scratch):
    q, k, v = ins
    attend_rows(q(), k, v, outs, *scratch)


def attend(q, k, v):
    total = k.shape[0]
    pair = total // 2
    return staged(
        attend_body,
        [home(q, cut=(pl.ds(0, pair),), shape=(pair, PAD)), ready(k), ready(v)],
        attend_outs(total),
        near=(1, 2),
        name="attend",
        mib=32,
        us=8,
        scratch=attend_scratch(total),
    )


def second_body(_, ins, outs, hold_ref, *scratch):
    xa, xb, cams, embedding, gain, shift, weight = ins
    pair = hold_ref.shape[0]
    keys_ref, values_ref = outs[10].ref, outs[11].ref
    sems, *scratch = scratch
    first = pl.ds(0, pair)
    k, v = (
        Incoming(out.target.at[first], ref.at[first], sems.at[i], ref)
        for i, (out, ref) in enumerate(((outs[4], keys_ref), (outs[5], values_ref)))
    )
    there = (pl.ds(pair, pair),)
    triple = [(outs[3].ref, 0, outs[3]), (k.buffer, pair, outs[4]), (v.buffer, pair, outs[5])]
    outs[4].ref, outs[5].ref = k.buffer, v.buffer
    project_rows((xa, xb), cams, embedding, gain, shift, weight, [*outs[:3], *triple], there, hold_ref)
    attend_rows(outs[3].ref, k, v, outs[6:10], *scratch)
    k()
    v()


def second_half(xa, xb, cams, embedding, gain, shift, weight, held):
    rows, width = xa.shape[-2:]
    pair, total = 2 * rows, 4 * rows
    outs = project_outs(total, width)
    buffers = {i: (pair, o[0][1]) for i, o in enumerate(outs)}
    buffers[4] = buffers[5] = (16, PAD)
    return staged(
        second_body,
        [xa, ready(xb), ready(cams), embedding, gain, shift, weight],
        [*outs, *attend_outs(total), ((total, PAD), BF), ((total, PAD), BF)],
        near=(7, 8, 10, 11),
        name="second_half",
        mib=44,
        us=10,
        scratch=[
            pltpu.VMEM((pair, width), F32),
            pltpu.SemaphoreType.DMA((2,)),
            *attend_scratch(total),
        ],
        held=held,
        buffers=buffers,
    )


def back_heads(heads, q_ref, v_ref, g_ref, kt_ref, delta_of, expos, dq_ref, dk_ref, dv_ref):
    pair = q_ref.shape[0] // 2
    work = [(h, i, at, size) for h in heads for i in range(2) for at, size in blocks_of(pair)]
    dq_ref[...] = jnp.zeros_like(dq_ref)

    def cut(ref, h, i, at, size):
        return one_head(ref[i * pair + at : i * pair + at + size, :], h)

    ahead_grad = cut(g_ref, *work[0])
    ahead = dott(v_ref[...], ahead_grad)
    for n, (h, i, at, size) in enumerate(work):
        if i == at == 0:
            expos[2 * heads.index(h)]()
            expos[2 * heads.index(h) + 1]()
        grad, prob_grad = ahead_grad, ahead
        if n + 1 < len(work):
            ahead_grad = cut(g_ref, *work[n + 1])
            ahead = dott(v_ref[...], ahead_grad)
        expo = expos[2 * heads.index(h) + i]()[:, at : at + size]
        score_grad = (expo.astype(F32) * (prob_grad - delta_of(h, i, at, size))).astype(BF)
        value_part = dot(expo, grad)
        key_part = dot(score_grad, cut(q_ref, h, i, at, size))
        if n:
            value_part += dv_ref[...]
            key_part += dk_ref[...]
        dv_ref[...] = value_part
        dk_ref[...] = key_part
        mine = slice(h * HEAD % TILE, h * HEAD % TILE + HEAD)
        dq_ref[i, mine, at : at + size] = dot(kt_ref[mine, :], score_grad)


def back_first_body(code, ins, outs, g_ref, kt_ref, dq_ref, dk_ref, dv_ref, hold_ref):
    grads, invs, mixes, (v, k, q), expos = ins[:4], ins[4:6], ins[6:10], ins[10:13], ins[13:]
    dq, dk, dv, g_rest, delta = outs
    total = q.buffer.shape[0]
    pair, rows = total // 2, grads[0].buffer.shape[0]
    for arrival in (*grads, *invs, *mixes):
        arrival()
    hold_ref[...] = jnp.zeros_like(hold_ref)
    for i, grad in enumerate(grads):
        hold_ref[i * rows : (i + 1) * rows, :MINE] = grad()[...].astype(F32)
    lane = lax.broadcasted_iota(jnp.int32, (8, PAD), 1) // HEAD
    pick = (lane == lax.broadcasted_iota(jnp.int32, (8, PAD), 0)).astype(F32).astype(BF)
    for i in range(2):
        here = slice(i * pair, (i + 1) * pair)
        inverse = invs[i]()[...].T[:pair, :]
        lane = lax.broadcasted_iota(jnp.int32, (pair, PAD), 1) // HEAD
        scale = jnp.zeros((pair, PAD), F32)
        for h in range(MINE // HEAD):
            scale = jnp.where(lane == h, inverse[:, h : h + 1], scale)
        scaled = (hold_ref[here, :] * scale).astype(BF)
        g_ref[here, :] = scaled[:, :TILE]
        g_rest.ref[here, :] = scaled[:, TILE:]
        for j in range(2):
            rows_here = slice(i * pair + j * rows, i * pair + (j + 1) * rows)
            hold_ref[rows_here, :MINE] = mixes[2 * i + j]()[...].astype(F32)
        prod = scaled.astype(F32) * hold_ref[here, :]
        high = prod.astype(BF)
        low = (prod - high.astype(F32)).astype(BF)
        delta.ref[8 * i : 8 * i + 8, :pair] = dott(pick, high) + dott(pick, low)
        delta.ref[8 * i : 8 * i + 8, pair:] = jnp.zeros((8, delta.ref.shape[1] - pair), F32)
    g_rest.send()
    delta.send()
    for arrival in (v, k, q, *expos[:2]):
        arrival()
    kt_ref[...] = k()[...].astype(F32).T.astype(BF)

    def delta_of(h, i, at, size):
        return delta.ref[8 * i + h : 8 * i + h + 1, at : at + size]

    back_heads((0, 1), q(), v(), g_ref, kt_ref, delta_of, expos, dq_ref, dk_ref, dv_ref)
    for i in range(2):
        dq.ref[i * pair : (i + 1) * pair, :] = (dq_ref[i].T[:pair] * HEAD**-0.5).astype(BF)
    dq.send()
    dk.ref[...] = dk_ref[...].astype(BF)
    dk.send()
    dv.ref[...] = dv_ref[...].astype(BF)
    dv.send()


def back_last_body(code, ins, outs, kt_ref, dq_ref, dk_ref, dv_ref, piece_ref):
    v, g, k, q, delta, *expos = ins[:7]
    dq0, dk0, dv0, normed = ins[7:]
    dqk, dv, keep, send = outs
    pair = q.buffer.shape[0] // 2
    for arrival in (v, g, k, q, delta):
        arrival()
    kt_ref[...] = k()[...].astype(F32).T.astype(BF)

    def delta_of(h, i, at, size):
        return delta()[8 * i + h : 8 * i + h + 1, at : at + size]

    back_heads((2,), q(), v(), g(), kt_ref, delta_of, expos, dq_ref, dk_ref, dv_ref)
    rest = MINE - TILE
    dqk.ref[:, :TILE] = dq0()[...]
    for i in range(2):
        dq = (dq_ref[i].T[:pair] * HEAD**-0.5).astype(BF)
        dqk.ref[i * pair : (i + 1) * pair, TILE:MINE] = dq[:, :rest]
    dqk.ref[:, MINE : MINE + TILE] = dk0()[...]
    dqk.ref[:, MINE + TILE :] = dk_ref[:, :rest].astype(BF)
    dv.ref[:, :TILE] = dv0()[...]
    dv.ref[:, TILE:] = dv_ref[:, :rest].astype(BF)
    weight_grad(code, normed, dqk.ref, dv.ref, keep, send, piece_ref)
    dqk.send()
    dv.send()


PIECES = 8


def weight_grad(code, normed, dqk_ref, dv_ref, keep, send, hold_ref):
    width = normed().shape[1]
    rows = width // PIECES
    piece = rows + rows // 2
    mine = code[0]
    qk = tdot(normed()[...], dqk_ref[...]).astype(BF)
    v = tdot(normed()[...], dv_ref[...]).astype(BF)
    for p in range(PIECES):
        at = pl.multiple_of((p ^ mine) * piece, 16)
        hold_ref[pl.ds(at, rows), :] = qk[p * rows : (p + 1) * rows]
        at = pl.multiple_of((p ^ mine) * piece + rows, 16)
        top = v[p * rows : p * rows + rows // 2]
        low = v[p * rows + rows // 2 : (p + 1) * rows]
        hold_ref[pl.ds(at, rows // 2), :] = jnp.concatenate([top, low], 1)
    half = PIECES * piece // 2
    send.ref[...] = hold_ref[half:, :]
    send.send()
    keep.ref[...] = hold_ref[:half, :]
    keep.send()


def back_scratch(total):
    wide = -(-(total // 2) // 128) * 128
    return [
        pltpu.VMEM((TILE, total), BF),
        pltpu.VMEM((2, TILE, wide), F32),
        pltpu.VMEM((total, TILE), F32),
        pltpu.VMEM((total, TILE), F32),
    ]


def tile_cut(array, tile):
    return home(array, cut=(slice(None), pl.ds(tile * TILE, TILE)), shape=(array.shape[0], TILE))


def back_first(q, k, v, e0, e1, grads, mixes, inv0, inv1):
    total = k.shape[0]
    pair = total // 2
    wide = -(-pair // 128) * 128
    args = [*map(ready, grads), inv0, inv1, *map(ready, mixes)] + [tile_cut(a, 0) for a in (v, k, q)]
    args += [home(e, cut=(h,), shape=(total, pair)) for h in range(2) for e in (e0, e1)]
    return staged(
        back_first_body,
        args,
        [((total, TILE), BF)] * 4 + [((16, wide), F32)],
        near=(0, 1, 2, 3, 4),
        name="back_first",
        mib=40,
        us=12,
        scratch=[pltpu.VMEM((total, TILE), BF), *back_scratch(total), pltpu.VMEM((total, PAD), F32)],
    )


def back_last(codes, q, k, v, e0, e1, first, normed):
    total, width = k.shape[0], normed.shape[1]
    pair = total // 2
    dq, dk, dv, g, delta = first
    piece = width // PIECES * 3 // 2
    half = ((PIECES * piece // 2, 2 * MINE), BF)
    args = [tile_cut(v, 1), ready(g), tile_cut(k, 1), tile_cut(q, 1), ready(delta)]
    args += [home(e, cut=(2,), shape=(total, pair)) for e in (e0, e1)]
    return staged(
        back_last_body,
        [*args, *map(ready, (dq, dk, dv)), normed],
        [((total, 2 * MINE), BF), ((total, MINE), BF), half, half],
        near=(0, 1, 2, 3),
        name="back_last",
        mib=40,
        us=10,
        scratch=[*back_scratch(total), pltpu.VMEM((PIECES * piece, 2 * MINE), BF)],
        code=codes,
    )


STEP = 512


def feed_forward_body(code, ins, outs):
    summed, own, near, far, rest, combiner, baseline, gain, shift, expander, priming, squeezer, tangent = ins
    residual, own_wide, wide, own_slim, slim = outs
    me = code[2]
    first = code[3] == 0
    total = summed()[...] + baseline()[...]
    for r, block in ((2, far), (3, rest), (0, own), (1, near)):
        at = pl.multiple_of((me ^ r) * MINE, 16)
        total += dot(block()[...], combiner()[pl.ds(at, MINE), :])
    residual.ref[...] = total
    residual.send()
    unit, _ = normalise(total)
    low = (unit * gain()[...] + shift()[...]).astype(BF)
    own_slim.ref[...] = jnp.where(first, tangent()[...], low)
    own_slim.send()
    slim.ref[...] = jnp.where(first, low, tangent()[...])
    slim.send()
    for at in range(0, expander().shape[1], STEP):
        cut = slice(at, at + STEP)
        hidden = dot(low, expander()[:, cut]) + priming()[cut]
        back = dott(tangent()[...], squeezer()[cut, :])
        phi = 0.5 * (1.0 + lax.erf(hidden * (2.0**-0.5)))
        density = jnp.exp(-0.5 * hidden * hidden) * 0.3989422804014327
        active = (hidden * phi).astype(BF)
        grad = (back * (phi + hidden * density)).astype(BF)
        own_wide.ref[:, cut] = jnp.where(first, active, grad)
        wide.ref[:, cut] = jnp.where(first, grad, active)
        part = (slice(None), pl.ds(at, STEP))
        own_wide.send(part, part)
        wide.send(part, part)


def feed_forward(codes, summed, own, near, far, rest, combiner, baseline, gain, shift, expander, priming, squeezer, tangent):
    rows, width = summed.shape
    hid = expander.shape[1]
    weights = [combiner, baseline, gain, shift, expander, priming, squeezer, tangent]
    return staged(
        feed_forward_body,
        [*map(ready, (summed, own, near, far, rest)), *weights],
        [((rows, width), F32), ((rows, hid), BF), ((rows, hid), BF), ((rows, width), BF), ((rows, width), BF)],
        near=(0, 1, 2, 3, 4),
        name="feed_forward",
        mib=24,
        us=6,
        code=codes,
    )


def feed_back_body(code, ins, outs, grad_ref, sem):
    expander, residual, gain, tangent, combiner, own_wide, wide = ins
    residual_grad, low, *grads, rows = outs
    me = code[2]
    pltpu.make_async_copy(wide(), grad_ref, sem.at[0]).wait()
    second_grad = dott(grad_ref[...], expander()[...])
    unit, rstd = normalise(residual()[...])
    slope = tangent()[...].astype(F32)
    total = slope + norm_back(second_grad * gain()[...], unit, rstd)
    low.ref[...] = total.astype(BF)
    low.send()
    for r in (2, 3, 1, 0):
        at = pl.multiple_of((me ^ r) * MINE, 16)
        grads[r].ref[...] = dott(low.ref[...], combiner()[pl.ds(at, MINE), :]).astype(BF)
        grads[r].send()
    residual_grad.ref[...] = total
    residual_grad.send()
    width = total.shape[1]
    rows.ref[0:1, :] = jnp.sum(slope, 0, keepdims=True)
    rows.ref[1:2, :] = jnp.sum(low.ref[...].astype(F32), 0, keepdims=True)
    rows.ref[2:3, :] = jnp.sum(second_grad * unit, 0, keepdims=True)
    rows.ref[3:4, :] = jnp.sum(second_grad, 0, keepdims=True)
    for j in range(grad_ref.shape[1] // width):
        block = grad_ref[:, j * width : (j + 1) * width].astype(F32)
        rows.ref[4 + j : 5 + j, :] = jnp.sum(block, 0, keepdims=True)
    rows.ref[6:8, :] = jnp.zeros((2, width), F32)
    rows.send()


def pick_wide(on_zero, on_one):
    def early(code, operands, scratch):
        for core, place in enumerate((on_zero, on_one)):

            @pl.when(code[3] == core)
            def _():
                pltpu.make_async_copy(operands[place], scratch[0], scratch[1].at[0]).start()

    return early


def feed_back(codes, residual, own_wide, wide, tangent, expander, gain, combiner):
    rows, width = residual.shape
    return staged(
        feed_back_body,
        [expander, ready(residual), gain, tangent, combiner, apart(own_wide), apart(wide)],
        [((rows, width), F32), ((rows, width), BF)] + [((rows, MINE), BF)] * 4 + [((8, width), F32)],
        early=pick_wide(6, 5),
        near=(1, 2, 3, 4, 5),
        name="feed_back",
        mib=24,
        us=6,
        scratch=[pltpu.VMEM(wide.shape, BF), pltpu.SemaphoreType.DMA((1,))],
        code=codes,
    )


def outcome_body(code, ins, outs, active_ref, sem):
    squeezer, residual, leveling, own_wide, wide = ins
    pltpu.make_async_copy(wide(), active_ref, sem.at[0]).wait()
    outs[0].ref[...] = (residual()[...] + dot(active_ref[...], squeezer()[...]) + leveling()[...]).astype(BF)
    outs[0].send()


def outcome_of(codes, residual, own_wide, wide, squeezer, leveling):
    rows, width = residual.shape
    return staged(
        outcome_body,
        [squeezer, home(residual), leveling, apart(own_wide), apart(wide)],
        [((rows, width), BF)],
        early=pick_wide(3, 4),
        name="outcome",
        mib=16,
        us=4,
        scratch=[pltpu.VMEM(wide.shape, BF), pltpu.SemaphoreType.DMA((1,))],
        code=codes,
    )[0]


PARTS = 16


def place(code, piece, size):
    return pl.multiple_of((piece ^ code) * size, 8)


def segments(first, rows, low, size):
    out, at = [], first
    while at < first + rows:
        piece, offset = divmod(at - low, size)
        count = min(size - offset, first + rows - at)
        out.append((piece, offset, at - first, count))
        at += count
    return out


def spread(hold_ref, block, first, low, size, code):
    for piece, offset, start, count in segments(first, block.shape[0], low, size):
        at = pl.multiple_of(place(code, piece, size) + offset, 8)
        hold_ref[pl.ds(at, count), :] = block[start : start + count]


def feed_grad_body(sizes, code, ins, outs, tokens_ref, sems, *holds):
    own_wide, own_slim, wide, slim, own, far, near, rest, resid, other = ins
    hid, width = own_wide().shape[1], own_slim().shape[1]
    assert hid == 2 * width
    bulk = PARTS * sizes[0]
    rows = own_slim().shape[0]
    room = tokens_ref.shape[1] // 2
    gap = rows // 16 * 16
    loads = []
    for n, (big, small) in enumerate(((own_wide, own_slim), (wide, slim))):
        first = n * room
        for j in range(3):
            tokens_ref[j, first + gap : first + room, :] = jnp.zeros((room - gap, width), BF)
    for n, (big, small) in enumerate(((own_wide, own_slim), (wide, slim))):
        there = pl.ds(n * room, rows)
        for j in range(hid // width):
            source = big().at[:, pl.ds(j * width, width)]
            loads.append(pltpu.make_async_copy(source, tokens_ref.at[j, there], sems.at[3 * n + j]))
        loads.append(pltpu.make_async_copy(small(), tokens_ref.at[2, there], sems.at[3 * n + 2]))
    for load in loads:
        load.start()
    for load in loads:
        load.wait()

    def put(block, row):
        for part, low, high in ((0, 0, bulk), (1, bulk, bulk + PARTS * sizes[1])):
            first, last = max(row, low), min(row + block.shape[0], high)
            if first < last:
                spread(holds[part], block[first - row : last - row], first, low, sizes[part], code[4 + 2 * part])

    for j in range(hid // width):
        left = jnp.where(code[3] == 0, j, 2)
        right = jnp.where(code[3] == 0, 2, j)
        block = tdot(tokens_ref[left], tokens_ref[right])
        put(block, j * width)

    upper = code[2] < 2
    for i in range(2):
        here = jnp.where(upper, (own, far)[i]()[...], (far, own)[i]()[...])
        peer = jnp.where(upper, (near, rest)[i]()[...], (rest, near)[i]()[...])
        put(tdot(here, resid()[...]) + tdot(peer, other()[...]), hid + i * MINE)
    for part, hold_ref in enumerate(holds):
        keep, send = outs[2 * part : 2 * part + 2]
        half = hold_ref.shape[0] // 2
        send.ref[...] = hold_ref[half:, :].astype(BF)
        send.send()
        keep.ref[...] = hold_ref[:half, :].astype(BF)
        keep.send()


def feed_grad(codes, sizes, feed, mixed):
    rows, width = feed[1].shape
    halves = [((PARTS * size // 2, width), BF) for size in sizes]
    return staged(
        functools.partial(feed_grad_body, sizes),
        [apart(feed[0]), apart(feed[1]), *map(ready, feed[2:]), *map(ready, mixed)],
        [halves[0], halves[0], halves[1], halves[1]],
        near=(0, 1, 2, 3),
        name="feed_grad",
        mib=40,
        us=7,
        scratch=[
            pltpu.VMEM((3, 2 * (-(-rows // 16) * 16), width), BF),
            pltpu.SemaphoreType.DMA((6,)),
            *[pltpu.VMEM((PARTS * size, width), F32) for size in sizes],
        ],
        code=codes,
    )


def feed_assemble_body(side, sizes, code, ins, outs, sems, *holds):
    squeezer, expander, combiner = (out.target for out in outs)
    hid, width = squeezer.shape

    def targets(core, row, count):
        out = []
        while count:
            if row < hid and core == 0:
                take = min(count, hid - row)
                out.append((squeezer.at[pl.ds(row, take), :], take))
            elif row < hid:
                j = row // width
                take = min(count, (j + 1) * width - row)
                cut = pl.ds(row - j * width, take), pl.ds(j * width, width)
                out.append((expander.at[cut], take))
            else:
                view, at = divmod(row - hid, MINE)
                take = min(count, MINE - at)
                out.append((combiner.at[pl.ds((core + 2 * view) * MINE + at, take), :], take))
            row, count = row + take, count - take
        return out

    for i, hold_ref in enumerate(holds):
        half = hold_ref.shape[0] // 2
        hold_ref[:half, :] = ins[2 * i]()[...].astype(F32)
        hold_ref[half:, :] = ins[2 * i + 1]()[...].astype(F32)
    for core in range(2):

        @pl.when(code[3] == core ^ side)
        def _():
            moves, low = [], 0
            for part, size in enumerate(sizes):
                for piece in range(PARTS):
                    start = pl.multiple_of((piece ^ code[4 + 2 * part + side]) * size, 8)
                    at = 0
                    for target, count in targets(core, low + piece * size, size):
                        source = holds[part].at[pl.ds(pl.multiple_of(start + at, 8), count), :]
                        moves.append(pltpu.make_async_copy(source, target, sems.at[len(moves)]))
                        moves[-1].start()
                        at += count
                low += PARTS * size
            for move in moves:
                move.wait()


def feed_assemble(codes, side, blocks, hid, held=()):
    width = blocks[0].shape[1]
    sizes = [blocks[0].shape[0] // 8, blocks[2].shape[0] // 8]
    return staged(
        functools.partial(feed_assemble_body, side, sizes),
        [ready(b) for b in blocks],
        [((hid, width), F32), ((width, hid), F32), ((width, width), F32)],
        name="feed_assemble",
        mib=24,
        us=5,
        scratch=[pltpu.SemaphoreType.DMA((48,))] + [pltpu.VMEM((PARTS * n, width), F32) for n in sizes],
        code=codes,
        held=held,
        buffers={0: (8, 128), 1: (8, 128), 2: (8, 128)},
    )


def input_grad_body(_, ins, outs, hold_ref):
    dqk, dv, weight, unit, rstd, gain, *rest = ins
    near_cams, far_cams, resid = rest
    small = outs[4]
    patches = resid.buffer.shape[0]
    groups = small.ref.shape[0] - 2
    slope = dott(dqk()[:, :MINE], weight()[:, :MINE]) + dott(dqk()[:, MINE:], weight()[:, PAD : PAD + MINE])
    slope += dott(dv()[...], weight()[:, 2 * PAD : 2 * PAD + MINE])
    values = unit()[...].astype(F32)
    small.ref[groups : groups + 1, :] = jnp.sum(slope * values, 0, keepdims=True)
    small.ref[groups + 1 : groups + 2, :] = jnp.sum(slope, 0, keepdims=True)
    hold_ref[...] = norm_back(slope * gain()[...], values, rstd()[...])
    for r in (1, 3, 0, 2):
        part = hold_ref[r * patches : (r + 1) * patches, :]
        outs[r].ref[...] = part.astype(outs[r].ref.dtype)
        outs[r].send()
    hold_ref[:patches, :] = hold_ref[:patches, :] + resid()[...]
    table = jnp.zeros((groups, slope.shape[1]), F32)
    for i, cams in enumerate((near_cams, far_cams)):
        part = hold_ref[2 * i * patches : 2 * (i + 1) * patches, :]
        hot = onehot_t(cams()[...], groups)
        for piece in split3(part)[:2]:
            table += dot(hot, piece)
    small.ref[:groups, :] = table
    small.send()


def input_grad(dqk, dv, weight, unit, rstd, gain, cams, resid, groups):
    total, width = unit.shape
    patches = resid.shape[0]
    low, full = ((patches, width), BF), ((patches, width), F32)
    return staged(
        input_grad_body,
        [ready(dqk), ready(dv), home(weight), home(unit), home(rstd), gain, *cams, home(resid)],
        [full, low, full, low, ((groups + 2, width), F32)],
        near=(0, 1, 2, 3, 4),
        name="input_grad",
        mib=48,
        us=9,
        scratch=[pltpu.VMEM((total, width), F32)],
    )


def assemble_body(code, ins, outs):
    out, table, *vectors = outs
    rows, width = out.ref.shape[0] // PIECES, out.ref.shape[1] // 3
    piece = rows * 3 // 2
    blocks = [arrival() for arrival in ins[:4]]
    for p in range(PIECES):
        cut = []
        for i, which in enumerate((0, 1, 0, 1)):
            r = (p ^ code[which]) % 4
            core = code[3] if which == 0 else 1 - code[3]
            far = i // 2
            middle = jnp.where(core == 0, r // 2 * 2 + far, far * 2 + r // 2)
            at = pl.multiple_of((middle * 2 + r % 2) * piece, 16)
            upper = (p ^ code[which]) >= PIECES // 2
            lower_block = blocks[2 * which][pl.ds(at, piece), :]
            upper_block = blocks[2 * which + 1][pl.ds(at, piece), :]
            cut.append(jnp.where(upper, upper_block, lower_block).astype(F32))
        low = p * rows
        for v, block in enumerate(by_view(cut, code[2])):
            at = v * MINE
            out.ref[low : low + rows, at : at + MINE] = block[:rows, :MINE]
            out.ref[low : low + rows, width + at : width + at + MINE] = block[:rows, MINE:]
            at += 2 * width
            out.ref[low : low + rows // 2, at : at + MINE] = block[rows:, :MINE]
            out.ref[low + rows // 2 : low + rows, at : at + MINE] = block[rows:, MINE:]
        out.send((pl.ds(low, rows),), (pl.ds(low, rows),))
    total = ins[4]()[...].astype(F32) + ins[5]()[...].astype(F32)
    count, half, groups = total.shape[0] // 2, width // 2, table.ref.shape[0]
    table.ref[:, :half] = total[:groups, :]
    table.ref[:, half:] = total[count : count + groups, :]
    table.send()
    row = groups
    for vector in vectors:
        for at in range(0, vector.ref.shape[0], width):
            vector.ref[at : at + half] = total[row, :]
            vector.ref[at + half : at + width] = total[count + row, :]
            row += 1
        vector.send()


def assemble(codes, blocks, smalls, groups, sizes, width):
    return staged(
        assemble_body,
        [ready(b) for b in (*blocks, *smalls)],
        [((width, 3 * width), F32), ((groups, width), F32)] + [((size,), F32) for size in sizes],
        name="assemble",
        mib=24,
        us=5,
        code=codes,
    )


def turned(block):
    half = block.shape[0] // 2
    return jnp.concatenate([block[half:], block[:half]], 0)


def after(values, *others):
    out = lax.optimization_barrier((*values, *others))
    return out[: len(values)]


def halve(keep, got):
    cut = keep.shape[0] // 2
    return keep[:cut] + got[:cut], keep[cut:] + got[cut:]


class Part:
    def __init__(self, keep, got, stages):
        self.value, self.got, self.stages, self.step, self.lower, self.peer = keep, got, stages, 0, None, None

    def begin(self):
        self.value, send = halve(self.value, self.got)
        self.got = swap_by_core(send, self.stages[2])

    def advance(self, got):
        self.step += 1
        if self.step == 1:
            self.value = lax.optimization_barrier(whole_slice(self.value + got))
            self.got = swap_by_core(self.value, self.stages[3])
        elif self.step == 2:
            self.value = lax.optimization_barrier(self.value + turned(got))
            self.got = swap_by_core(self.value, self.stages[2])
        elif self.step == 3:
            self.value = jnp.concatenate([self.value, got], 0)
            self.got = swap_by_core(self.value, self.stages[1])
        elif self.step == 4:
            self.value = jnp.concatenate([self.value, got], 0)
            self.got, peer = swap_by_core(self.value, self.stages[0]), swap(self.value, "view", 1)
            self.lower = (self.value, peer)
        else:
            self.got, self.peer = got, swap(got, "view", 1)
            return []
        return [self.value]


PLAN = ("LAB", "LAG", "BI", "A", "B", "L", "AI", "L", "B", "LpO", "AB", "P", "Lkq")


def on_device(
    inputs,
    cameras,
    embedding,
    scaling,
    shifting,
    projector,
    combiner,
    baseline,
    rescaling,
    reshifting,
    expander,
    priming,
    squeezer,
    leveling,
    cotangent,
):
    me = lax.axis_index("view")
    core = me % 2
    patches, width = inputs.shape[2], inputs.shape[3]
    groups, hid = embedding.shape[0], expander.shape[1]
    codes = [code_of(SCENE, core), code_of(SCENE, 1 - core), me, core]
    codes += [code_of(WIDE, core), code_of(WIDE, 1 - core), code_of(THIN, core), code_of(THIN, core)]
    codes = jnp.stack(codes).astype(jnp.int32)
    tangent = cotangent.reshape(patches, width)
    x0 = inputs.reshape(patches, width)
    c0 = cameras.reshape(1, patches)
    x2 = swap(x0, "view", 2)
    x1, c1 = swap(x0, "view", 1), swap(c0, "view", 1)
    near_cams = jnp.concatenate([c0, c1], 1)
    far_cams = swap(near_cams, "view", 2)
    hole = jnp.zeros((width, PAD - MINE), BF)
    padded = []
    for part in range(3):
        padded += [lax.dynamic_slice_in_dim(projector, part * width + me * MINE, MINE, 1), hole]
    padded = jnp.concatenate(padded, 1)
    *held, summed = project(x0, x1, near_cams, embedding, scaling, shifting, padded)
    x2, far_cams = after((x2, far_cams), *held)
    x3 = swap(x2, "view", 1)
    normed, unit1, rstd1, q, k, v, e1, far, rest, inv1, near_k, near_v = second_half(
        x2, x3, far_cams, embedding, scaling, shifting, padded, held
    )
    mine_far, mine_rest = far, rest
    far, rest = swap(far, "view", 2), swap(rest, "view", 3)
    e0, own, near, inv0 = attend(q, near_k, near_v)
    mixes = [own, near, mine_far, mine_rest]
    near, own, far, rest = after((near, own, far, rest))
    near, peer_rest = swap(near, "view", 1), swap(rest, "view", 1)

    residual, own_wide, wide, own_slim, slim = feed_forward(
        codes, summed, own, near, far, rest, combiner, baseline, rescaling, reshifting, expander, priming,
        squeezer, tangent,
    )
    peer_near = swap(near, "view", 1)
    peer_wide, peer_slim = swap(wide, "view", 1), swap(slim, "view", 1)
    residual_grad, resid_low, *grads, rows = feed_back(
        codes, residual, own_wide, wide, tangent, expander, rescaling, combiner
    )
    peer_near, peer_rest, resid_low, *grads = after((peer_near, peer_rest, resid_low, *grads))
    grads = [grads[0]] + [swap(grads[r], "view", r) for r in (1, 2, 3)]
    other = swap(resid_low, "view", 1)
    sizes = [(hid + width // 2) // 24, (hid + width // 2) // 48]
    keep0, send0, keep1, send1 = feed_grad(
        codes, sizes, [own_wide, own_slim, peer_wide, peer_slim],
        [own, far, peer_near, peer_rest, resid_low, other],
    )
    *grads, keep0, send0, keep1, send1 = after((*grads, keep0, send0, keep1, send1))
    got0, got1 = swap_by_core(send0, WIDE[0]), swap_by_core(send1, THIN[0])
    first = back_first(q, k, v, e0, e1, grads, mixes, inv0, inv1)
    got0, got1, *first = after((got0, got1, *first))
    keep0, send0 = halve(keep0, got0)
    keep1, send1 = halve(keep1, got1)
    got0, got1 = swap_by_core(send0, WIDE[1]), swap_by_core(send1, THIN[1])
    dqk, dv, keep, send = back_last(codes, q, k, v, e0, e1, first, normed)
    got0, got1, dqk, dv, keep, send = after((got0, got1, dqk, dv, keep, send))
    wide_part = Part(keep0, got0, WIDE)
    thin_part = Part(keep1, got1, THIN)
    got_l = swap_by_core(send, SCENE[0])
    wide_part.begin()
    thin_part.begin()
    parts = dict(A=wide_part, B=thin_part)
    l_step, i_step = 0, 0
    message = near_keep = near_got = other = small = None
    outcome = inputs_grad = feed_grads = None
    last = []
    gate = [codes, dqk]
    extra = 0

    def grow(message, got):
        small = rounded(message[-extra:].astype(F32) + got[-extra:].astype(F32))
        return jnp.concatenate([message[:-extra], got[:-extra], small], 0)

    for group in PLAN:
        tied = []
        if "O" in group:
            outcome = outcome_of(gate[0], residual, own_wide, wide, squeezer, leveling)
            tied.append(outcome)
        if "G" in group:
            own, near, far, rest, small = input_grad(
                gate.pop(), dv, padded, unit1, rstd1, scaling, (near_cams, far_cams), residual_grad, groups
            )
            tied += [near, rest, small]
        if "P" in group:
            blocks = [b for n in "AB" for b in (parts[n].lower[0], parts[n].got)]
            feed_grads = feed_assemble(gate[0], 0, blocks, hid)
            tied += feed_grads
        waits = []
        for name in group:
            if name in "AB":
                waits.append(parts[name].got)
            elif name == "L":
                waits.append(got_l)
            elif name == "I":
                waits += [near, rest] if i_step == 0 else [far]
            elif name == "p":
                waits += [parts["A"].lower[1], parts["B"].lower[1]]
            elif name == "k":
                waits.append(near_keep)
            elif name == "q":
                waits += [parts[n].peer for n in "AB"]
        bundle = list(after((*waits, *tied, *last, *gate)))
        new_waits, rest_of = bundle[: len(waits)], bundle[len(waits) :]
        new_tied, gate = rest_of[: len(tied)], rest_of[len(rest_of) - len(gate) :]
        if "O" in group:
            outcome = new_tied.pop(0)
        if "G" in group:
            near, rest, small = new_tied[:3]
            new_tied = new_tied[3:]
        if "P" in group:
            feed_grads = new_tied
        last = []
        for name in group:
            if name in "AB":
                last += parts[name].advance(new_waits.pop(0))
            elif name == "p":
                for n in "AB":
                    parts[n].lower = (parts[n].lower[0], new_waits.pop(0))
            elif name == "k":
                near_keep = new_waits.pop(0)
            elif name == "q":
                for n in "AB":
                    parts[n].peer = new_waits.pop(0)
            elif name == "I":
                if i_step == 0:
                    near, rest = new_waits.pop(0), new_waits.pop(0)
                    far = lax.optimization_barrier((far + rest.astype(F32)).astype(BF))
                    last.append(far)
                    far = swap(far, "view", 2)
                else:
                    far = new_waits.pop(0)
                    inputs_grad = (residual_grad + own + near.astype(F32) + far.astype(F32)).astype(BF)
                    last.append(inputs_grad)
                i_step += 1
            elif name == "L":
                got = new_waits.pop(0)
                if l_step == 0:
                    keep, send = halve(keep, got)
                    got_l = swap_by_core(send, SCENE[1])
                elif l_step == 1:
                    block = jnp.concatenate([small, rows[:6]], 0)
                    block = rounded(jnp.concatenate([block[:, : width // 2], block[:, width // 2 :]], 0))
                    extra = block.shape[0]
                    message = jnp.concatenate([keep + got, block], 0)
                    message = lax.optimization_barrier(whole_slice(message))
                    got_l = swap_by_core(message, SCENE[2])
                elif l_step == 2:
                    got = jnp.concatenate([turned(got[:-extra]), got[-extra:]], 0)
                    message = rounded(message.astype(F32) + got.astype(F32))
                    got_l = swap_by_core(message, LATE[0])
                elif l_step < 5:
                    message = grow(message, got)
                    got_l = swap_by_core(message, LATE[l_step - 2])
                    if l_step == 4:
                        near_keep = swap(message[:-extra], "view", 1)
                else:
                    got_l = got
                    near_got = swap(got, "view", 1)
                    small = rounded(message[-extra:].astype(F32) + got[-extra:].astype(F32))
                    other = swap(small, "view", 1)
                if l_step:
                    last.append(message if l_step < 5 else small)
                else:
                    last += [keep, send]
                l_step += 1
            elif name == "G":
                near, rest = swap(near, "view", 1), swap(rest, "view", 1)
    assert l_step == 6 and i_step == 2 and outcome is not None
    blocks = [b for n in "AB" for b in (parts[n].lower[1], parts[n].peer)]
    grad_squeezer, grad_expander, grad_combiner = feed_assemble(gate[0], 1, blocks, hid, feed_grads)
    near_got, other, grad_squeezer = after((near_got, other, grad_squeezer))
    vectors = [width] * 6 + [hid]
    grad_projector, table, *vectors = assemble(
        gate[0], [message, got_l, near_keep, near_got], [small, other], groups, vectors, width
    )
    grad_scaling, grad_shifting, grad_leveling, grad_baseline, grad_rescaling, grad_reshifting, grad_priming = vectors

    return (
        outcome.reshape(inputs.shape),
        inputs_grad.reshape(inputs.shape),
        table,
        grad_scaling,
        grad_shifting,
        grad_projector,
        grad_combiner,
        grad_baseline,
        grad_rescaling,
        grad_reshifting,
        grad_expander,
        grad_priming,
        grad_squeezer,
        grad_leveling,
    )


def solution(mesh):
    tokens = P("scene", "view", None, None)
    placed = (tokens, P("scene", "view", None)) + (P(),) * 12 + (tokens,)
    return jax.shard_map(
        on_device,
        mesh=mesh,
        in_specs=placed,
        out_specs=(tokens, tokens) + (P(),) * 12,
        check_vma=False,
    )
```

```python
import functools

import jax
import jax.numpy as jnp
from jax import lax
from jax.experimental import pallas as pl
from jax.experimental.pallas import tpu as pltpu
from jax.sharding import PartitionSpec as P

HEADS = 12
HEAD = 64
BF = jnp.bfloat16
F32 = jnp.float32
BOTH = ("scene", "view")
MINE = HEADS // 4 * HEAD
PAD = 256
MIB = 1 << 20


def swap(value, axis, mask):
    count = lax.axis_size(axis)
    return lax.ppermute(value, axis, [(i, i ^ mask) for i in range(count)])


def swap_by_core(value, masks):
    scenes, views = lax.axis_size("scene"), lax.axis_size("view")
    pairs = []
    for s in range(scenes):
        for v in range(views):
            ds, dv = masks[v % 2]
            pairs.append((s * views + v, (s ^ ds) * views + (v ^ dv)))
    return lax.ppermute(value, BOTH, pairs)


def side_of(masks, core):
    scene, view = lax.axis_index("scene"), lax.axis_index("view")
    bits = [((scene & ds) + (view & dv) > 0).astype(jnp.int32) for ds, dv in masks]
    return jnp.where(core == 0, bits[0], bits[1])


def code_of(stages, core):
    total = 0
    for masks in stages:
        total = 2 * total + side_of(masks, core)
    return total


X, Y, Z1, Z2 = (1, 0), (0, 2), (2, 0), (4, 0)
WIDE = ((X, Z1), (Y, X), (Z1, Y), (Z2, Z2))
THIN = ((Y, Y), (Z1, Z1), (X, X), (Z2, Z2))
SCENE = ((X, Z1), (Z1, X), (Z2, Z2))
LATE = ((Y, X), (Z1, Y), (X, Z1))


def rounded(value):
    return lax.optimization_barrier(lax.reduce_precision(value, 8, 7).astype(BF))


def whole_slice(value):
    bit = 8
    while bit < lax.axis_size("scene"):
        value = rounded(value.astype(F32) + swap(value, "scene", bit).astype(F32))
        bit *= 2
    return value


def by_view(blocks, me):
    a, b, c, d = blocks
    one = (me & 1) == 1
    a, b = jnp.where(one, b, a), jnp.where(one, a, b)
    c, d = jnp.where(one, d, c), jnp.where(one, c, d)
    two = (me & 2) == 2
    a, c = jnp.where(two, c, a), jnp.where(two, a, c)
    b, d = jnp.where(two, d, b), jnp.where(two, b, d)
    return a, b, c, d


def normalise(values):
    centre = values - jnp.mean(values, axis=-1, keepdims=True)
    rstd = lax.rsqrt(jnp.mean(centre * centre, axis=-1, keepdims=True) + 1e-05)
    return centre * rstd, rstd


def norm_back(grad, unit, rstd):
    return (
        grad
        - jnp.mean(grad, axis=-1, keepdims=True)
        - unit * jnp.mean(grad * unit, axis=-1, keepdims=True)
    ) * rstd


def dot(a, b):
    return jnp.dot(a, b, preferred_element_type=F32)


def tdot(a, b):
    return lax.dot_general(a, b, (((0,), (0,)), ((), ())), preferred_element_type=F32)


def dott(a, b):
    return lax.dot_general(a, b, (((1,), (1,)), ((), ())), preferred_element_type=F32)


def split3(values):
    high = values.astype(BF)
    rest = values - high.astype(F32)
    middle = rest.astype(BF)
    return high, middle, (rest - middle.astype(F32)).astype(BF)


def onehot_t(cameras, groups):
    rows = lax.broadcasted_iota(jnp.int32, (groups, cameras.shape[1]), 0)
    return (rows == cameras).astype(F32).astype(BF)


class Incoming:
    def __init__(self, source, buffer, sem, whole=None):
        self.copy, self.there = pltpu.make_async_copy(source, buffer, sem), False
        self.buffer = buffer if whole is None else whole
        self.copy.start()

    def __call__(self):
        if not self.there:
            self.copy.wait()
            self.there = True
        return self.buffer


class Present:
    def __init__(self, ref):
        self.buffer = ref

    def __call__(self):
        return self.buffer


class Outgoing:
    def __init__(self, target, buffer, sems, moves):
        self.target, self.ref, self.sems, self.moves = target, buffer, sems, moves

    def send(self, here=None, there=None):
        if self.ref is self.target:
            return
        source = self.ref if here is None else self.ref.at[here]
        target = self.target if there is None else self.target.at[there]
        move = pltpu.make_async_copy(source, target, self.sems.at[len(self.moves)])
        move.start()
        self.moves.append(move)


class Operand:
    def __init__(self, array, *, home=False, ready=False, cut=None, shape=None):
        self.array, self.ready, self.cut, self.apart = array, ready, cut, False
        if home:
            self.array = pltpu.with_memory_space_constraint(array, pltpu.HBM)
        self.shape = array.shape if shape is None else shape


def apart(array):
    operand = Operand(array)
    operand.apart = True
    return operand


def home(array, **more):
    return Operand(array, home=True, **more)


def ready(array):
    return Operand(array, ready=True)


def staged(body, args, outs, *, name, mib, us, scratch=(), code=None, held=(), buffers=None, early=None, near=()):
    buffers = buffers or {}
    args = [a if isinstance(a, Operand) else home(a) for a in args]
    n_code, n_in, n_held, n_out = int(code is not None), len(args), len(held), len(outs)
    loads = [i for i, a in enumerate(args) if not (a.ready or a.apart)]

    def kernel(*refs):
        code_ref = refs[0] if n_code else None
        refs = refs[n_code:]
        ins, refs = refs[:n_in], refs[n_in + n_held :]
        targets, refs = refs[:n_out], refs[n_out:]
        in_bufs, refs = refs[: len(loads)], refs[len(loads) :]
        out_bufs, refs = list(refs[: n_out - len(near)]), refs[n_out - len(near) :]
        for i in sorted(near):
            out_bufs.insert(i, targets[i])
        in_sems, out_sems, rest = refs[0], refs[1], refs[2:]
        arrivals = [Present(ref) for ref in ins]
        if early is not None:
            early(code_ref, ins, rest)
        for n, i in enumerate(loads):
            source = ins[i] if args[i].cut is None else ins[i].at[args[i].cut]
            arrivals[i] = Incoming(source, in_bufs[n], in_sems.at[n])
        moves = []
        leaving = [Outgoing(t, b, out_sems, moves) for t, b in zip(targets, out_bufs, strict=True)]
        body(code_ref, arrivals, leaving, *rest)
        for arrival in arrivals:
            arrival()
        for move in moves:
            move.wait()

    anywhere, vmem = pl.BlockSpec(memory_space=pl.ANY), pl.BlockSpec(memory_space=pltpu.VMEM)
    specs = [pl.BlockSpec(memory_space=pltpu.SMEM)] * n_code
    specs += [vmem if a.ready else anywhere for a in args] + [anywhere] * n_held
    operands = ([code] if n_code else []) + [a.array for a in args]
    operands += [pltpu.with_memory_space_constraint(a, pltpu.HBM) for a in held]
    bufs = [pltpu.VMEM(args[i].shape, args[i].array.dtype) for i in loads]
    return pl.pallas_call(
        kernel,
        in_specs=specs,
        out_specs=[vmem if i in near else anywhere for i in range(n_out)],
        out_shape=[(jax.ShapeDtypeStruct if i in near else pltpu.HBM)(*o) for i, o in enumerate(outs)],
        scratch_shapes=bufs
        + [pltpu.VMEM(buffers.get(i, o[0]), o[1]) for i, o in enumerate(outs) if i not in near]
        + [pltpu.SemaphoreType.DMA((max(len(loads), 1),)), pltpu.SemaphoreType.DMA((48,))]
        + list(scratch),
        input_output_aliases={n_code + n_in + i: i for i in range(n_held)},
        compiler_params=pltpu.CompilerParams(vmem_limit_bytes=mib * MIB),
        cost_estimate=pl.CostEstimate(flops=0, bytes_accessed=0, transcendentals=0),
        name=name,
    )(*operands)


def project_rows(tokens, cams, embedding, gain, shift, weight, outs, there, hold_ref, summed=None):
    normed, unit, rstd, *triple = outs
    rows = tokens[0].buffer.shape[0]
    pair = 2 * rows
    table = jnp.concatenate(split3(embedding()[...]), 0)
    hot = onehot_t(cams()[...], embedding().shape[0])
    hold_ref[...] = tdot(jnp.concatenate([hot] * 3, 0), table)
    for at, x in enumerate(tokens):
        here = slice(at * rows, (at + 1) * rows)
        values = x()[...].astype(F32) + hold_ref[here, :]
        if at == 0 and summed is not None:
            summed.ref[...] = values
            summed.send()
        values, scale = normalise(values)
        hold_ref[here, :] = values
        rstd.ref[here, :] = scale
    values = hold_ref[...]
    low = (values * gain()[...] + shift()[...]).astype(BF)
    normed.ref[...] = low
    lane = lax.broadcasted_iota(jnp.int32, (pair, PAD), 1)
    for i, (ref, first, out) in enumerate(triple):
        block = dot(low, weight()[:, i * PAD : (i + 1) * PAD])
        if i == 0:
            block = block * HEAD**-0.5
        if i == 2:
            block = jnp.where(lane < MINE, block, 1.0)
        ref[first : first + pair, :] = block.astype(BF)
        out.send((pl.ds(first, pair),), there)
    normed.send(None, there)
    unit.ref[...] = values.astype(BF)
    unit.send(None, there)
    rstd.send(None, there)


def project_outs(total, width):
    outs = [((total, width), BF), ((total, width), BF), ((total, 1), F32)]
    return outs + [((total, PAD), BF)] * 3


def project_body(_, ins, outs, hold_ref):
    xa, xb, cams, embedding, gain, shift, weight = ins
    there = (pl.ds(0, hold_ref.shape[0]),)
    triple = [(out.ref, 0, out) for out in outs[3:6]]
    project_rows((xa, xb), cams, embedding, gain, shift, weight, [*outs[:3], *triple], there, hold_ref, outs[6])


def project(xa, xb, cams, embedding, gain, shift, weight):
    rows, width = xa.shape[-2:]
    pair, total = 2 * rows, 4 * rows
    outs = project_outs(total, width)
    return staged(
        project_body,
        [xa, ready(xb), cams, embedding, gain, shift, weight],
        [*outs, ((rows, width), F32)],
        near=(6,),
        name="project",
        mib=32,
        us=5,
        scratch=[pltpu.VMEM((pair, width), F32)],
        buffers={i: (pair, o[0][1]) for i, o in enumerate(outs)},
    )


def blocks_of(total):
    return [(at, min(256, total - at)) for at in range(0, total, 256)]


TILE = 128


def tile_of(head):
    at = head * HEAD // TILE * TILE
    return slice(at, at + TILE)


def one_head(block, head):
    lane = lax.broadcasted_iota(jnp.int32, block.shape, 1) // HEAD
    return jnp.where(lane == head % (TILE // HEAD), block, jnp.zeros_like(block))


def attend_rows(q_ref, keys, values_of, outs, vt_ref, mt_ref):
    e, first, second, inv = outs
    pair, heads = q_ref.shape[0], e.ref.shape[0]
    work = [(h, at, size) for h in range(heads) for at, size in blocks_of(pair)]

    def scores(h, at, size):
        return dott(keys()[:, tile_of(h)], one_head(q_ref[at : at + size, tile_of(h)], h))

    keys(), values_of()
    ahead = scores(*work[0])
    vt_ref[...] = values_of()[...].astype(F32).T.astype(BF)
    mt_ref[...] = jnp.zeros_like(mt_ref)
    inv.ref[...] = jnp.zeros_like(inv.ref)
    for i, (h, at, size) in enumerate(work):
        here = ahead
        if i + 1 < len(work):
            ahead = scores(*work[i + 1])
        mine = slice(h * HEAD, (h + 1) * HEAD)
        expo = jnp.exp(here - jnp.max(here, 0, keepdims=True)).astype(BF)
        cut = (h, slice(None), slice(at, at + size))
        e.ref[cut] = expo
        if at + size == pair:
            e.send((h,), (h,))
        values = jnp.concatenate([vt_ref[mine, :], vt_ref[MINE : MINE + 16, :]], 0)
        out = dot(values, expo)
        inverse = 1.0 / out[HEAD : HEAD + 1, :]
        mt_ref[mine, at : at + size] = out[:HEAD, :] * inverse
        inv.ref[h : h + 1, at : at + size] = inverse
    mixed = mt_ref[...].T[:pair]
    first.ref[...] = mixed[: pair // 2, :MINE].astype(BF)
    first.send()
    second.ref[...] = mixed[pair // 2 :, :MINE].astype(BF)
    second.send()
    inv.send()


def attend_outs(total):
    pair, heads = total // 2, MINE // HEAD
    wide = -(-pair // 128) * 128
    part = ((pair // 2, MINE), BF)
    return [((heads, total, pair), BF), part, part, ((8, wide), F32)]


def attend_scratch(total):
    wide = -(-(total // 2) // 128) * 128
    return [pltpu.VMEM((PAD, total), BF), pltpu.VMEM((PAD, wide), F32)]


def attend_body(_, ins, outs, *scratch):
    q, k, v = ins
    attend_rows(q(), k, v, outs, *scratch)


def attend(q, k, v):
    total = k.shape[0]
    pair = total // 2
    return staged(
        attend_body,
        [home(q, cut=(pl.ds(0, pair),), shape=(pair, PAD)), ready(k), ready(v)],
        attend_outs(total),
        near=(1, 2),
        name="attend",
        mib=32,
        us=8,
        scratch=attend_scratch(total),
    )


def second_body(_, ins, outs, hold_ref, *scratch):
    xa, xb, cams, embedding, gain, shift, weight = ins
    pair = hold_ref.shape[0]
    keys_ref, values_ref = outs[10].ref, outs[11].ref
    sems, *scratch = scratch
    first = pl.ds(0, pair)
    k, v = (
        Incoming(out.target.at[first], ref.at[first], sems.at[i], ref)
        for i, (out, ref) in enumerate(((outs[4], keys_ref), (outs[5], values_ref)))
    )
    there = (pl.ds(pair, pair),)
    triple = [(outs[3].ref, 0, outs[3]), (k.buffer, pair, outs[4]), (v.buffer, pair, outs[5])]
    outs[4].ref, outs[5].ref = k.buffer, v.buffer
    project_rows((xa, xb), cams, embedding, gain, shift, weight, [*outs[:3], *triple], there, hold_ref)
    attend_rows(outs[3].ref, k, v, outs[6:10], *scratch)
    k()
    v()


def second_half(xa, xb, cams, embedding, gain, shift, weight, held):
    rows, width = xa.shape[-2:]
    pair, total = 2 * rows, 4 * rows
    outs = project_outs(total, width)
    buffers = {i: (pair, o[0][1]) for i, o in enumerate(outs)}
    buffers[4] = buffers[5] = (16, PAD)
    return staged(
        second_body,
        [xa, ready(xb), ready(cams), embedding, gain, shift, weight],
        [*outs, *attend_outs(total), ((total, PAD), BF), ((total, PAD), BF)],
        near=(7, 8, 10, 11),
        name="second_half",
        mib=44,
        us=10,
        scratch=[
            pltpu.VMEM((pair, width), F32),
            pltpu.SemaphoreType.DMA((2,)),
            *attend_scratch(total),
        ],
        held=held,
        buffers=buffers,
    )


def back_heads(heads, q_ref, v_ref, g_ref, kt_ref, delta_of, expos, dq_ref, dk_ref, dv_ref):
    pair = q_ref.shape[0] // 2
    work = [(h, i, at, size) for h in heads for i in range(2) for at, size in blocks_of(pair)]
    dq_ref[...] = jnp.zeros_like(dq_ref)

    def cut(ref, h, i, at, size):
        return one_head(ref[i * pair + at : i * pair + at + size, :], h)

    ahead_grad = cut(g_ref, *work[0])
    ahead = dott(v_ref[...], ahead_grad)
    for n, (h, i, at, size) in enumerate(work):
        if i == at == 0:
            expos[2 * heads.index(h)]()
            expos[2 * heads.index(h) + 1]()
        grad, prob_grad = ahead_grad, ahead
        if n + 1 < len(work):
            ahead_grad = cut(g_ref, *work[n + 1])
            ahead = dott(v_ref[...], ahead_grad)
        expo = expos[2 * heads.index(h) + i]()[:, at : at + size]
        score_grad = (expo.astype(F32) * (prob_grad - delta_of(h, i, at, size))).astype(BF)
        value_part = dot(expo, grad)
        key_part = dot(score_grad, cut(q_ref, h, i, at, size))
        if n:
            value_part += dv_ref[...]
            key_part += dk_ref[...]
        dv_ref[...] = value_part
        dk_ref[...] = key_part
        mine = slice(h * HEAD % TILE, h * HEAD % TILE + HEAD)
        dq_ref[i, mine, at : at + size] = dot(kt_ref[mine, :], score_grad)


def back_first_body(code, ins, outs, g_ref, kt_ref, dq_ref, dk_ref, dv_ref, hold_ref):
    grads, invs, mixes, (v, k, q), expos = ins[:4], ins[4:6], ins[6:10], ins[10:13], ins[13:]
    dq, dk, dv, g_rest, delta = outs
    total = q.buffer.shape[0]
    pair, rows = total // 2, grads[0].buffer.shape[0]
    for arrival in (*grads, *invs, *mixes):
        arrival()
    hold_ref[...] = jnp.zeros_like(hold_ref)
    for i, grad in enumerate(grads):
        hold_ref[i * rows : (i + 1) * rows, :MINE] = grad()[...].astype(F32)
    lane = lax.broadcasted_iota(jnp.int32, (8, PAD), 1) // HEAD
    pick = (lane == lax.broadcasted_iota(jnp.int32, (8, PAD), 0)).astype(F32).astype(BF)
    for i in range(2):
        here = slice(i * pair, (i + 1) * pair)
        inverse = invs[i]()[...].T[:pair, :]
        lane = lax.broadcasted_iota(jnp.int32, (pair, PAD), 1) // HEAD
        scale = jnp.zeros((pair, PAD), F32)
        for h in range(MINE // HEAD):
            scale = jnp.where(lane == h, inverse[:, h : h + 1], scale)
        scaled = (hold_ref[here, :] * scale).astype(BF)
        g_ref[here, :] = scaled[:, :TILE]
        g_rest.ref[here, :] = scaled[:, TILE:]
        for j in range(2):
            rows_here = slice(i * pair + j * rows, i * pair + (j + 1) * rows)
            hold_ref[rows_here, :MINE] = mixes[2 * i + j]()[...].astype(F32)
        prod = scaled.astype(F32) * hold_ref[here, :]
        high = prod.astype(BF)
        low = (prod - high.astype(F32)).astype(BF)
        delta.ref[8 * i : 8 * i + 8, :pair] = dott(pick, high) + dott(pick, low)
        delta.ref[8 * i : 8 * i + 8, pair:] = jnp.zeros((8, delta.ref.shape[1] - pair), F32)
    g_rest.send()
    delta.send()
    for arrival in (v, k, q, *expos[:2]):
        arrival()
    kt_ref[...] = k()[...].astype(F32).T.astype(BF)

    def delta_of(h, i, at, size):
        return delta.ref[8 * i + h : 8 * i + h + 1, at : at + size]

    back_heads((0, 1), q(), v(), g_ref, kt_ref, delta_of, expos, dq_ref, dk_ref, dv_ref)
    for i in range(2):
        dq.ref[i * pair : (i + 1) * pair, :] = (dq_ref[i].T[:pair] * HEAD**-0.5).astype(BF)
    dq.send()
    dk.ref[...] = dk_ref[...].astype(BF)
    dk.send()
    dv.ref[...] = dv_ref[...].astype(BF)
    dv.send()


def back_last_body(code, ins, outs, kt_ref, dq_ref, dk_ref, dv_ref, piece_ref):
    v, g, k, q, delta, *expos = ins[:7]
    dq0, dk0, dv0, normed = ins[7:]
    dqk, dv, keep, send = outs
    pair = q.buffer.shape[0] // 2
    for arrival in (v, g, k, q, delta):
        arrival()
    kt_ref[...] = k()[...].astype(F32).T.astype(BF)

    def delta_of(h, i, at, size):
        return delta()[8 * i + h : 8 * i + h + 1, at : at + size]

    back_heads((2,), q(), v(), g(), kt_ref, delta_of, expos, dq_ref, dk_ref, dv_ref)
    rest = MINE - TILE
    dqk.ref[:, :TILE] = dq0()[...]
    for i in range(2):
        dq = (dq_ref[i].T[:pair] * HEAD**-0.5).astype(BF)
        dqk.ref[i * pair : (i + 1) * pair, TILE:MINE] = dq[:, :rest]
    dqk.ref[:, MINE : MINE + TILE] = dk0()[...]
    dqk.ref[:, MINE + TILE :] = dk_ref[:, :rest].astype(BF)
    dv.ref[:, :TILE] = dv0()[...]
    dv.ref[:, TILE:] = dv_ref[:, :rest].astype(BF)
    weight_grad(code, normed, dqk.ref, dv.ref, keep, send, piece_ref)
    dqk.send()
    dv.send()


PIECES = 8


def weight_grad(code, normed, dqk_ref, dv_ref, keep, send, hold_ref):
    width = normed().shape[1]
    rows = width // PIECES
    piece = rows + rows // 2
    mine = code[0]
    qk = tdot(normed()[...], dqk_ref[...]).astype(BF)
    v = tdot(normed()[...], dv_ref[...]).astype(BF)
    for p in range(PIECES):
        at = pl.multiple_of((p ^ mine) * piece, 16)
        hold_ref[pl.ds(at, rows), :] = qk[p * rows : (p + 1) * rows]
        at = pl.multiple_of((p ^ mine) * piece + rows, 16)
        top = v[p * rows : p * rows + rows // 2]
        low = v[p * rows + rows // 2 : (p + 1) * rows]
        hold_ref[pl.ds(at, rows // 2), :] = jnp.concatenate([top, low], 1)
    half = PIECES * piece // 2
    send.ref[...] = hold_ref[half:, :]
    send.send()
    keep.ref[...] = hold_ref[:half, :]
    keep.send()


def back_scratch(total):
    wide = -(-(total // 2) // 128) * 128
    return [
        pltpu.VMEM((TILE, total), BF),
        pltpu.VMEM((2, TILE, wide), F32),
        pltpu.VMEM((total, TILE), F32),
        pltpu.VMEM((total, TILE), F32),
    ]


def tile_cut(array, tile):
    return home(array, cut=(slice(None), pl.ds(tile * TILE, TILE)), shape=(array.shape[0], TILE))


def back_first(q, k, v, e0, e1, grads, mixes, inv0, inv1):
    total = k.shape[0]
    pair = total // 2
    wide = -(-pair // 128) * 128
    args = [*map(ready, grads), inv0, inv1, *map(ready, mixes)] + [tile_cut(a, 0) for a in (v, k, q)]
    args += [home(e, cut=(h,), shape=(total, pair)) for h in range(2) for e in (e0, e1)]
    return staged(
        back_first_body,
        args,
        [((total, TILE), BF)] * 4 + [((16, wide), F32)],
        near=(0, 1, 2, 3, 4),
        name="back_first",
        mib=40,
        us=12,
        scratch=[pltpu.VMEM((total, TILE), BF), *back_scratch(total), pltpu.VMEM((total, PAD), F32)],
    )


def back_last(codes, q, k, v, e0, e1, first, normed):
    total, width = k.shape[0], normed.shape[1]
    pair = total // 2
    dq, dk, dv, g, delta = first
    piece = width // PIECES * 3 // 2
    half = ((PIECES * piece // 2, 2 * MINE), BF)
    args = [tile_cut(v, 1), ready(g), tile_cut(k, 1), tile_cut(q, 1), ready(delta)]
    args += [home(e, cut=(2,), shape=(total, pair)) for e in (e0, e1)]
    return staged(
        back_last_body,
        [*args, *map(ready, (dq, dk, dv)), normed],
        [((total, 2 * MINE), BF), ((total, MINE), BF), half, half],
        near=(0, 1, 2, 3),
        name="back_last",
        mib=40,
        us=10,
        scratch=[*back_scratch(total), pltpu.VMEM((PIECES * piece, 2 * MINE), BF)],
        code=codes,
    )


STEP = 512


def feed_forward_body(code, ins, outs):
    summed, own, near, far, rest, combiner, baseline, gain, shift, expander, priming, squeezer, tangent = ins
    residual, own_wide, wide, own_slim, slim = outs
    me = code[2]
    first = code[3] == 0
    total = summed()[...] + baseline()[...]
    for r, block in ((2, far), (3, rest), (0, own), (1, near)):
        at = pl.multiple_of((me ^ r) * MINE, 16)
        total += dot(block()[...], combiner()[pl.ds(at, MINE), :])
    residual.ref[...] = total
    residual.send()
    unit, _ = normalise(total)
    low = (unit * gain()[...] + shift()[...]).astype(BF)
    own_slim.ref[...] = jnp.where(first, tangent()[...], low)
    own_slim.send()
    slim.ref[...] = jnp.where(first, low, tangent()[...])
    slim.send()
    for at in range(0, expander().shape[1], STEP):
        cut = slice(at, at + STEP)
        hidden = dot(low, expander()[:, cut]) + priming()[cut]
        back = dott(tangent()[...], squeezer()[cut, :])
        phi = 0.5 * (1.0 + lax.erf(hidden * (2.0**-0.5)))
        density = jnp.exp(-0.5 * hidden * hidden) * 0.3989422804014327
        active = (hidden * phi).astype(BF)
        grad = (back * (phi + hidden * density)).astype(BF)
        own_wide.ref[:, cut] = jnp.where(first, active, grad)
        wide.ref[:, cut] = jnp.where(first, grad, active)
        part = (slice(None), pl.ds(at, STEP))
        own_wide.send(part, part)
        wide.send(part, part)


def feed_forward(codes, summed, own, near, far, rest, combiner, baseline, gain, shift, expander, priming, squeezer, tangent):
    rows, width = summed.shape
    hid = expander.shape[1]
    weights = [combiner, baseline, gain, shift, expander, priming, squeezer, tangent]
    return staged(
        feed_forward_body,
        [*map(ready, (summed, own, near, far, rest)), *weights],
        [((rows, width), F32), ((rows, hid), BF), ((rows, hid), BF), ((rows, width), BF), ((rows, width), BF)],
        near=(0, 1, 2, 3, 4),
        name="feed_forward",
        mib=24,
        us=6,
        code=codes,
    )


def feed_back_body(code, ins, outs, grad_ref, sem):
    expander, residual, gain, tangent, combiner, own_wide, wide = ins
    residual_grad, low, *grads, rows = outs
    me = code[2]
    pltpu.make_async_copy(wide(), grad_ref, sem.at[0]).wait()
    second_grad = dott(grad_ref[...], expander()[...])
    unit, rstd = normalise(residual()[...])
    slope = tangent()[...].astype(F32)
    total = slope + norm_back(second_grad * gain()[...], unit, rstd)
    low.ref[...] = total.astype(BF)
    low.send()
    for r in (2, 3, 1, 0):
        at = pl.multiple_of((me ^ r) * MINE, 16)
        grads[r].ref[...] = dott(low.ref[...], combiner()[pl.ds(at, MINE), :]).astype(BF)
        grads[r].send()
    residual_grad.ref[...] = total
    residual_grad.send()
    width = total.shape[1]
    rows.ref[0:1, :] = jnp.sum(slope, 0, keepdims=True)
    rows.ref[1:2, :] = jnp.sum(low.ref[...].astype(F32), 0, keepdims=True)
    rows.ref[2:3, :] = jnp.sum(second_grad * unit, 0, keepdims=True)
    rows.ref[3:4, :] = jnp.sum(second_grad, 0, keepdims=True)
    for j in range(grad_ref.shape[1] // width):
        block = grad_ref[:, j * width : (j + 1) * width].astype(F32)
        rows.ref[4 + j : 5 + j, :] = jnp.sum(block, 0, keepdims=True)
    rows.ref[6:8, :] = jnp.zeros((2, width), F32)
    rows.send()


def pick_wide(on_zero, on_one):
    def early(code, operands, scratch):
        for core, place in enumerate((on_zero, on_one)):

            @pl.when(code[3] == core)
            def _():
                pltpu.make_async_copy(operands[place], scratch[0], scratch[1].at[0]).start()

    return early


def feed_back(codes, residual, own_wide, wide, tangent, expander, gain, combiner):
    rows, width = residual.shape
    return staged(
        feed_back_body,
        [expander, ready(residual), gain, tangent, combiner, apart(own_wide), apart(wide)],
        [((rows, width), F32), ((rows, width), BF)] + [((rows, MINE), BF)] * 4 + [((8, width), F32)],
        early=pick_wide(6, 5),
        near=(1, 2, 3, 4, 5),
        name="feed_back",
        mib=24,
        us=6,
        scratch=[pltpu.VMEM(wide.shape, BF), pltpu.SemaphoreType.DMA((1,))],
        code=codes,
    )


def outcome_body(code, ins, outs, active_ref, sem):
    squeezer, residual, leveling, own_wide, wide = ins
    pltpu.make_async_copy(wide(), active_ref, sem.at[0]).wait()
    outs[0].ref[...] = (residual()[...] + dot(active_ref[...], squeezer()[...]) + leveling()[...]).astype(BF)
    outs[0].send()


def outcome_of(codes, residual, own_wide, wide, squeezer, leveling):
    rows, width = residual.shape
    return staged(
        outcome_body,
        [squeezer, home(residual), leveling, apart(own_wide), apart(wide)],
        [((rows, width), BF)],
        early=pick_wide(3, 4),
        name="outcome",
        mib=16,
        us=4,
        scratch=[pltpu.VMEM(wide.shape, BF), pltpu.SemaphoreType.DMA((1,))],
        code=codes,
    )[0]


PARTS = 16


def place(code, piece, size):
    return pl.multiple_of((piece ^ code) * size, 8)


def segments(first, rows, low, size):
    out, at = [], first
    while at < first + rows:
        piece, offset = divmod(at - low, size)
        count = min(size - offset, first + rows - at)
        out.append((piece, offset, at - first, count))
        at += count
    return out


def spread(hold_ref, block, first, low, size, code):
    for piece, offset, start, count in segments(first, block.shape[0], low, size):
        at = pl.multiple_of(place(code, piece, size) + offset, 8)
        hold_ref[pl.ds(at, count), :] = block[start : start + count]


def feed_grad_body(sizes, code, ins, outs, mine_ref, peer_ref, sems, *holds):
    own_wide, own_slim, wide, slim, own, far, near, rest, resid, other = ins
    hid, width = own_wide().shape[1], own_slim().shape[1]
    assert hid == 2 * width
    bulk = PARTS * sizes[0]
    loads = []
    for n, (hold_ref, big, small) in enumerate(((mine_ref, own_wide, own_slim), (peer_ref, wide, slim))):
        for j in range(hid // width):
            loads.append(pltpu.make_async_copy(big().at[:, pl.ds(j * width, width)], hold_ref.at[j], sems.at[3 * n + j]))
        loads.append(pltpu.make_async_copy(small(), hold_ref.at[2], sems.at[3 * n + 2]))
    for load in loads:
        load.start()
    for load in loads:
        load.wait()

    def put(block, row):
        for part, low, high in ((0, 0, bulk), (1, bulk, bulk + PARTS * sizes[1])):
            first, last = max(row, low), min(row + block.shape[0], high)
            if first < last:
                spread(holds[part], block[first - row : last - row], first, low, sizes[part], code[4 + 2 * part])

    for j in range(hid // width):
        left = jnp.where(code[3] == 0, j, 2)
        right = jnp.where(code[3] == 0, 2, j)
        block = tdot(mine_ref[left], mine_ref[right]) + tdot(peer_ref[left], peer_ref[right])
        put(block, j * width)

    upper = code[2] < 2
    for i in range(2):
        here = jnp.where(upper, (own, far)[i]()[...], (far, own)[i]()[...])
        peer = jnp.where(upper, (near, rest)[i]()[...], (rest, near)[i]()[...])
        put(tdot(here, resid()[...]) + tdot(peer, other()[...]), hid + i * MINE)
    for part, hold_ref in enumerate(holds):
        keep, send = outs[2 * part : 2 * part + 2]
        half = hold_ref.shape[0] // 2
        send.ref[...] = hold_ref[half:, :].astype(BF)
        send.send()
        keep.ref[...] = hold_ref[:half, :].astype(BF)
        keep.send()


def feed_grad(codes, sizes, feed, mixed):
    rows, width = feed[1].shape
    halves = [((PARTS * size // 2, width), BF) for size in sizes]
    return staged(
        functools.partial(feed_grad_body, sizes),
        [apart(feed[0]), apart(feed[1]), *map(ready, feed[2:]), *map(ready, mixed)],
        [halves[0], halves[0], halves[1], halves[1]],
        near=(0, 1, 2, 3),
        name="feed_grad",
        mib=40,
        us=7,
        scratch=[
            pltpu.VMEM((3, rows, width), BF),
            pltpu.VMEM((3, rows, width), BF),
            pltpu.SemaphoreType.DMA((6,)),
            *[pltpu.VMEM((PARTS * size, width), F32) for size in sizes],
        ],
        code=codes,
    )


def feed_assemble_body(side, sizes, code, ins, outs, sems, *holds):
    squeezer, expander, combiner = (out.target for out in outs)
    hid, width = squeezer.shape

    def targets(core, row, count):
        out = []
        while count:
            if row < hid and core == 0:
                take = min(count, hid - row)
                out.append((squeezer.at[pl.ds(row, take), :], take))
            elif row < hid:
                j = row // width
                take = min(count, (j + 1) * width - row)
                cut = pl.ds(row - j * width, take), pl.ds(j * width, width)
                out.append((expander.at[cut], take))
            else:
                view, at = divmod(row - hid, MINE)
                take = min(count, MINE - at)
                out.append((combiner.at[pl.ds((core + 2 * view) * MINE + at, take), :], take))
            row, count = row + take, count - take
        return out

    for i, hold_ref in enumerate(holds):
        half = hold_ref.shape[0] // 2
        hold_ref[:half, :] = ins[2 * i]()[...].astype(F32)
        hold_ref[half:, :] = ins[2 * i + 1]()[...].astype(F32)
    for core in range(2):

        @pl.when(code[3] == core ^ side)
        def _():
            moves, low = [], 0
            for part, size in enumerate(sizes):
                for piece in range(PARTS):
                    start = pl.multiple_of((piece ^ code[4 + 2 * part + side]) * size, 8)
                    at = 0
                    for target, count in targets(core, low + piece * size, size):
                        source = holds[part].at[pl.ds(pl.multiple_of(start + at, 8), count), :]
                        moves.append(pltpu.make_async_copy(source, target, sems.at[len(moves)]))
                        moves[-1].start()
                        at += count
                low += PARTS * size
            for move in moves:
                move.wait()


def feed_assemble(codes, side, blocks, hid, held=()):
    width = blocks[0].shape[1]
    sizes = [blocks[0].shape[0] // 8, blocks[2].shape[0] // 8]
    return staged(
        functools.partial(feed_assemble_body, side, sizes),
        [ready(b) for b in blocks],
        [((hid, width), F32), ((width, hid), F32), ((width, width), F32)],
        name="feed_assemble",
        mib=24,
        us=5,
        scratch=[pltpu.SemaphoreType.DMA((48,))] + [pltpu.VMEM((PARTS * n, width), F32) for n in sizes],
        code=codes,
        held=held,
        buffers={0: (8, 128), 1: (8, 128), 2: (8, 128)},
    )


def input_grad_body(_, ins, outs, hold_ref):
    dqk, dv, weight, unit, rstd, gain, *rest = ins
    near_cams, far_cams, resid = rest
    small = outs[4]
    patches = resid.buffer.shape[0]
    groups = small.ref.shape[0] - 2
    slope = dott(dqk()[:, :MINE], weight()[:, :MINE]) + dott(dqk()[:, MINE:], weight()[:, PAD : PAD + MINE])
    slope += dott(dv()[...], weight()[:, 2 * PAD : 2 * PAD + MINE])
    values = unit()[...].astype(F32)
    small.ref[groups : groups + 1, :] = jnp.sum(slope * values, 0, keepdims=True)
    small.ref[groups + 1 : groups + 2, :] = jnp.sum(slope, 0, keepdims=True)
    hold_ref[...] = norm_back(slope * gain()[...], values, rstd()[...])
    for r in (1, 3, 0, 2):
        part = hold_ref[r * patches : (r + 1) * patches, :]
        outs[r].ref[...] = part.astype(outs[r].ref.dtype)
        outs[r].send()
    hold_ref[:patches, :] = hold_ref[:patches, :] + resid()[...]
    table = jnp.zeros((groups, slope.shape[1]), F32)
    for i, cams in enumerate((near_cams, far_cams)):
        part = hold_ref[2 * i * patches : 2 * (i + 1) * patches, :]
        hot = onehot_t(cams()[...], groups)
        for piece in split3(part)[:2]:
            table += dot(hot, piece)
    small.ref[:groups, :] = table
    small.send()


def input_grad(dqk, dv, weight, unit, rstd, gain, cams, resid, groups):
    total, width = unit.shape
    patches = resid.shape[0]
    low, full = ((patches, width), BF), ((patches, width), F32)
    return staged(
        input_grad_body,
        [ready(dqk), ready(dv), home(weight), home(unit), home(rstd), gain, *cams, home(resid)],
        [full, low, full, low, ((groups + 2, width), F32)],
        near=(0, 1, 2, 3, 4),
        name="input_grad",
        mib=48,
        us=9,
        scratch=[pltpu.VMEM((total, width), F32)],
    )


def assemble_body(code, ins, outs):
    out, table, *vectors = outs
    rows, width = out.ref.shape[0] // PIECES, out.ref.shape[1] // 3
    piece = rows * 3 // 2
    blocks = [arrival() for arrival in ins[:4]]
    for p in range(PIECES):
        cut = []
        for i, which in enumerate((0, 1, 0, 1)):
            r = (p ^ code[which]) % 4
            core = code[3] if which == 0 else 1 - code[3]
            far = i // 2
            middle = jnp.where(core == 0, r // 2 * 2 + far, far * 2 + r // 2)
            at = pl.multiple_of((middle * 2 + r % 2) * piece, 16)
            upper = (p ^ code[which]) >= PIECES // 2
            lower_block = blocks[2 * which][pl.ds(at, piece), :]
            upper_block = blocks[2 * which + 1][pl.ds(at, piece), :]
            cut.append(jnp.where(upper, upper_block, lower_block).astype(F32))
        low = p * rows
        for v, block in enumerate(by_view(cut, code[2])):
            at = v * MINE
            out.ref[low : low + rows, at : at + MINE] = block[:rows, :MINE]
            out.ref[low : low + rows, width + at : width + at + MINE] = block[:rows, MINE:]
            at += 2 * width
            out.ref[low : low + rows // 2, at : at + MINE] = block[rows:, :MINE]
            out.ref[low + rows // 2 : low + rows, at : at + MINE] = block[rows:, MINE:]
        out.send((pl.ds(low, rows),), (pl.ds(low, rows),))
    total = ins[4]()[...].astype(F32) + ins[5]()[...].astype(F32)
    count, half, groups = total.shape[0] // 2, width // 2, table.ref.shape[0]
    table.ref[:, :half] = total[:groups, :]
    table.ref[:, half:] = total[count : count + groups, :]
    table.send()
    row = groups
    for vector in vectors:
        for at in range(0, vector.ref.shape[0], width):
            vector.ref[at : at + half] = total[row, :]
            vector.ref[at + half : at + width] = total[count + row, :]
            row += 1
        vector.send()


def assemble(codes, blocks, smalls, groups, sizes, width):
    return staged(
        assemble_body,
        [ready(b) for b in (*blocks, *smalls)],
        [((width, 3 * width), F32), ((groups, width), F32)] + [((size,), F32) for size in sizes],
        name="assemble",
        mib=24,
        us=5,
        code=codes,
    )


def turned(block):
    half = block.shape[0] // 2
    return jnp.concatenate([block[half:], block[:half]], 0)


def after(values, *others):
    out = lax.optimization_barrier((*values, *others))
    return out[: len(values)]


def halve(keep, got):
    cut = keep.shape[0] // 2
    return keep[:cut] + got[:cut], keep[cut:] + got[cut:]


class Part:
    def __init__(self, keep, got, stages):
        self.value, self.got, self.stages, self.step, self.lower, self.peer = keep, got, stages, 0, None, None

    def begin(self):
        self.value, send = halve(self.value, self.got)
        self.got = swap_by_core(send, self.stages[2])

    def advance(self, got):
        self.step += 1
        if self.step == 1:
            self.value = lax.optimization_barrier(whole_slice(self.value + got))
            self.got = swap_by_core(self.value, self.stages[3])
        elif self.step == 2:
            self.value = lax.optimization_barrier(self.value + turned(got))
            self.got = swap_by_core(self.value, self.stages[2])
        elif self.step == 3:
            self.value = jnp.concatenate([self.value, got], 0)
            self.got = swap_by_core(self.value, self.stages[1])
        elif self.step == 4:
            self.value = jnp.concatenate([self.value, got], 0)
            self.got, peer = swap_by_core(self.value, self.stages[0]), swap(self.value, "view", 1)
            self.lower = (self.value, peer)
        else:
            self.got, self.peer = got, swap(got, "view", 1)
            return []
        return [self.value]


PLAN = ("LAB", "LAG", "BI", "A", "B", "L", "AI", "L", "B", "LpO", "AB", "P", "Lkq")


def on_device(
    inputs,
    cameras,
    embedding,
    scaling,
    shifting,
    projector,
    combiner,
    baseline,
    rescaling,
    reshifting,
    expander,
    priming,
    squeezer,
    leveling,
    cotangent,
):
    me = lax.axis_index("view")
    core = me % 2
    patches, width = inputs.shape[2], inputs.shape[3]
    groups, hid = embedding.shape[0], expander.shape[1]
    codes = [code_of(SCENE, core), code_of(SCENE, 1 - core), me, core]
    codes += [code_of(WIDE, core), code_of(WIDE, 1 - core), code_of(THIN, core), code_of(THIN, core)]
    codes = jnp.stack(codes).astype(jnp.int32)
    tangent = cotangent.reshape(patches, width)
    x0 = inputs.reshape(patches, width)
    c0 = cameras.reshape(1, patches)
    x2 = swap(x0, "view", 2)
    x1, c1 = swap(x0, "view", 1), swap(c0, "view", 1)
    near_cams = jnp.concatenate([c0, c1], 1)
    far_cams = swap(near_cams, "view", 2)
    hole = jnp.zeros((width, PAD - MINE), BF)
    padded = []
    for part in range(3):
        padded += [lax.dynamic_slice_in_dim(projector, part * width + me * MINE, MINE, 1), hole]
    padded = jnp.concatenate(padded, 1)
    *held, summed = project(x0, x1, near_cams, embedding, scaling, shifting, padded)
    x2, far_cams = after((x2, far_cams), *held)
    x3 = swap(x2, "view", 1)
    normed, unit1, rstd1, q, k, v, e1, far, rest, inv1, near_k, near_v = second_half(
        x2, x3, far_cams, embedding, scaling, shifting, padded, held
    )
    mine_far, mine_rest = far, rest
    far, rest = swap(far, "view", 2), swap(rest, "view", 3)
    e0, own, near, inv0 = attend(q, near_k, near_v)
    mixes = [own, near, mine_far, mine_rest]
    near, own, far, rest = after((near, own, far, rest))
    near, peer_rest = swap(near, "view", 1), swap(rest, "view", 1)

    residual, own_wide, wide, own_slim, slim = feed_forward(
        codes, summed, own, near, far, rest, combiner, baseline, rescaling, reshifting, expander, priming,
        squeezer, tangent,
    )
    peer_near = swap(near, "view", 1)
    peer_wide, peer_slim = swap(wide, "view", 1), swap(slim, "view", 1)
    residual_grad, resid_low, *grads, rows = feed_back(
        codes, residual, own_wide, wide, tangent, expander, rescaling, combiner
    )
    peer_near, peer_rest, resid_low, *grads = after((peer_near, peer_rest, resid_low, *grads))
    grads = [grads[0]] + [swap(grads[r], "view", r) for r in (1, 2, 3)]
    other = swap(resid_low, "view", 1)
    sizes = [(hid + width // 2) // 24, (hid + width // 2) // 48]
    keep0, send0, keep1, send1 = feed_grad(
        codes, sizes, [own_wide, own_slim, peer_wide, peer_slim],
        [own, far, peer_near, peer_rest, resid_low, other],
    )
    *grads, keep0, send0, keep1, send1 = after((*grads, keep0, send0, keep1, send1))
    got0, got1 = swap_by_core(send0, WIDE[0]), swap_by_core(send1, THIN[0])
    first = back_first(q, k, v, e0, e1, grads, mixes, inv0, inv1)
    got0, got1, *first = after((got0, got1, *first))
    keep0, send0 = halve(keep0, got0)
    keep1, send1 = halve(keep1, got1)
    got0, got1 = swap_by_core(send0, WIDE[1]), swap_by_core(send1, THIN[1])
    dqk, dv, keep, send = back_last(codes, q, k, v, e0, e1, first, normed)
    got0, got1, dqk, dv, keep, send = after((got0, got1, dqk, dv, keep, send))
    wide_part = Part(keep0, got0, WIDE)
    thin_part = Part(keep1, got1, THIN)
    got_l = swap_by_core(send, SCENE[0])
    wide_part.begin()
    thin_part.begin()
    parts = dict(A=wide_part, B=thin_part)
    l_step, i_step = 0, 0
    message = near_keep = near_got = other = small = None
    outcome = inputs_grad = feed_grads = None
    last = []
    gate = [codes, dqk]
    extra = 0

    def grow(message, got):
        small = rounded(message[-extra:].astype(F32) + got[-extra:].astype(F32))
        return jnp.concatenate([message[:-extra], got[:-extra], small], 0)

    for group in PLAN:
        tied = []
        if "O" in group:
            outcome = outcome_of(gate[0], residual, own_wide, wide, squeezer, leveling)
            tied.append(outcome)
        if "G" in group:
            own, near, far, rest, small = input_grad(
                gate.pop(), dv, padded, unit1, rstd1, scaling, (near_cams, far_cams), residual_grad, groups
            )
            tied += [near, rest, small]
        if "P" in group:
            blocks = [b for n in "AB" for b in (parts[n].lower[0], parts[n].got)]
            feed_grads = feed_assemble(gate[0], 0, blocks, hid)
            tied += feed_grads
        waits = []
        for name in group:
            if name in "AB":
                waits.append(parts[name].got)
            elif name == "L":
                waits.append(got_l)
            elif name == "I":
                waits += [near, rest] if i_step == 0 else [far]
            elif name == "p":
                waits += [parts["A"].lower[1], parts["B"].lower[1]]
            elif name == "k":
                waits.append(near_keep)
            elif name == "q":
                waits += [parts[n].peer for n in "AB"]
        bundle = list(after((*waits, *tied, *last, *gate)))
        new_waits, rest_of = bundle[: len(waits)], bundle[len(waits) :]
        new_tied, gate = rest_of[: len(tied)], rest_of[len(rest_of) - len(gate) :]
        if "O" in group:
            outcome = new_tied.pop(0)
        if "G" in group:
            near, rest, small = new_tied[:3]
            new_tied = new_tied[3:]
        if "P" in group:
            feed_grads = new_tied
        last = []
        for name in group:
            if name in "AB":
                last += parts[name].advance(new_waits.pop(0))
            elif name == "p":
                for n in "AB":
                    parts[n].lower = (parts[n].lower[0], new_waits.pop(0))
            elif name == "k":
                near_keep = new_waits.pop(0)
            elif name == "q":
                for n in "AB":
                    parts[n].peer = new_waits.pop(0)
            elif name == "I":
                if i_step == 0:
                    near, rest = new_waits.pop(0), new_waits.pop(0)
                    far = lax.optimization_barrier((far + rest.astype(F32)).astype(BF))
                    last.append(far)
                    far = swap(far, "view", 2)
                else:
                    far = new_waits.pop(0)
                    inputs_grad = (residual_grad + own + near.astype(F32) + far.astype(F32)).astype(BF)
                    last.append(inputs_grad)
                i_step += 1
            elif name == "L":
                got = new_waits.pop(0)
                if l_step == 0:
                    keep, send = halve(keep, got)
                    got_l = swap_by_core(send, SCENE[1])
                elif l_step == 1:
                    block = jnp.concatenate([small, rows[:6]], 0)
                    block = rounded(jnp.concatenate([block[:, : width // 2], block[:, width // 2 :]], 0))
                    extra = block.shape[0]
                    message = jnp.concatenate([keep + got, block], 0)
                    message = lax.optimization_barrier(whole_slice(message))
                    got_l = swap_by_core(message, SCENE[2])
                elif l_step == 2:
                    got = jnp.concatenate([turned(got[:-extra]), got[-extra:]], 0)
                    message = rounded(message.astype(F32) + got.astype(F32))
                    got_l = swap_by_core(message, LATE[0])
                elif l_step < 5:
                    message = grow(message, got)
                    got_l = swap_by_core(message, LATE[l_step - 2])
                    if l_step == 4:
                        near_keep = swap(message[:-extra], "view", 1)
                else:
                    got_l = got
                    near_got = swap(got, "view", 1)
                    small = rounded(message[-extra:].astype(F32) + got[-extra:].astype(F32))
                    other = swap(small, "view", 1)
                if l_step:
                    last.append(message if l_step < 5 else small)
                else:
                    last += [keep, send]
                l_step += 1
            elif name == "G":
                near, rest = swap(near, "view", 1), swap(rest, "view", 1)
    assert l_step == 6 and i_step == 2 and outcome is not None
    blocks = [b for n in "AB" for b in (parts[n].lower[1], parts[n].peer)]
    grad_squeezer, grad_expander, grad_combiner = feed_assemble(gate[0], 1, blocks, hid, feed_grads)
    near_got, other, grad_squeezer = after((near_got, other, grad_squeezer))
    vectors = [width] * 6 + [hid]
    grad_projector, table, *vectors = assemble(
        gate[0], [message, got_l, near_keep, near_got], [small, other], groups, vectors, width
    )
    grad_scaling, grad_shifting, grad_leveling, grad_baseline, grad_rescaling, grad_reshifting, grad_priming = vectors

    return (
        outcome.reshape(inputs.shape),
        inputs_grad.reshape(inputs.shape),
        table,
        grad_scaling,
        grad_shifting,
        grad_projector,
        grad_combiner,
        grad_baseline,
        grad_rescaling,
        grad_reshifting,
        grad_expander,
        grad_priming,
        grad_squeezer,
        grad_leveling,
    )


def solution(mesh):
    tokens = P("scene", "view", None, None)
    placed = (tokens, P("scene", "view", None)) + (P(),) * 12 + (tokens,)
    return jax.shard_map(
        on_device,
        mesh=mesh,
        in_specs=placed,
        out_specs=(tokens, tokens) + (P(),) * 12,
        check_vma=False,
    )
```
